256 devices in a mesh: list: 32 (over z_lo, y, core), tensor: 8 (over x, z_hi).
Axes of the slice: x: 4, y: 4, z: 8 (z_hi: 2, z_lo: 4; z = z_hi * 4 + z_lo), core: 2. Of those that a mesh axis runs over, the one named last changes fastest.
Arguments:
- states: bfloat16 [768, 16, 4096], P('list', None, 'tensor')
- lengths: int32 [768], P('list'), may hold values from 2 to 16, as said below
- assign: int32 [768], P('list'), may hold values from 0 to 131071, as said below
- norm_gain: float32 [4096], replicated, may hold values from 0.1 to 1.9
- gate_weight: bfloat16 [4096, 7168], P('list', 'tensor'), may hold values from -0.09375 to 0.09375
- up_weight: bfloat16 [4096, 7168], P('list', 'tensor'), may hold values from -0.09375 to 0.09375
- down_weight: bfloat16 [7168, 4096], P('tensor', 'list'), may hold values from -0.0625 to 0.0625
- out_gain: float32 [4096], P('tensor'), may hold values from 0.25 to 1.75
- centroids: bfloat16 [131072, 4096], P('list', 'tensor'), may hold values from -6 to 6
Outputs:
- embedding: float32 [768, 4096], P('list', 'tensor')
- residual: float32 [768, 4096], P('list', 'tensor')
The draws below stay inside these ranges and needn't reach their ends.
Inputs may be any that keep to these rules, and one draw needn't show every extreme that they name: `lengths`: some passage has all 16 slots filled in every draw. `assign`: centroids of index o of list are rows o * 4096 to (o + 1) * 4096 - 1. Of the 24 passages of one index of list at most 2 are assigned to centroids of any one index of list, and in every draw some index of list is assigned exactly 2 passages by every index of list.
All inputs are finite; a program needn't handle non-finite values.
Results may differ from the reference program's by a relative error of at most 0.0065.
Values may be sent and summed in bfloat16 or wider, within the bound.
A program may use at most 128 MiB of HBM per device.

```python
import jax
import jax.numpy as jnp
from jax import lax

D = 4096
FF = 7168
SEQ = 16
PASS_DEV = 24
CAP = 2
CPL = 4096
PASSAGES = 768
NC = 131072
N_LIST = 32


def draw_states(key, part):
    key = jax.random.fold_in(key, 11)
    first = jax.random.fold_in(key, 0)
    columns = 0.6 * jnp.power(3.0, jnp.arange(D, dtype=jnp.float32) / D)
    values = jax.random.normal(first, (PASSAGES, SEQ, D), jnp.float32) * columns[None, None, :]
    return values.astype(jnp.bfloat16)


def draw_lengths(key, part):
    key = jax.random.fold_in(key, 23)
    first, second = jax.random.split(key)
    values = jax.random.randint(first, (PASSAGES,), SEQ // 8, SEQ + 1, dtype=jnp.int32)
    filled = jax.random.randint(second, (), 0, PASSAGES, dtype=jnp.int32)
    places = jnp.arange(PASSAGES, dtype=jnp.int32)
    return jnp.where(places == filled, jnp.int32(SEQ), values).astype(jnp.int32)


def draw_assign(key, part):
    key = jax.random.fold_in(key, 37)
    key_hot, key_pick, key_order, key_row = jax.random.split(key, 4)
    hot = jax.random.randint(key_hot, (), 0, N_LIST, dtype=jnp.int32)
    slot_count = CAP * N_LIST
    slot_owner = jnp.arange(slot_count, dtype=jnp.int32) // CAP
    raw = jax.random.randint(key_pick, (N_LIST, slot_count), 0, 1 << 20, dtype=jnp.int32)
    scores = raw * slot_count + jnp.arange(slot_count, dtype=jnp.int32)[None, :]
    scores = jnp.where(slot_owner[None, :] == hot, -1, scores)
    order = jnp.argsort(-scores, axis=1, stable=True)
    others = slot_owner[order[:, :PASS_DEV - CAP]]
    block = jnp.concatenate([jnp.full((N_LIST, CAP), hot, jnp.int32), others.astype(jnp.int32)], axis=1)
    mix_raw = jax.random.randint(key_order, (N_LIST, PASS_DEV), 0, 1 << 20, dtype=jnp.int32)
    mix = jnp.argsort(mix_raw * PASS_DEV + jnp.arange(PASS_DEV, dtype=jnp.int32)[None, :], axis=1, stable=True)
    owners = jnp.take_along_axis(block, mix, axis=1).reshape(PASSAGES)
    within = jax.random.randint(key_row, (PASSAGES,), 0, CPL, dtype=jnp.int32)
    return (owners * CPL + within).astype(jnp.int32)


def levels(key, dims, cuts, least, largest):
    gain = 1.0
    for position, blocks in cuts:
        heights = jax.random.uniform(jax.random.fold_in(jax.random.fold_in(key, 6), position), (blocks,), jnp.float32, least / len(cuts), largest / len(cuts))
        gain = gain * jnp.repeat(jnp.exp(heights), dims[position] // blocks).reshape((-1,) + (1,) * (len(dims) - 1 - position))
    return gain


def centred(own_key, dims, scale, reach, shards=(), held_as=jnp.bfloat16):
    result = jax.random.normal(own_key, dims, jnp.float32) * scale
    if len(shards) > 0:
        result = levels(own_key, dims, shards, -0.22, 0.18) * result
    return jnp.clip(result, min=-reach, max=reach).astype(held_as)


def setup_inputs(seed: int = 0) -> dict:
    seeds = jax.random.split(jax.random.key(seed), 10)
    states = draw_states(jax.random.fold_in(seeds[9], 71), 0)
    lengths = draw_lengths(jax.random.fold_in(seeds[9], 71), 0)
    assign = draw_assign(jax.random.fold_in(seeds[9], 71), 0)
    norm_gain = jnp.clip(1.0 + 0.18 * jax.random.normal(seeds[3], (D,), jnp.float32), 0.1, 1.9)
    gate_weight = centred(seeds[4], (D, FF), D ** -0.5, 0.09375, ((0, 32), (1, 8)))
    up_weight = centred(seeds[5], (D, FF), D ** -0.5, 0.09375, ((0, 32), (1, 8)))
    down_weight = centred(seeds[6], (FF, D), FF ** -0.5, 0.0625, ((0, 8), (1, 32)))
    out_gain = jnp.clip(1.0 + 0.15 * jax.random.normal(seeds[7], (D,), jnp.float32), 0.25, 1.75)
    centroids = centred(seeds[8], (NC, D), 1.0, 6.0, ((0, 32), (1, 8)))
    return dict(states=states, lengths=lengths, assign=assign, norm_gain=norm_gain, gate_weight=gate_weight, up_weight=up_weight, down_weight=down_weight, out_gain=out_gain, centroids=centroids)


def encode_group(states, lengths, norm_gain, gate_weight, up_weight, down_weight):
    flat = states.reshape(-1, D).astype(jnp.float32)
    scale = lax.rsqrt(lax.optimization_barrier(jnp.mean(flat * flat, axis=1, keepdims=True)) + 1e-05)
    normed = (flat * scale * norm_gain[None, :]).astype(jnp.bfloat16)
    gate = jnp.dot(normed, gate_weight, preferred_element_type=jnp.float32)
    up = jnp.dot(normed, up_weight, preferred_element_type=jnp.float32)
    hidden = (jax.nn.silu(gate) * up).astype(jnp.bfloat16)
    mixed = jnp.dot(hidden, down_weight, preferred_element_type=jnp.float32)
    layer = (flat + mixed).reshape(-1, SEQ, D)
    slots = jnp.arange(SEQ, dtype=jnp.int32)
    valid = (slots[None, :] < lengths[:, None]).astype(jnp.float32)
    pool_w = valid / lengths[:, None].astype(jnp.float32)
    return jnp.einsum('ps,psd->pd', pool_w, layer)

def reference(states, lengths, assign, norm_gain, gate_weight, up_weight, down_weight, out_gain, centroids):
    grouped = states.reshape(N_LIST, PASS_DEV, SEQ, D)
    grouped_len = lengths.reshape(N_LIST, PASS_DEV)

    def one_group(item):
        return encode_group(item[0], item[1], norm_gain, gate_weight, up_weight, down_weight)
    pooled = lax.map(one_group, (grouped, grouped_len)).reshape(PASSAGES, D)
    total = lax.optimization_barrier(jnp.mean(pooled * pooled, axis=1, keepdims=True))
    embedding = pooled * lax.rsqrt(total + 1e-05) * out_gain[None, :]
    chosen = jnp.take(centroids, assign, axis=0).astype(jnp.float32)
    residual = embedding - chosen
    return (embedding, residual)
```

```python
import jax
import jax.numpy as jnp
from jax import lax
from jax.sharding import PartitionSpec as P

CAP = 2


def per_device(
    states, lengths, assign, norm_gain, gate_weight, up_weight, down_weight, out_gain, centroids
):
    passes, seq, width_part = states.shape
    n_list = lax.axis_size("list")
    n_tensor = lax.axis_size("tensor")
    per_owner = centroids.shape[0]
    down_part = down_weight.shape[1]
    me = lax.axis_index("list")
    everyone = lax.all_gather(assign, "list", axis=0)
    mine = everyone // per_owner == me
    rank = jnp.cumsum(mine.astype(jnp.int32), axis=1) - 1
    slot_hit = mine[:, None, :] & (rank[:, None, :] == jnp.arange(CAP, dtype=jnp.int32)[None, :, None])
    local = jnp.sum(jnp.where(slot_hit, (everyone - me * per_owner)[:, None, :], 0), axis=2)
    rows = jnp.take(centroids, local, axis=0)
    back = lax.all_to_all(rows, "list", split_axis=0, concat_axis=0, tiled=True)
    owner = assign // per_owner
    places = jnp.arange(passes, dtype=jnp.int32)
    same_owner = owner[:, None] == owner[None, :]
    earlier = places[:, None] > places[None, :]
    my_rank = jnp.sum((same_owner & earlier).astype(jnp.int32), axis=1)
    pick = (owner * CAP + my_rank)[:, None] == jnp.arange(n_list * CAP, dtype=jnp.int32)[None, :]
    chosen = jnp.dot(
        pick.astype(jnp.bfloat16),
        back.reshape(n_list * CAP, width_part),
        preferred_element_type=jnp.float32,
    )

    whole = lax.all_gather(states, "tensor", axis=2, tiled=True)
    width = whole.shape[2]
    rows_n = passes * seq
    flat = whole.reshape(rows_n, width).astype(jnp.float32)
    scale = lax.rsqrt(jnp.mean(flat * flat, axis=1, keepdims=True) + 1e-05)
    normed = (flat * scale * norm_gain[None, :]).astype(jnp.bfloat16)
    gate = jnp.dot(
        normed,
        lax.all_gather(gate_weight, "list", axis=0, tiled=True),
        preferred_element_type=jnp.float32,
    )
    up = jnp.dot(
        normed,
        lax.all_gather(up_weight, "list", axis=0, tiled=True),
        preferred_element_type=jnp.float32,
    )
    hidden = jax.nn.silu(gate) * up
    slots = jnp.arange(seq, dtype=jnp.int32)
    valid = (slots[None, :] < lengths[:, None]).astype(jnp.float32)
    pool_w = valid / lengths[:, None].astype(jnp.float32)
    pool_hidden = jnp.sum(hidden.reshape(passes, seq, -1) * pool_w[:, :, None], axis=1)
    pool_states = jnp.sum(states.astype(jnp.float32) * pool_w[:, :, None], axis=1)
    all_hidden = lax.all_gather(pool_hidden.astype(jnp.bfloat16), "list", axis=0, tiled=True)
    terms = jnp.dot(all_hidden, down_weight, preferred_element_type=jnp.float32)
    terms = terms.reshape(n_list, passes, down_part)
    part = lax.psum_scatter(terms, "tensor", scatter_dimension=0, tiled=True)
    per = n_list // n_tensor
    t = lax.axis_index("tensor")
    gathered = lax.all_gather(part, "list", axis=0)
    full = gathered.transpose(1, 2, 0, 3).reshape(per, passes, n_tensor, width_part)
    mine_out = lax.all_to_all(full, "tensor", split_axis=2, concat_axis=0, tiled=True)
    mixed = mine_out.reshape(n_list, passes, width_part)
    mixed = lax.dynamic_index_in_dim(mixed, me, axis=0, keepdims=False)
    pooled = pool_states + mixed
    total = lax.psum(jnp.sum(pooled * pooled, axis=1), "tensor")
    embedding = pooled * lax.rsqrt(total[:, None] / width + 1e-05) * out_gain[None, :]
    residual = embedding - chosen
    return (embedding, residual)


def solution(mesh):
    return jax.shard_map(
        per_device,
        mesh=mesh,
        in_specs=(
            P("list", None, "tensor"),
            P("list"),
            P("list"),
            P(),
            P("list", "tensor"),
            P("list", "tensor"),
            P("tensor", "list"),
            P("tensor"),
            P("list", "tensor"),
        ),
        out_specs=(P("list", "tensor"), P("list", "tensor")),
        check_vma=False,
    )
```

```python
import functools

import jax
import jax.numpy as jnp
from jax import lax
from jax.experimental import pallas as pl
from jax.experimental.pallas import tpu as pltpu
from jax.sharding import PartitionSpec as P

MESH = pl.DeviceIdType.MESH
BF = jnp.bfloat16
F32 = jnp.float32

PASSES, SEQ, PART, WIDTH = 24, 16, 512, 4096
ROWS = PASSES * SEQ
HID = 896
TILES = HID // 128
PAD = 32
OWN_ROWS = 4096

R_Z = 0
R_Y = 4
R_H = 12
R_SC = 20
R_SY = 24
R_SH = 32
R_DN = 40
R_CR = 44
R_X = 46
R_G = 62
R_1 = 70
R_2 = 74
R_3 = 82
R_END = 90
N_SEND = 96


def kernel(
    lengths, assign, states, gain, gate, up, down, out_gain, centroids,
    emb_out, res_out,
    wbuf, xbuf, acc, cbuf, dbuf, sbuf, g_in, u_in, gain_in, og_in,
    scale_s, mask_s, inv_s, hb, tf, tb, r1b, qs, rb, sb, abuf, pick, cacc, resp, gotc, chosen_s, smean,
    ss, rs, ls, req_s, req_r, rsp_s, rsp_r,
):
    lst = lax.axis_index("list")
    ten = lax.axis_index("tensor")
    core = lax.rem(lst, 2)
    y = lax.rem(lst // 2, 4)
    zl = lst // 8
    x = ten // 2
    zh = lax.rem(ten, 2)
    me_g = lax.rem(lst, 8)

    def dev(list_=None, tensor=None):
        return {"list": lst if list_ is None else list_, "tensor": ten if tensor is None else tensor}

    def at_z(z):
        return dev(list_=z * 8 + me_g)

    def at_y(step):
        return dev(list_=zl * 8 + lax.rem(y + step + 4, 4) * 2 + core)

    def at_x(step):
        return dev(tensor=lax.rem(x + step + 4, 4) * 2 + zh)

    sibling = dev(list_=lst + 1 - 2 * core)
    partner = dev(tensor=x * 2 + 1 - zh)

    sends = []

    def send(src, dst, recv, device, cond=None):
        n = len(sends)
        cp = pltpu.make_async_remote_copy(
            src_ref=src, dst_ref=dst, send_sem=ss.at[n], recv_sem=rs.at[recv],
            device_id=device, device_id_type=MESH,
        )
        sends.append((cp, cond))
        if cond is None:
            cp.start()
        else:
            pl.when(cond)(cp.start)

    def arrived(dst, recv):
        pltpu.make_async_remote_copy(
            src_ref=dst, dst_ref=dst, send_sem=ss.at[0], recv_sem=rs.at[recv],
            device_id=sibling, device_id_type=MESH,
        ).wait_recv()

    locals_ = []

    def local(src, dst):
        cp = pltpu.make_async_copy(src, dst, ls.at[len(locals_)])
        locals_.append(cp)
        cp.start()
        return cp

    def xslot(z_hi, half, x_):
        return xbuf.at[z_hi * 2 + half, :, pl.ds(pl.multiple_of(x_ * 256, 256), 256)]

    cps_w = [local(gate, g_in), local(up, u_in), local(gain, gain_in)]
    for half in range(2):
        send(states.at[:, pl.ds(half * 256, 256)], xslot(zh, half, x), R_CR + half, partner)
    for step in (1, -1, 2):
        for half in range(2):
            send(states.at[:, pl.ds(half * 256, 256)], xslot(zh, half, x), R_X + x * 2 + half, at_x(step))
    cps_x = [local(states.at[:, pl.ds(half * 256, 256)], xslot(zh, half, x)) for half in range(2)]

    for cp in cps_w:
        cp.wait()
    eye = lax.broadcasted_iota(jnp.int32, (128, 128), 0) == lax.broadcasted_iota(jnp.int32, (128, 128), 1)
    gcol = jnp.sum(jnp.where(eye, gain_in[pl.ds(lst, 1), :], 0.0), axis=1, keepdims=True)
    own_rows = pl.ds(pl.multiple_of(zl * 256 + core * 128, 128), 128)
    for j in range(TILES):
        wbuf[y, own_rows, j * 256 : j * 256 + 128] = (g_in[:, j * 128 : j * 128 + 128].astype(F32) * gcol).astype(BF)
        wbuf[y, own_rows, j * 256 + 128 : j * 256 + 256] = (u_in[:, j * 128 : j * 128 + 128].astype(F32) * gcol).astype(BF)

    def wblock(y_, z_, c_, start=0, rows=128):
        return wbuf.at[y_, pl.ds(pl.multiple_of(z_ * 256 + c_ * 128 + start, 64), rows)]

    def place(k):
        inner = (zl == 1) | (zl == 2)
        o = jnp.where(inner, 1 - k, k) if k < 2 else k
        return jnp.where(zl < 2, o, 3 - o)

    def y_of(step):
        return lax.rem(y + step + 4, 4)

    def column(k):
        z_ = place(k)
        block = wblock(y, z_, core)
        if k == 0:
            send(block, block, R_Z + z_, at_z(lax.rem(zl + 1, 4)), zl < 3)
            send(block, block, R_Z + z_, at_z(lax.rem(zl + 3, 4)), zl > 0)
        else:
            arrived(block, R_Z + z_)
            onward = jnp.where(z_ < zl, zl + 1, zl - 1)
            there = (onward >= 0) & (onward < 4)
            send(block, block, R_Z + z_, at_z(lax.rem(onward + 4, 4)), there)
        send(block, block, R_Y + k, at_y(1))
        send(block, block, R_Y + 4 + k, at_y(-1))
        send(block, block, R_SC + k, sibling)

    def neighbour(k):
        z_ = place(k)
        for d, step in ((0, -1), (1, 1)):
            block = wblock(y_of(step), z_, core)
            arrived(block, R_Y + d * 4 + k)
            part = wblock(y_of(step), z_, core, d * 64, 64)
            send(part, part, R_H + d * 4 + k, at_y(-step))
            send(block, block, R_SY + d * 4 + k, sibling)

    def halves(k):
        z_ = place(k)
        for d in range(2):
            part = wblock(y_of(2), z_, core, d * 64, 64)
            arrived(part, R_H + d * 4 + k)
            send(part, part, R_SH + d * 4 + k, sibling)

    def dslot(z_):
        return dbuf.at[:, pl.ds(pl.multiple_of(z_ * 128, 128), 128)]

    def down_column(k):
        z_ = place(k)
        if k == 0:
            send(down, dslot(z_), R_DN + z_, at_z(lax.rem(zl + 1, 4)), zl < 3)
            send(down, dslot(z_), R_DN + z_, at_z(lax.rem(zl + 3, 4)), zl > 0)
        else:
            arrived(dslot(z_), R_DN + z_)
            onward = jnp.where(z_ < zl, zl + 1, zl - 1)
            there = (onward >= 0) & (onward < 4)
            send(dslot(z_), dslot(z_), R_DN + z_, at_z(lax.rem(onward + 4, 4)), there)

    column(0)

    cp_d = local(down, dslot(zl))
    cp_s = local(states, sbuf)
    cp_c = local(centroids, cbuf)
    cp_o = local(out_gain, og_in)
    lane = lax.broadcasted_iota(jnp.int32, (1, 128), 1)
    arow = jnp.full((1, 128), -1, jnp.int32)
    sub = lax.broadcasted_iota(jnp.int32, (PAD, 128), 0)
    acol = jnp.full((PAD, 128), -1, jnp.int32)
    lcol = jnp.ones((PAD, 128), jnp.int32)
    for p in range(PASSES):
        arow = jnp.where(lane == p, assign[p], arow)
        acol = jnp.where(sub == p, assign[p], acol)
        lcol = jnp.where(sub == p, lengths[p], lcol)
    abuf[lst] = arow

    def req_copy(i):
        peer = lax.rem(lst + i, 32)
        return pltpu.make_async_remote_copy(
            src_ref=abuf.at[lst], dst_ref=abuf.at[lst], send_sem=req_s.at[peer], recv_sem=req_r.at[lst],
            device_id=dev(list_=peer), device_id_type=MESH,
        )

    pl.loop(1, 32)(lambda i: req_copy(i).start())

    slot_row = lax.broadcasted_iota(jnp.int32, (PAD, ROWS), 0)
    slot_col = lax.broadcasted_iota(jnp.int32, (PAD, ROWS), 1)
    length = lcol[:, :1]
    in_pass = (slot_col >= slot_row * SEQ) & (slot_col < slot_row * SEQ + length) & (slot_row < PASSES)
    mask_s[...] = jnp.where(in_pass, 1.0, 0.0).astype(BF)
    inv_s[...] = 1.0 / lcol.astype(F32)
    cp_s.wait()
    smean[...] = jnp.dot(mask_s[...], sbuf[...], preferred_element_type=F32) * inv_s[:, :1]

    column(1)
    neighbour(0)

    def req_from(i):
        peer = lax.rem(lst + i, 32)
        pltpu.make_async_remote_copy(
            src_ref=abuf.at[peer], dst_ref=abuf.at[peer], send_sem=req_s.at[peer], recv_sem=req_r.at[peer],
            device_id=sibling, device_id_type=MESH,
        ).wait_recv()

    pl.loop(1, 32)(req_from)
    cp_c.wait()
    wanted = jnp.broadcast_to(abuf[...], (32, 8, 128))
    lanes3 = lax.broadcasted_iota(jnp.int32, (32, 8, 128), 2)
    odd3 = lax.rem(lax.broadcasted_iota(jnp.int32, (32, 8, 128), 1), 2) == 1
    mine = (wanted >= lst * OWN_ROWS) & (wanted < lst * OWN_ROWS + OWN_ROWS)
    first = jnp.min(jnp.where(mine, lanes3, 128), axis=2, keepdims=True)
    last = jnp.max(jnp.where(mine, lanes3, -1), axis=2, keepdims=True)
    chosen_lane = jnp.where(odd3, last, first)
    hit = mine & (lanes3 == chosen_lane)
    ids = jnp.sum(jnp.where(hit, wanted - lst * OWN_ROWS, 0), axis=2, keepdims=True)
    pick[...] = jnp.broadcast_to(ids, (32, 8, 128)).reshape(256, 128)
    cacc[...] = jnp.zeros_like(cacc)

    @pl.loop(0, 8)
    def _(kc):
        base = lax.broadcasted_iota(jnp.int32, (256, 512), 1) + kc * 512
        one = jnp.where(base == pick[:, :1], 1.0, 0.0).astype(BF)
        cacc[...] += jnp.dot(one, cbuf[pl.ds(pl.multiple_of(kc * 512, 512), 512), :], preferred_element_type=F32)

    quarter = lax.rem(lax.broadcasted_iota(jnp.int32, (256, 128), 0), 8) // 2
    out_rows = jnp.zeros((256, 128), F32)
    for q in range(4):
        out_rows = jnp.where(quarter == q, cacc[:, q * 128 : q * 128 + 128], out_rows)
    resp[...] = out_rows.reshape(32, 8, 128)
    gotc[lst] = resp[lst]

    def rsp_copy(i):
        peer = lax.rem(lst + i, 32)
        return pltpu.make_async_remote_copy(
            src_ref=resp.at[peer], dst_ref=gotc.at[lst], send_sem=rsp_s.at[peer], recv_sem=rsp_r.at[lst],
            device_id=dev(list_=peer), device_id_type=MESH,
        )

    pl.loop(1, 32)(lambda i: rsp_copy(i).start())

    column(2)
    neighbour(1)
    down_column(0)
    column(3)

    for half in range(2):
        arrived(xslot(1 - zh, half, x), R_CR + half)
        for step in (1, -1, 2):
            send(xslot(1 - zh, half, x), xslot(1 - zh, half, x), R_X + 8 + x * 2 + half, at_x(step))

    neighbour(2)
    down_column(1)
    neighbour(3)
    down_column(2)

    for cp in cps_x:
        cp.wait()
    for crossed, z_hi in ((0, zh), (1, 1 - zh)):
        for step in (1, -1, 2):
            x_ = lax.rem(x + step + 4, 4)
            for half in range(2):
                arrived(xslot(z_hi, half, x_), R_X + crossed * 8 + x_ * 2 + half)

    @pl.loop(0, ROWS // 32)
    def _(r):
        rows = pl.ds(pl.multiple_of(r * 32, 32), 32)
        total = jnp.zeros((32, 128), F32)
        for yy in range(4):
            for c in range(8):
                v = xbuf[yy, rows, c * 128 : c * 128 + 128].astype(F32)
                total = total + v * v
        mean = jnp.sum(total, axis=1, keepdims=True) / WIDTH
        scale_s[rows, :] = jnp.broadcast_to(lax.rsqrt(mean + 1e-05), (32, 128))

    def product(yy, start, depth, init):
        @pl.loop(0, TILES)
        def _(j):
            cols = pl.ds(pl.multiple_of(j * 256, 256), 256)
            ks = pl.ds(start, depth)
            r = jnp.dot(xbuf[yy, :, ks], wbuf[yy, ks, cols], preferred_element_type=F32)
            if init:
                acc[j] = r
            else:
                acc[j] += r

    for k in range(4):
        arrived(wblock(y, place(k), 1 - core), R_SC + k)
    product(y, 0, 1024, True)
    for d, step in ((0, -1), (1, 1)):
        for k in range(4):
            arrived(wblock(y_of(step), place(k), 1 - core), R_SY + d * 4 + k)
        product(y_of(step), 0, 1024, False)
    for k in range(4):
        halves(k)
        for d in range(2):
            arrived(wblock(y_of(2), place(k), 1 - core, d * 64, 64), R_SH + d * 4 + k)
        if k < 3:
            product(y_of(2), pl.multiple_of(place(k) * 256, 256), 256, False)
    down_column(3)
    cp_d.wait()
    cp_o.wait()

    yy = y_of(2)
    ks = pl.ds(pl.multiple_of(place(3) * 256, 256), 256)
    for j in range(TILES):
        r = acc[j] + jnp.dot(xbuf[yy, :, ks], wbuf[yy, ks, j * 256 : j * 256 + 256], preferred_element_type=F32)
        g = r[:, :128] * scale_s[...]
        u = r[:, 128:] * scale_s[...]
        h = (g / (1.0 + jnp.exp(-g)) * u).astype(BF)
        pooled_h = jnp.dot(mask_s[...], h, preferred_element_type=F32) * inv_s[...]
        hb[me_g, :, j * 128 : j * 128 + 128] = pooled_h.astype(BF)

    for i in range(1, 8):
        g_ = lax.rem(me_g + i, 8)
        send(hb.at[me_g], hb.at[me_g], R_G + me_g, dev(list_=zl * 8 + g_))

    def rsp_from(i):
        peer = lax.rem(lst + i, 32)
        pltpu.make_async_remote_copy(
            src_ref=gotc.at[peer], dst_ref=gotc.at[peer], send_sem=rsp_s.at[peer], recv_sem=rsp_r.at[peer],
            device_id=sibling, device_id_type=MESH,
        ).wait_recv()

    pl.loop(1, 32)(rsp_from)
    own_col = acol >> 12
    own_row = jnp.where(lane < PASSES, arow >> 12, -1)
    before = (own_col == own_row) & (lax.broadcasted_iota(jnp.int32, (PAD, 128), 1) < sub)
    slot = jnp.max(jnp.where(before, 1, 0), axis=1, keepdims=True)
    wide = lax.broadcasted_iota(jnp.int32, (PAD, 256), 1)
    table = gotc[...].reshape(256, 128).astype(BF)
    for q in range(4):
        one = jnp.where(wide == own_col[:, :1] * 8 + q * 2 + slot, 1.0, 0.0).astype(BF)
        chosen_s[:, q * 128 : q * 128 + 128] = jnp.dot(one, table, preferred_element_type=F32)

    for i in range(1, 8):
        g_ = lax.rem(me_g + i, 8)
        arrived(hb.at[g_], R_G + g_)

    for z_ in range(4):
        term = jnp.dot(hb[...].reshape(8 * PAD, HID), dbuf[:, z_ * 128 : z_ * 128 + 128], preferred_element_type=F32)
        tf[z_] = term
        tb[z_] = term.astype(BF)
    for step in (1, -1, 2):
        x_ = lax.rem(x + step + 4, 4)
        send(tb.at[x_], r1b.at[x], R_1 + x, at_x(step))
    q_sum = tf[x]
    for step in (1, -1, 2):
        x_ = lax.rem(x + step + 4, 4)
        arrived(r1b.at[x_], R_1 + x_)
        q_sum = q_sum + r1b[x_].astype(F32)
    qs[...] = q_sum.reshape(8, PAD, 128)

    slot2 = zh * 4 + lax.rem(y, 2) * 2 + core
    side = y // 2
    for i in range(8):
        g_ = lax.rem(me_g + i, 8)
        target = dev(list_=zl * 8 + g_, tensor=x * 2 + side)
        cond = (zh != side) if i == 0 else None
        send(qs.at[g_, pl.ds(0, PASSES)], rb.at[slot2], R_2 + slot2, target, cond)

    @pl.when(zh == side)
    def _():
        rb[slot2] = qs[me_g, :PASSES, :]

    for s in range(8):
        own = (zh == s // 4) & (y == zh * 2 + (s % 4) // 2) & (core == s % 2)

        @pl.when(jnp.logical_not(own))
        def _():
            arrived(rb.at[s], R_2 + s)

    pooled = []
    squares = jnp.zeros((PASSES, 128), F32)
    for i in range(4):
        v = smean[:PASSES, i * 128 : i * 128 + 128] + rb[i] + rb[4 + i]
        squares = squares + v * v
        pooled.append(v)
    sb[ten] = jnp.broadcast_to(jnp.sum(squares, axis=1, keepdims=True), (PASSES, 128))
    for i in range(1, 8):
        t_ = lax.rem(ten + i, 8)
        send(sb.at[ten], sb.at[ten], R_3 + ten, dev(tensor=t_))
    for i in range(1, 8):
        t_ = lax.rem(ten + i, 8)
        arrived(sb.at[t_], R_3 + t_)
    total = sb[0]
    for t_ in range(1, 8):
        total = total + sb[t_]
    norm = lax.rsqrt(total / WIDTH + 1e-05)
    for i in range(4):
        cols = slice(i * 128, i * 128 + 128)
        e = pooled[i] * norm * og_in[:, cols]
        emb_out[:, cols] = e
        res_out[:, cols] = e - chosen_s[:PASSES, cols]

    for cp, cond in sends:
        if cond is None:
            cp.wait_send()
        else:
            pl.when(cond)(cp.wait_send)
    pl.loop(1, 32)(lambda i: req_copy(i).wait_send())
    pl.loop(1, 32)(lambda i: rsp_copy(i).wait_send())


def per_device(
    states, lengths, assign, norm_gain, gate_weight, up_weight, down_weight, out_gain, centroids
):
    any_ = pl.BlockSpec(memory_space=pl.ANY)
    smem = pl.BlockSpec(memory_space=pltpu.SMEM)
    vmem = pl.BlockSpec(memory_space=pltpu.VMEM)
    out = jax.ShapeDtypeStruct((PASSES, PART), F32)
    return pl.pallas_call(
        kernel,
        out_shape=(out, out),
        in_specs=[smem, smem] + [any_] * 7,
        out_specs=(vmem, vmem),
        scratch_shapes=[
            pltpu.VMEM((4, 1024, 2 * HID), BF),
            pltpu.VMEM((4, ROWS, 1024), BF),
            pltpu.VMEM((TILES, ROWS, 256), F32),
            pltpu.VMEM((OWN_ROWS, PART), BF),
            pltpu.VMEM((HID, 512), BF),
            pltpu.VMEM((ROWS, PART), BF),
            pltpu.VMEM((128, HID), BF),
            pltpu.VMEM((128, HID), BF),
            pltpu.VMEM((32, 128), F32),
            pltpu.VMEM((1, PART), F32),
            pltpu.VMEM((ROWS, 128), F32),
            pltpu.VMEM((PAD, ROWS), BF),
            pltpu.VMEM((PAD, 128), F32),
            pltpu.VMEM((8, PAD, HID), BF),
            pltpu.VMEM((4, 8 * PAD, 128), F32),
            pltpu.VMEM((4, 8 * PAD, 128), BF),
            pltpu.VMEM((4, 8 * PAD, 128), BF),
            pltpu.VMEM((8, PAD, 128), F32),
            pltpu.VMEM((8, PASSES, 128), F32),
            pltpu.VMEM((8, PASSES, 128), F32),
            pltpu.VMEM((32, 1, 128), jnp.int32),
            pltpu.VMEM((256, 128), jnp.int32),
            pltpu.VMEM((256, 512), F32),
            pltpu.VMEM((32, 8, 128), F32),
            pltpu.VMEM((32, 8, 128), F32),
            pltpu.VMEM((PAD, PART), F32),
            pltpu.VMEM((PAD, PART), F32),
            pltpu.SemaphoreType.DMA((N_SEND,)),
            pltpu.SemaphoreType.DMA((R_END,)),
            pltpu.SemaphoreType.DMA((12,)),
            pltpu.SemaphoreType.DMA((32,)),
            pltpu.SemaphoreType.DMA((32,)),
            pltpu.SemaphoreType.DMA((32,)),
            pltpu.SemaphoreType.DMA((32,)),
        ],
        compiler_params=pltpu.CompilerParams(has_side_effects=True, vmem_limit_bytes=56 << 20),
        name="passages",
    )(
        lengths,
        assign,
        states.reshape(ROWS, PART),
        norm_gain.reshape(32, 128),
        gate_weight,
        up_weight,
        down_weight,
        out_gain.reshape(1, PART),
        centroids,
    )


def solution(mesh):
    return jax.shard_map(
        per_device,
        mesh=mesh,
        in_specs=(
            P("list", None, "tensor"),
            P("list"),
            P("list"),
            P(),
            P("list", "tensor"),
            P("list", "tensor"),
            P("tensor", "list"),
            P("tensor"),
            P("list", "tensor"),
        ),
        out_specs=(P("list", "tensor"), P("list", "tensor")),
        check_vma=False,
    )
```

```python
import functools

import jax
import jax.numpy as jnp
from jax import lax
from jax.experimental import pallas as pl
from jax.experimental.pallas import tpu as pltpu
from jax.sharding import PartitionSpec as P

MESH = pl.DeviceIdType.MESH
BF = jnp.bfloat16
F32 = jnp.float32

PASSES, SEQ, PART, WIDTH = 24, 16, 512, 4096
ROWS = PASSES * SEQ
HID = 896
TILES = HID // 128
PAD = 32
OWN_ROWS = 4096

R_Z = 0
R_Y = 4
R_H = 12
R_SC = 20
R_SY = 24
R_SH = 32
R_DN = 40
R_CR = 44
R_X = 46
R_G = 62
R_1 = 66
R_2 = 70
R_3 = 74
R_DS = 82
R_END = 86
N_SEND = 96


def kernel(
    lengths, assign, states, gain, gate, up, down, out_gain, centroids,
    emb_out, res_out,
    wbuf, xbuf, acc, cbuf, dbuf, sbuf, g_in, u_in, gain_in, og_in,
    scale_s, mask_s, inv_s, hb, tf, tb, r1b, qs, rb, sb, abuf, pick, cacc, resp, gotc, chosen_s, smean,
    ss, rs, ls, req_s, req_r, rsp_s, rsp_r,
):
    lst = lax.axis_index("list")
    ten = lax.axis_index("tensor")
    core = lax.rem(lst, 2)
    y = lax.rem(lst // 2, 4)
    zl = lst // 8
    x = ten // 2
    zh = lax.rem(ten, 2)
    me_g = lax.rem(lst, 8)

    def dev(list_=None, tensor=None):
        return {"list": lst if list_ is None else list_, "tensor": ten if tensor is None else tensor}

    def at_z(z):
        return dev(list_=z * 8 + me_g)

    def at_y(step):
        return dev(list_=zl * 8 + lax.rem(y + step + 4, 4) * 2 + core)

    def at_x(step):
        return dev(tensor=lax.rem(x + step + 4, 4) * 2 + zh)

    sibling = dev(list_=lst + 1 - 2 * core)
    partner = dev(tensor=x * 2 + 1 - zh)

    sends = []

    def send(src, dst, recv, device, cond=None):
        n = len(sends)
        cp = pltpu.make_async_remote_copy(
            src_ref=src, dst_ref=dst, send_sem=ss.at[n], recv_sem=rs.at[recv],
            device_id=device, device_id_type=MESH,
        )
        sends.append((cp, cond))
        if cond is None:
            cp.start()
        else:
            pl.when(cond)(cp.start)

    def arrived(dst, recv):
        pltpu.make_async_remote_copy(
            src_ref=dst, dst_ref=dst, send_sem=ss.at[0], recv_sem=rs.at[recv],
            device_id=sibling, device_id_type=MESH,
        ).wait_recv()

    locals_ = []

    def local(src, dst):
        cp = pltpu.make_async_copy(src, dst, ls.at[len(locals_)])
        locals_.append(cp)
        cp.start()
        return cp

    def dslot(z_, c_):
        return dbuf.at[:, pl.ds(pl.multiple_of(z_ * 256 + c_ * 128, 128), 128)]

    def xslot(z_hi, half, x_):
        return xbuf.at[z_hi * 2 + half, :, pl.ds(pl.multiple_of(x_ * 256, 256), 256)]

    def xslot(z_hi, half, x_):
        return xbuf.at[z_hi * 2 + half, :, pl.ds(pl.multiple_of(x_ * 256, 256), 256)]

    cps_w = [local(gate, g_in), local(up, u_in), local(gain, gain_in)]
    cps_x = [local(states.at[:, pl.ds(half * 256, 256)], xslot(zh, half, x)) for half in range(2)]
    cp_d = local(down, dslot(zl, core))
    cp_s = local(states, sbuf)
    cp_c = local(centroids, cbuf)
    cp_o = local(out_gain, og_in)
    barrier = pltpu.get_barrier_semaphore()

    def greet_list(i):
        pl.semaphore_signal(barrier, inc=1, device_id=dev(list_=lax.rem(lst + i, 32)), device_id_type=MESH)

    def greet_tensor(i):
        pl.semaphore_signal(barrier, inc=1, device_id=dev(tensor=lax.rem(ten + i, 8)), device_id_type=MESH)

    def greet_across(i):
        there = dev(list_=zl * 8 + lax.rem(y + i, 4) * 2 + core, tensor=x * 2 + 1 - zh)
        pl.semaphore_signal(barrier, inc=1, device_id=there, device_id_type=MESH)

    pl.loop(1, 32)(greet_list)
    pl.loop(1, 8)(greet_tensor)
    pl.loop(1, 4)(greet_across)
    pl.semaphore_wait(barrier, 31 + 7 + 3)
    for step in (1, -1, 2):
        for half in range(2):
            send(states.at[:, pl.ds(half * 256, 256)], xslot(zh, half, x), R_X + x * 2 + half, at_x(step))

    def cross(n):
        half = lax.rem(y + n, 2)
        send(states.at[:, pl.ds(pl.multiple_of(half * 256, 256), 256)], xslot(zh, half, x), R_CR + n, partner)

    def crossed(n):
        half = lax.rem(y + n, 2)
        block = xslot(1 - zh, half, x)
        arrived(block, R_CR + n)
        for step in (1, -1, 2):
            send(block, block, R_X + 8 + x * 2 + n, at_x(step))

    def x_arrived(n):
        for step in (1, -1, 2):
            x_ = lax.rem(x + step + 4, 4)
            if n is None:
                for half in range(2):
                    arrived(xslot(zh, half, x_), R_X + x_ * 2 + half)
            else:
                arrived(xslot(1 - zh, lax.rem(y + n, 2), x_), R_X + 8 + x_ * 2 + n)

    for cp in cps_w:
        cp.wait()
    eye = lax.broadcasted_iota(jnp.int32, (128, 128), 0) == lax.broadcasted_iota(jnp.int32, (128, 128), 1)
    gcol = jnp.sum(jnp.where(eye, gain_in[pl.ds(lst, 1), :], 0.0), axis=1, keepdims=True)
    own_rows = pl.ds(pl.multiple_of(zl * 256 + core * 128, 128), 128)
    for j in range(TILES):
        wbuf[y, own_rows, j * 256 : j * 256 + 128] = (g_in[:, j * 128 : j * 128 + 128].astype(F32) * gcol).astype(BF)
        wbuf[y, own_rows, j * 256 + 128 : j * 256 + 256] = (u_in[:, j * 128 : j * 128 + 128].astype(F32) * gcol).astype(BF)

    def wblock(y_, z_, c_, start=0, rows=128):
        return wbuf.at[y_, pl.ds(pl.multiple_of(z_ * 256 + c_ * 128 + start, 64), rows)]

    def place(k):
        inner = (zl == 1) | (zl == 2)
        o = jnp.where(inner, 1 - k, k) if k < 2 else k
        return jnp.where(zl < 2, o, 3 - o)

    def y_of(step):
        return lax.rem(y + step + 4, 4)

    def column(k):
        z_ = place(k)
        block = wblock(y, z_, core)
        if k == 0:
            send(block, block, R_Z + z_, at_z(lax.rem(zl + 1, 4)), zl < 3)
            send(block, block, R_Z + z_, at_z(lax.rem(zl + 3, 4)), zl > 0)
        else:
            arrived(block, R_Z + z_)
            onward = jnp.where(z_ < zl, zl + 1, zl - 1)
            there = (onward >= 0) & (onward < 4)
            send(block, block, R_Z + z_, at_z(lax.rem(onward + 4, 4)), there)
        send(block, block, R_Y + k, at_y(1))
        send(block, block, R_Y + 4 + k, at_y(-1))
        send(block, block, R_SC + k, sibling)

    def neighbour(k):
        z_ = place(k)
        for d, step in ((0, -1), (1, 1)):
            block = wblock(y_of(step), z_, core)
            arrived(block, R_Y + d * 4 + k)
            part = wblock(y_of(step), z_, core, d * 64, 64)
            send(part, part, R_H + d * 4 + k, at_y(-step))
            send(block, block, R_SY + d * 4 + k, sibling)

    def halves(k):
        z_ = place(k)
        for d in range(2):
            part = wblock(y_of(2), z_, core, d * 64, 64)
            arrived(part, R_H + d * 4 + k)
            send(part, part, R_SH + d * 4 + k, sibling)

    def down_column(k):
        z_ = place(k)
        block = dslot(z_, core)
        if k == 0:
            cp_d.wait()
            send(block, block, R_DN + z_, at_z(lax.rem(zl + 1, 4)), zl < 3)
            send(block, block, R_DN + z_, at_z(lax.rem(zl + 3, 4)), zl > 0)
        else:
            arrived(block, R_DN + z_)
            onward = jnp.where(z_ < zl, zl + 1, zl - 1)
            there = (onward >= 0) & (onward < 4)
            send(block, block, R_DN + z_, at_z(lax.rem(onward + 4, 4)), there)
        send(block, block, R_DS + k, sibling)

    def product(yy, k):
        ks = pl.ds(pl.multiple_of(place(k) * 256, 256), 256)
        for j in range(TILES):
            acc[j] += jnp.dot(xbuf[yy, :, ks], wbuf[yy, ks, j * 256 : j * 256 + 256], preferred_element_type=F32)

    def from_sibling_column(k):
        arrived(wblock(y, place(k), 1 - core), R_SC + k)

    def from_sibling_neighbour(d, k):
        arrived(wblock(y_of(2 * d - 1), place(k), 1 - core), R_SY + d * 4 + k)

    def from_sibling_halves(k):
        for d in range(2):
            arrived(wblock(y_of(2), place(k), 1 - core, d * 64, 64), R_SH + d * 4 + k)

    column(0)

    lane = lax.broadcasted_iota(jnp.int32, (1, 128), 1)
    arow = jnp.full((1, 128), -1, jnp.int32)
    sub = lax.broadcasted_iota(jnp.int32, (PAD, 128), 0)
    acol = jnp.full((PAD, 128), -1, jnp.int32)
    lcol = jnp.ones((PAD, 128), jnp.int32)
    for p in range(PASSES):
        arow = jnp.where(lane == p, assign[p], arow)
        acol = jnp.where(sub == p, assign[p], acol)
        lcol = jnp.where(sub == p, lengths[p], lcol)
    abuf[lst] = arow

    def req_copy(i):
        peer = lax.rem(lst + i, 32)
        return pltpu.make_async_remote_copy(
            src_ref=abuf.at[lst], dst_ref=abuf.at[lst], send_sem=req_s.at[peer], recv_sem=req_r.at[lst],
            device_id=dev(list_=peer), device_id_type=MESH,
        )

    pl.loop(1, 32)(lambda i: req_copy(i).start())

    slot_row = lax.broadcasted_iota(jnp.int32, (PAD, ROWS), 0)
    slot_col = lax.broadcasted_iota(jnp.int32, (PAD, ROWS), 1)
    length = lcol[:, :1]
    in_pass = (slot_col >= slot_row * SEQ) & (slot_col < slot_row * SEQ + length) & (slot_row < PASSES)
    mask_s[...] = jnp.where(in_pass, 1.0, 0.0).astype(BF)
    inv_s[...] = 1.0 / lcol.astype(F32)
    cp_s.wait()
    smean[...] = jnp.dot(mask_s[...], sbuf[...], preferred_element_type=F32) * inv_s[:, :1]

    column(1)
    cross(0)
    neighbour(0)

    def req_from(i):
        peer = lax.rem(lst + i, 32)
        pltpu.make_async_remote_copy(
            src_ref=abuf.at[peer], dst_ref=abuf.at[peer], send_sem=req_s.at[peer], recv_sem=req_r.at[peer],
            device_id=sibling, device_id_type=MESH,
        ).wait_recv()

    pl.loop(1, 32)(req_from)
    cp_c.wait()
    wanted = jnp.broadcast_to(abuf[...], (32, 8, 128))
    lanes3 = lax.broadcasted_iota(jnp.int32, (32, 8, 128), 2)
    odd3 = lax.rem(lax.broadcasted_iota(jnp.int32, (32, 8, 128), 1), 2) == 1
    mine = (wanted >= lst * OWN_ROWS) & (wanted < lst * OWN_ROWS + OWN_ROWS)
    first = jnp.min(jnp.where(mine, lanes3, 128), axis=2, keepdims=True)
    last = jnp.max(jnp.where(mine, lanes3, -1), axis=2, keepdims=True)
    chosen_lane = jnp.where(odd3, last, first)
    hit = mine & (lanes3 == chosen_lane)
    ids = jnp.sum(jnp.where(hit, wanted - lst * OWN_ROWS, 0), axis=2, keepdims=True)
    pick[...] = jnp.broadcast_to(ids, (32, 8, 128)).reshape(256, 128)
    cacc[...] = jnp.zeros_like(cacc)

    @pl.loop(0, 8)
    def _(kc):
        base = lax.broadcasted_iota(jnp.int32, (256, 512), 1) + kc * 512
        one = jnp.where(base == pick[:, :1], 1.0, 0.0).astype(BF)
        cacc[...] += jnp.dot(one, cbuf[pl.ds(pl.multiple_of(kc * 512, 512), 512), :], preferred_element_type=F32)

    quarter = lax.rem(lax.broadcasted_iota(jnp.int32, (256, 128), 0), 8) // 2
    out_rows = jnp.zeros((256, 128), F32)
    for q in range(4):
        out_rows = jnp.where(quarter == q, cacc[:, q * 128 : q * 128 + 128], out_rows)
    resp[...] = out_rows.reshape(32, 8, 128)
    gotc[lst] = resp[lst]

    def rsp_copy(i):
        peer = lax.rem(lst + i, 32)
        return pltpu.make_async_remote_copy(
            src_ref=resp.at[peer], dst_ref=gotc.at[lst], send_sem=rsp_s.at[peer], recv_sem=rsp_r.at[lst],
            device_id=dev(list_=peer), device_id_type=MESH,
        )

    pl.loop(1, 32)(lambda i: rsp_copy(i).start())

    column(2)
    cross(1)
    neighbour(1)
    halves(0)
    crossed(0)
    acc[...] = jnp.zeros_like(acc)
    for cp in cps_x:
        cp.wait()
    x_arrived(None)
    x_arrived(0)
    for k in range(3):
        from_sibling_column(k)
        product(y, k)
    column(3)
    down_column(0)
    crossed(1)
    from_sibling_column(3)
    product(y, 3)
    neighbour(2)
    y_a = jnp.where(y // 2 == zh, y + 1 - 2 * lax.rem(y, 2), lax.rem(y + 3 - 2 * lax.rem(y, 2), 4))
    y_b = lax.rem(y_a + 2, 4)
    for k in range(3):
        for d in range(2):
            from_sibling_neighbour(d, k)
        product(y_a, k)
    for k in (1, 2):
        halves(k)
    for k in range(3):
        from_sibling_halves(k)
        product(y_of(2), k)
    neighbour(3)
    down_column(1)
    for d in range(2):
        from_sibling_neighbour(d, 3)
    product(y_a, 3)
    x_arrived(1)
    @pl.loop(0, ROWS // 32)
    def _(r):
        rows = pl.ds(pl.multiple_of(r * 32, 32), 32)
        total = jnp.zeros((32, 128), F32)
        for yy in range(4):
            for c in range(8):
                v = xbuf[yy, rows, c * 128 : c * 128 + 128].astype(F32)
                total = total + v * v
        mean = jnp.sum(total, axis=1, keepdims=True) / WIDTH
        scale_s[rows, :] = jnp.broadcast_to(lax.rsqrt(mean + 1e-05), (32, 128))

    for k in range(4):
        product(y_b, k)
    down_column(2)
    halves(3)
    from_sibling_halves(3)
    yy = y_of(2)
    ks = pl.ds(pl.multiple_of(place(3) * 256, 256), 256)
    for j in range(TILES):
        r = acc[j] + jnp.dot(xbuf[yy, :, ks], wbuf[yy, ks, j * 256 : j * 256 + 256], preferred_element_type=F32)
        g = r[:, :128] * scale_s[...]
        u = r[:, 128:] * scale_s[...]
        h = (g / (1.0 + jnp.exp(-g)) * u).astype(BF)
        pooled_h = jnp.dot(mask_s[...], h, preferred_element_type=F32) * inv_s[...]
        hb[y, :, j * 128 : j * 128 + 128] = pooled_h.astype(BF)

    for step in (1, -1, 2):
        send(hb.at[y], hb.at[y], R_G + y, at_y(step))
    down_column(3)
    for k in range(4):
        arrived(dslot(place(k), 1 - core), R_DS + k)
    cp_o.wait()

    def rsp_from(i):
        peer = lax.rem(lst + i, 32)
        pltpu.make_async_remote_copy(
            src_ref=gotc.at[peer], dst_ref=gotc.at[peer], send_sem=rsp_s.at[peer], recv_sem=rsp_r.at[peer],
            device_id=sibling, device_id_type=MESH,
        ).wait_recv()

    pl.loop(1, 32)(rsp_from)
    own_col = acol >> 12
    own_row = jnp.where(lane < PASSES, arow >> 12, -1)
    before = (own_col == own_row) & (lax.broadcasted_iota(jnp.int32, (PAD, 128), 1) < sub)
    slot = jnp.max(jnp.where(before, 1, 0), axis=1, keepdims=True)
    wide = lax.broadcasted_iota(jnp.int32, (PAD, 256), 1)
    table = gotc[...].reshape(256, 128).astype(BF)
    for q in range(4):
        one = jnp.where(wide == own_col[:, :1] * 8 + q * 2 + slot, 1.0, 0.0).astype(BF)
        chosen_s[:, q * 128 : q * 128 + 128] = jnp.dot(one, table, preferred_element_type=F32)

    for step in (1, -1, 2):
        y_ = y_of(step)
        arrived(hb.at[y_], R_G + y_)

    for z_ in range(4):
        term = jnp.dot(hb[...].reshape(4 * PAD, HID), dbuf[:, z_ * 256 : z_ * 256 + 256], preferred_element_type=F32)
        tf[z_] = term
        tb[z_] = term.astype(BF)
    for step in (1, -1, 2):
        x_ = lax.rem(x + step + 4, 4)
        send(tb.at[x_], r1b.at[x], R_1 + x, at_x(step))
    q_sum = tf[x]
    for step in (1, -1, 2):
        x_ = lax.rem(x + step + 4, 4)
        arrived(r1b.at[x_], R_1 + x_)
        q_sum = q_sum + r1b[x_].astype(F32)
    qs[...] = q_sum.reshape(4, PAD, 256)
    slot2 = zh * 2 + lax.rem(y, 2)
    side = y // 2
    for step in (0, 1, -1, 2):
        y_ = y_of(step)
        target = dev(list_=zl * 8 + y_ * 2 + core, tensor=x * 2 + side)
        cond = (zh != side) if step == 0 else None
        send(qs.at[y_, pl.ds(0, PASSES)], rb.at[slot2], R_2 + slot2, target, cond)

    @pl.when(zh == side)
    def _():
        rb[slot2] = qs[y, :PASSES, :]

    for n in range(4):
        own = (zh == n // 2) & (y == zh * 2 + n % 2)

        @pl.when(jnp.logical_not(own))
        def _():
            arrived(rb.at[n], R_2 + n)

    pooled = []
    squares = jnp.zeros((PASSES, 128), F32)
    for i in range(4):
        half = slice(i % 2 * 128, i % 2 * 128 + 128)
        v = smean[:PASSES, i * 128 : i * 128 + 128] + rb[i // 2, :, half] + rb[2 + i // 2, :, half]
        squares = squares + v * v
        pooled.append(v)
    sb[ten] = jnp.broadcast_to(jnp.sum(squares, axis=1, keepdims=True), (PASSES, 128))
    for i in range(1, 8):
        t_ = lax.rem(ten + i, 8)
        send(sb.at[ten], sb.at[ten], R_3 + ten, dev(tensor=t_))
    for i in range(1, 8):
        t_ = lax.rem(ten + i, 8)
        arrived(sb.at[t_], R_3 + t_)
    total = sb[0]
    for t_ in range(1, 8):
        total = total + sb[t_]
    norm = lax.rsqrt(total / WIDTH + 1e-05)
    for i in range(4):
        cols = slice(i * 128, i * 128 + 128)
        e = pooled[i] * norm * og_in[:, cols]
        emb_out[:, cols] = e
        res_out[:, cols] = e - chosen_s[:PASSES, cols]

    for cp, cond in sends:
        if cond is None:
            cp.wait_send()
        else:
            pl.when(cond)(cp.wait_send)
    pl.loop(1, 32)(lambda i: req_copy(i).wait_send())
    pl.loop(1, 32)(lambda i: rsp_copy(i).wait_send())


def per_device(
    states, lengths, assign, norm_gain, gate_weight, up_weight, down_weight, out_gain, centroids
):
    any_ = pl.BlockSpec(memory_space=pl.ANY)
    smem = pl.BlockSpec(memory_space=pltpu.SMEM)
    vmem = pl.BlockSpec(memory_space=pltpu.VMEM)
    out = jax.ShapeDtypeStruct((PASSES, PART), F32)
    return pl.pallas_call(
        kernel,
        out_shape=(out, out),
        in_specs=[smem, smem] + [any_] * 7,
        out_specs=(vmem, vmem),
        scratch_shapes=[
            pltpu.VMEM((4, 1024, 2 * HID), BF),
            pltpu.VMEM((4, ROWS, 1024), BF),
            pltpu.VMEM((TILES, ROWS, 256), F32),
            pltpu.VMEM((OWN_ROWS, PART), BF),
            pltpu.VMEM((HID, 1024), BF),
            pltpu.VMEM((ROWS, PART), BF),
            pltpu.VMEM((128, HID), BF),
            pltpu.VMEM((128, HID), BF),
            pltpu.VMEM((32, 128), F32),
            pltpu.VMEM((1, PART), F32),
            pltpu.VMEM((ROWS, 128), F32),
            pltpu.VMEM((PAD, ROWS), BF),
            pltpu.VMEM((PAD, 128), F32),
            pltpu.VMEM((4, PAD, HID), BF),
            pltpu.VMEM((4, 4 * PAD, 256), F32),
            pltpu.VMEM((4, 4 * PAD, 256), BF),
            pltpu.VMEM((4, 4 * PAD, 256), BF),
            pltpu.VMEM((4, PAD, 256), F32),
            pltpu.VMEM((4, PASSES, 256), F32),
            pltpu.VMEM((8, PASSES, 128), F32),
            pltpu.VMEM((32, 1, 128), jnp.int32),
            pltpu.VMEM((256, 128), jnp.int32),
            pltpu.VMEM((256, 512), F32),
            pltpu.VMEM((32, 8, 128), F32),
            pltpu.VMEM((32, 8, 128), F32),
            pltpu.VMEM((PAD, PART), F32),
            pltpu.VMEM((PAD, PART), F32),
            pltpu.SemaphoreType.DMA((N_SEND,)),
            pltpu.SemaphoreType.DMA((R_END,)),
            pltpu.SemaphoreType.DMA((12,)),
            pltpu.SemaphoreType.DMA((32,)),
            pltpu.SemaphoreType.DMA((32,)),
            pltpu.SemaphoreType.DMA((32,)),
            pltpu.SemaphoreType.DMA((32,)),
        ],
        compiler_params=pltpu.CompilerParams(collective_id=0, has_side_effects=True, vmem_limit_bytes=56 << 20),
        name="passages",
    )(
        lengths,
        assign,
        states.reshape(ROWS, PART),
        norm_gain.reshape(32, 128),
        gate_weight,
        up_weight,
        down_weight,
        out_gain.reshape(1, PART),
        centroids,
    )


def solution(mesh):
    return jax.shard_map(
        per_device,
        mesh=mesh,
        in_specs=(
            P("list", None, "tensor"),
            P("list"),
            P("list"),
            P(),
            P("list", "tensor"),
            P("list", "tensor"),
            P("tensor", "list"),
            P("tensor"),
            P("list", "tensor"),
        ),
        out_specs=(P("list", "tensor"), P("list", "tensor")),
        check_vma=False,
    )
```

```python
import functools

import jax
import jax.numpy as jnp
from jax import lax
from jax.experimental import pallas as pl
from jax.experimental.pallas import tpu as pltpu
from jax.sharding import PartitionSpec as P

MESH = pl.DeviceIdType.MESH
BF = jnp.bfloat16
F32 = jnp.float32

PASSES, SEQ, PART, WIDTH = 24, 16, 512, 4096
ROWS = PASSES * SEQ
HID = 896
TILES = HID // 128
PAD = 32
OWN_ROWS = 4096

R_Z = 0
R_Y = 4
R_H = 12
R_SC = 16
R_SY = 20
R_SH = 24
R_DN = 28
R_DS = 32
R_CR = 33
R_X = 35
R_G = 39
R_1 = 40
R_2 = 41
R_3 = 42
R_REQ = 43
R_RSP = 44
R_END = 45
S_W, S_Z, S_X, S_CR, S_DZ, S_DS, S_G, S_1, S_2, S_3, S_REQ, S_RSP, S_END = range(13)


def kernel(
    lengths, assign, states, gain, gate, up, down, out_gain, centroids,
    out,
    wbuf, xbuf, acc, cbuf, dbuf, sbuf, g_in, u_in, gain_in, og_in,
    scale_s, mask_s, inv_s, hb, tf, tb, r1b, qs, rb, sb, abuf, pick, cacc, resp, gotc, chosen_s, smean, out_s,
    ss, rs, ls,
):
    lst = lax.axis_index("list")
    ten = lax.axis_index("tensor")
    core = lax.rem(lst, 2)
    y = lax.rem(lst // 2, 4)
    zl = lst // 8
    x = ten // 2
    zh = lax.rem(ten, 2)
    me_g = lax.rem(lst, 8)

    def dev(list_=None, tensor=None):
        return {"list": lst if list_ is None else list_, "tensor": ten if tensor is None else tensor}

    def at_z(z):
        return dev(list_=z * 8 + me_g)

    def at_y(step):
        return dev(list_=zl * 8 + lax.rem(y + step + 4, 4) * 2 + core)

    def at_x(step):
        return dev(tensor=lax.rem(x + step + 4, 4) * 2 + zh)

    sibling = dev(list_=lst + 1 - 2 * core)
    partner = dev(tensor=x * 2 + 1 - zh)

    def remote(src, dst, kind, recv, device):
        return pltpu.make_async_remote_copy(
            src_ref=src, dst_ref=dst, send_sem=ss.at[kind], recv_sem=rs.at[recv],
            device_id=device, device_id_type=MESH,
        )

    def send(src, dst, kind, recv, device, cond=None):
        cp = remote(src, dst, kind, recv, device)
        if cond is None:
            cp.start()
        else:
            pl.when(cond)(cp.start)

    def arrived(dst, recv):
        remote(dst, dst, 0, recv, sibling).wait_recv()

    def sent(src, kind):
        remote(src, src, kind, 0, sibling).wait_send()

    locals_ = []

    def local(src, dst):
        cp = pltpu.make_async_copy(src, dst, ls.at[len(locals_)])
        locals_.append(cp)
        cp.start()
        return cp

    def dslot(z_, c_):
        return dbuf.at[:, pl.ds(pl.multiple_of(z_ * 256 + c_ * 128, 128), 128)]

    def xslot(z_hi, half, x_):
        return xbuf.at[z_hi * 2 + half, :, pl.ds(pl.multiple_of(x_ * 256, 256), 256)]

    def xslot(z_hi, half, x_):
        return xbuf.at[z_hi * 2 + half, :, pl.ds(pl.multiple_of(x_ * 256, 256), 256)]

    cps_w = [local(gate, g_in), local(up, u_in), local(gain, gain_in)]
    cps_x = [local(states.at[:, pl.ds(half * 256, 256)], xslot(zh, half, x)) for half in range(2)]
    cp_d = local(down, dslot(zl, core))
    cp_s = local(states, sbuf)
    cp_c = local(centroids, cbuf)
    cp_o = local(out_gain, og_in)
    barrier = pltpu.get_barrier_semaphore()

    def greet_list(i):
        pl.semaphore_signal(barrier, inc=1, device_id=dev(list_=lax.rem(lst + i, 32)), device_id_type=MESH)

    def greet_tensor(i):
        pl.semaphore_signal(barrier, inc=1, device_id=dev(tensor=lax.rem(ten + i, 8)), device_id_type=MESH)

    def greet_across(i):
        there = dev(list_=zl * 8 + lax.rem(y + i, 4) * 2 + core, tensor=x * 2 + 1 - zh)
        pl.semaphore_signal(barrier, inc=1, device_id=there, device_id_type=MESH)

    pl.loop(1, 32)(greet_list)
    pl.loop(1, 8)(greet_tensor)
    pl.loop(1, 4)(greet_across)
    for cp in cps_w:
        cp.wait()
    eye = lax.broadcasted_iota(jnp.int32, (128, 128), 0) == lax.broadcasted_iota(jnp.int32, (128, 128), 1)
    gcol = jnp.sum(jnp.where(eye, gain_in[pl.ds(lst, 1), :], 0.0), axis=1, keepdims=True)
    own_rows = pl.ds(pl.multiple_of(y * 1024 + zl * 256 + core * 128, 128), 128)
    for j in range(TILES):
        wbuf[own_rows, j * 256 : j * 256 + 128] = (g_in[:, j * 128 : j * 128 + 128].astype(F32) * gcol).astype(BF)
        wbuf[own_rows, j * 256 + 128 : j * 256 + 256] = (u_in[:, j * 128 : j * 128 + 128].astype(F32) * gcol).astype(BF)

    pl.semaphore_wait(barrier, 31 + 7 + 3)
    for step in (1, -1, 2):
        for half in range(2):
            send(states.at[:, pl.ds(half * 256, 256)], xslot(zh, half, x), S_X, R_X + half, at_x(step))

    def cross(n):
        half = lax.rem(y + n, 2)
        send(states.at[:, pl.ds(pl.multiple_of(half * 256, 256), 256)], xslot(zh, half, x), S_CR, R_CR + n, partner)

    def crossed(n):
        half = lax.rem(y + n, 2)
        block = xslot(1 - zh, half, x)
        arrived(block, R_CR + n)
        for step in (1, -1, 2):
            send(block, block, S_X, R_X + 2 + n, at_x(step))

    def x_arrived(n):
        arrived(xbuf.at[0, :, pl.ds(0, 768)], R_X + n)

    def wblock(y_, z_, c_, start=0, rows=128):
        return wbuf.at[pl.ds(pl.multiple_of(y_ * 1024 + z_ * 256 + c_ * 128 + start, 64), rows)]

    def place(k):
        inner = (zl == 1) | (zl == 2)
        o = jnp.where(inner, 1 - k, k) if k < 2 else k
        return jnp.where(zl < 2, o, 3 - o)

    inner_z = (zl == 1) | (zl == 2)

    def y_of(step):
        return lax.rem(y + step + 4, 4)

    def column(k):
        z_ = place(k)
        block = wblock(y, z_, core)
        if k == 0:
            send(block, block, S_Z, R_Z + z_, at_z(lax.rem(zl + 1, 4)), zl < 3)
            send(block, block, S_Z, R_Z + z_, at_z(lax.rem(zl + 3, 4)), zl > 0)
        else:
            arrived(block, R_Z + z_)
            onward = jnp.where(z_ < zl, zl + 1, zl - 1)
            send(block, block, S_Z, R_Z + z_, at_z(lax.rem(onward + 4, 4)), inner_z)
        send(block, block, S_W, R_Y + k, at_y(1))
        send(block, block, S_W, R_Y + 4 + k, at_y(-1))
        send(block, block, S_W, R_SC + k, sibling)

    def neighbour(k):
        z_ = place(k)
        for d, step in ((0, -1), (1, 1)):
            block = wblock(y_of(step), z_, core)
            arrived(block, R_Y + d * 4 + k)
            part = wblock(y_of(step), z_, core, d * 64, 64)
            send(part, part, S_W, R_H + k, at_y(-step))
            send(block, block, S_W, R_SY + k, sibling)

    def halves(k):
        block = wblock(y_of(2), place(k), core)
        arrived(block, R_H + k)
        send(block, block, S_W, R_SH + k, sibling)

    def down_column(k):
        z_ = place(k)
        block = dslot(z_, core)
        if k == 0:
            cp_d.wait()
            send(block, block, S_DZ, R_DN + z_, at_z(lax.rem(zl + 1, 4)), zl < 3)
            send(block, block, S_DZ, R_DN + z_, at_z(lax.rem(zl + 3, 4)), zl > 0)
        else:
            arrived(block, R_DN + z_)
            onward = jnp.where(z_ < zl, zl + 1, zl - 1)
            send(block, block, S_DZ, R_DN + z_, at_z(lax.rem(onward + 4, 4)), inner_z)
        send(block, block, S_DS, R_DS, sibling)

    def product(yy, k):
        ks = pl.ds(pl.multiple_of(place(k) * 256, 256), 256)
        rows = pl.ds(pl.multiple_of(yy * 1024 + place(k) * 256, 256), 256)
        for j in range(TILES):
            acc[j] += jnp.dot(xbuf[yy, :, ks], wbuf[rows, j * 256 : j * 256 + 256], preferred_element_type=F32)

    def squares_of(yy, init):
        @pl.loop(0, ROWS // 32)
        def _(r):
            rows = pl.ds(pl.multiple_of(r * 32, 32), 32)
            total = jnp.zeros((32, 128), F32) if init else scale_s[rows, :]
            for c in range(8):
                v = xbuf[yy, rows, c * 128 : c * 128 + 128].astype(F32)
                total = total + v * v
            scale_s[rows, :] = total

    def from_sibling_column(k):
        arrived(wblock(y, place(k), 1 - core), R_SC + k)

    def from_sibling_neighbours(k):
        arrived(wbuf.at[pl.ds(0, 256)], R_SY + k)

    def from_sibling_halves(k):
        arrived(wblock(y_of(2), place(k), 1 - core), R_SH + k)

    column(0)

    lane = lax.broadcasted_iota(jnp.int32, (1, 128), 1)
    arow = jnp.full((1, 128), -1, jnp.int32)
    sub = lax.broadcasted_iota(jnp.int32, (PAD, 128), 0)
    acol = jnp.full((PAD, 128), -1, jnp.int32)
    lcol = jnp.ones((PAD, 128), jnp.int32)
    for p in range(PASSES):
        arow = jnp.where(lane == p, assign[p], arow)
        acol = jnp.where(sub == p, assign[p], acol)
        lcol = jnp.where(sub == p, lengths[p], lcol)
    abuf[lst] = arow

    @pl.loop(1, 32)
    def _(i):
        peer = lax.rem(lst + i, 32)
        send(abuf.at[lst], abuf.at[lst], S_REQ, R_REQ, dev(list_=peer))

    slot_row = lax.broadcasted_iota(jnp.int32, (PAD, ROWS), 0)
    slot_col = lax.broadcasted_iota(jnp.int32, (PAD, ROWS), 1)
    length = lcol[:, :1]
    in_pass = (slot_col >= slot_row * SEQ) & (slot_col < slot_row * SEQ + length) & (slot_row < PASSES)
    mask_s[...] = jnp.where(in_pass, 1.0, 0.0).astype(BF)
    inv_s[...] = 1.0 / lcol.astype(F32)
    cp_s.wait()
    smean[...] = jnp.dot(mask_s[...], sbuf[...], preferred_element_type=F32) * inv_s[:, :1]

    column(1)
    cross(0)
    pl.when(inner_z)(lambda: column(2))
    neighbour(0)

    arrived(abuf.at[pl.ds(0, 31)], R_REQ)
    cp_c.wait()
    wanted = jnp.broadcast_to(abuf[...], (32, 8, 128))
    lanes3 = lax.broadcasted_iota(jnp.int32, (32, 8, 128), 2)
    odd3 = lax.rem(lax.broadcasted_iota(jnp.int32, (32, 8, 128), 1), 2) == 1
    mine = (wanted >= lst * OWN_ROWS) & (wanted < lst * OWN_ROWS + OWN_ROWS)
    first = jnp.min(jnp.where(mine, lanes3, 128), axis=2, keepdims=True)
    last = jnp.max(jnp.where(mine, lanes3, -1), axis=2, keepdims=True)
    chosen_lane = jnp.where(odd3, last, first)
    hit = mine & (lanes3 == chosen_lane)
    ids = jnp.sum(jnp.where(hit, wanted - lst * OWN_ROWS, 0), axis=2, keepdims=True)
    pick[...] = jnp.broadcast_to(ids, (32, 8, 128)).reshape(256, 128)
    cacc[...] = jnp.zeros_like(cacc)

    @pl.loop(0, 8)
    def _(kc):
        base = lax.broadcasted_iota(jnp.int32, (256, 512), 1) + kc * 512
        one = jnp.where(base == pick[:, :1], 1.0, 0.0).astype(BF)
        cacc[...] += jnp.dot(one, cbuf[pl.ds(pl.multiple_of(kc * 512, 512), 512), :], preferred_element_type=F32)

    quarter = lax.rem(lax.broadcasted_iota(jnp.int32, (256, 128), 0), 8) // 2
    out_rows = jnp.zeros((256, 128), F32)
    for q in range(4):
        out_rows = jnp.where(quarter == q, cacc[:, q * 128 : q * 128 + 128], out_rows)
    resp[...] = out_rows.reshape(32, 8, 128)
    gotc[lst] = resp[lst]

    @pl.loop(1, 32)
    def _(i):
        peer = lax.rem(lst + i, 32)
        send(resp.at[peer], gotc.at[lst], S_RSP, R_RSP, dev(list_=peer))

    outer_z = jnp.logical_not(inner_z)
    pl.when(inner_z)(lambda: column(3))
    neighbour(1)
    pl.when(outer_z)(lambda: column(2))
    cross(1)
    for cp in cps_x:
        cp.wait()
    for half in range(2):
        x_arrived(half)
    acc[...] = jnp.zeros_like(acc)
    squares_of(zh * 2, True)
    squares_of(zh * 2 + 1, False)
    halves(0)
    crossed(0)
    y_a = jnp.where(y // 2 == zh, y + 1 - 2 * lax.rem(y, 2), lax.rem(y + 3 - 2 * lax.rem(y, 2), 4))
    y_b = lax.rem(y_a + 2, 4)
    for k in range(2):
        from_sibling_neighbours(k)
        product(y_a, k)
    neighbour(2)
    pl.when(jnp.logical_not(inner_z))(lambda: column(3))
    crossed(1)
    down_column(0)
    halves(1)
    from_sibling_neighbours(2)
    product(y_a, 2)
    x_arrived(2)
    for k in range(4):
        from_sibling_column(k)
        product(y, k)
    squares_of((1 - zh) * 2 + lax.rem(y, 2), False)
    neighbour(3)
    halves(2)
    down_column(1)
    pl.when(inner_z)(lambda: down_column(2))
    for k in range(3):
        from_sibling_halves(k)
        product(y_of(2), k)
    from_sibling_neighbours(3)
    product(y_a, 3)
    x_arrived(3)
    squares_of((1 - zh) * 2 + lax.rem(y + 1, 2), False)
    for k in range(4):
        product(y_b, k)
    scale_s[...] = jnp.broadcast_to(
        lax.rsqrt(jnp.sum(scale_s[...], axis=1, keepdims=True) / WIDTH + 1e-05), (ROWS, 128)
    )
    halves(3)
    pl.when(inner_z)(lambda: down_column(3))
    from_sibling_halves(3)
    yy = y_of(2)
    ks = pl.ds(pl.multiple_of(place(3) * 256, 256), 256)
    wrows = pl.ds(pl.multiple_of(yy * 1024 + place(3) * 256, 256), 256)
    for j in range(TILES):
        r = acc[j] + jnp.dot(xbuf[yy, :, ks], wbuf[wrows, j * 256 : j * 256 + 256], preferred_element_type=F32)
        g = r[:, :128] * scale_s[...]
        u = r[:, 128:] * scale_s[...]
        h = (g / (1.0 + jnp.exp(-g)) * u).astype(BF)
        pooled_h = jnp.dot(mask_s[...], h, preferred_element_type=F32) * inv_s[...]
        hb[y, :, j * 128 : j * 128 + 128] = pooled_h.astype(BF)

    for step in (1, -1, 2):
        send(hb.at[y], hb.at[y], S_G, R_G, at_y(step))
    @pl.when(jnp.logical_not(inner_z))
    def _():
        down_column(2)
        down_column(3)

    arrived(dbuf.at[:, pl.ds(0, 512)], R_DS)
    cp_o.wait()

    arrived(gotc.at[pl.ds(0, 31)], R_RSP)
    own_col = acol >> 12
    own_row = jnp.where(lane < PASSES, arow >> 12, -1)
    before = (own_col == own_row) & (lax.broadcasted_iota(jnp.int32, (PAD, 128), 1) < sub)
    slot = jnp.max(jnp.where(before, 1, 0), axis=1, keepdims=True)
    wide = lax.broadcasted_iota(jnp.int32, (PAD, 256), 1)
    table = gotc[...].reshape(256, 128).astype(BF)
    for q in range(4):
        one = jnp.where(wide == own_col[:, :1] * 8 + q * 2 + slot, 1.0, 0.0).astype(BF)
        chosen_s[:, q * 128 : q * 128 + 128] = jnp.dot(one, table, preferred_element_type=F32)

    arrived(hb.at[pl.ds(0, 3)], R_G)

    for z_ in range(4):
        term = jnp.dot(hb[...].reshape(4 * PAD, HID), dbuf[:, z_ * 256 : z_ * 256 + 256], preferred_element_type=F32)
        term = jnp.concatenate([term[g * PAD : g * PAD + PASSES] for g in range(4)], axis=0)
        tf[z_] = term
        tb[z_] = term.astype(BF)
    for step in (1, -1, 2):
        x_ = lax.rem(x + step + 4, 4)
        send(tb.at[x_], r1b.at[x], S_1, R_1, at_x(step))
    arrived(r1b.at[pl.ds(0, 3)], R_1)
    q_sum = tf[x]
    for step in (1, -1, 2):
        x_ = lax.rem(x + step + 4, 4)
        q_sum = q_sum + r1b[x_].astype(F32)
    qs[...] = q_sum.reshape(4, PASSES, 256)
    slot2 = zh * 2 + lax.rem(y, 2)
    side = y // 2
    for step in (0, 1, -1, 2):
        y_ = y_of(step)
        target = dev(list_=zl * 8 + y_ * 2 + core, tensor=x * 2 + side)
        cond = (zh != side) if step == 0 else None
        send(qs.at[y_], rb.at[slot2], S_2, R_2, target, cond)

    @pl.when(zh == side)
    def _():
        rb[slot2] = qs[y]

    @pl.when(zh == side)
    def _():
        arrived(rb.at[pl.ds(0, 3)], R_2)

    @pl.when(zh != side)
    def _():
        arrived(rb, R_2)

    pooled = []
    squares = jnp.zeros((PASSES, 128), F32)
    for i in range(4):
        half = slice(i % 2 * 128, i % 2 * 128 + 128)
        v = smean[:PASSES, i * 128 : i * 128 + 128] + rb[i // 2, :, half] + rb[2 + i // 2, :, half]
        squares = squares + v * v
        pooled.append(v)
    turn = lax.broadcasted_iota(jnp.int32, (PASSES, 128), 0) == lax.broadcasted_iota(jnp.int32, (PASSES, 128), 1)
    sb[ten] = jnp.sum(jnp.where(turn, jnp.sum(squares, axis=1, keepdims=True), 0.0), axis=0, keepdims=True)
    for i in range(1, 8):
        t_ = lax.rem(ten + i, 8)
        send(sb.at[ten], sb.at[ten], S_3, R_3, dev(tensor=t_))

    sent(wbuf.at[pl.ds(0, 28 * 128)], S_W)
    sent(xbuf.at[pl.ds(0, 3)], S_X)
    sent(xbuf.at[0, :, pl.ds(0, 512)], S_CR)
    sent(dbuf.at[:, pl.ds(0, 512)], S_DS)
    sent(hb.at[pl.ds(0, 3)], S_G)
    sent(tb.at[pl.ds(0, 3)], S_1)
    sent(abuf.at[pl.ds(0, 31)], S_REQ)
    sent(resp.at[pl.ds(0, 31)], S_RSP)

    @pl.when(inner_z)
    def _():
        sent(wbuf.at[pl.ds(0, 5 * 128)], S_Z)
        sent(dbuf.at[:, pl.ds(0, 5 * 128)], S_DZ)

    @pl.when(jnp.logical_not(inner_z))
    def _():
        sent(wbuf.at[pl.ds(0, 128)], S_Z)
        sent(dbuf.at[:, pl.ds(0, 128)], S_DZ)

    @pl.when(zh == side)
    def _():
        sent(qs.at[pl.ds(0, 3)], S_2)

    @pl.when(zh != side)
    def _():
        sent(qs, S_2)

    arrived(sb.at[pl.ds(0, 7)], R_3)
    total = sb[0]
    for t_ in range(1, 8):
        total = total + sb[t_]
    total = jnp.sum(jnp.where(turn, total, 0.0), axis=1, keepdims=True)
    norm = lax.rsqrt(total / WIDTH + 1e-05)
    for i in range(4):
        cols = slice(i * 128, i * 128 + 128)
        out_s[:, cols] = pooled[i] * norm * og_in[:, cols]
        out_s[:, i * 128 + PART : i * 128 + PART + 128] = chosen_s[:PASSES, cols]
    local(out_s, out).wait()
    sent(sb.at[pl.ds(0, 7)], S_3)


def per_device(
    states, lengths, assign, norm_gain, gate_weight, up_weight, down_weight, out_gain, centroids
):
    any_ = pl.BlockSpec(memory_space=pl.ANY)
    smem = pl.BlockSpec(memory_space=pltpu.SMEM)
    both = pl.pallas_call(
        kernel,
        out_shape=jax.ShapeDtypeStruct((PASSES, 2 * PART), F32),
        in_specs=[smem, smem] + [any_] * 7,
        out_specs=any_,
        scratch_shapes=[
            pltpu.VMEM((WIDTH, 2 * HID), BF),
            pltpu.VMEM((4, ROWS, 1024), BF),
            pltpu.VMEM((TILES, ROWS, 256), F32),
            pltpu.VMEM((OWN_ROWS, PART), BF),
            pltpu.VMEM((HID, 1024), BF),
            pltpu.VMEM((ROWS, PART), BF),
            pltpu.VMEM((128, HID), BF),
            pltpu.VMEM((128, HID), BF),
            pltpu.VMEM((32, 128), F32),
            pltpu.VMEM((1, PART), F32),
            pltpu.VMEM((ROWS, 128), F32),
            pltpu.VMEM((PAD, ROWS), BF),
            pltpu.VMEM((PAD, 128), F32),
            pltpu.VMEM((4, PAD, HID), BF),
            pltpu.VMEM((4, 4 * PASSES, 256), F32),
            pltpu.VMEM((4, 4 * PASSES, 256), BF),
            pltpu.VMEM((4, 4 * PASSES, 256), BF),
            pltpu.VMEM((4, PASSES, 256), F32),
            pltpu.VMEM((4, PASSES, 256), F32),
            pltpu.VMEM((8, 1, 128), F32),
            pltpu.VMEM((32, 1, 128), jnp.int32),
            pltpu.VMEM((256, 128), jnp.int32),
            pltpu.VMEM((256, 512), F32),
            pltpu.VMEM((32, 8, 128), F32),
            pltpu.VMEM((32, 8, 128), F32),
            pltpu.VMEM((PAD, PART), F32),
            pltpu.VMEM((PAD, PART), F32),
            pltpu.VMEM((PASSES, 2 * PART), F32),
            pltpu.SemaphoreType.DMA((S_END,)),
            pltpu.SemaphoreType.DMA((R_END,)),
            pltpu.SemaphoreType.DMA((10,)),
        ],
        compiler_params=pltpu.CompilerParams(collective_id=0, has_side_effects=True, vmem_limit_bytes=56 << 20),
        name="passages",
    )(
        lengths,
        assign,
        states.reshape(ROWS, PART),
        norm_gain.reshape(32, 128),
        gate_weight,
        up_weight,
        down_weight,
        out_gain.reshape(1, PART),
        centroids,
    )
    embedding = both[:, :PART]
    return embedding, embedding - both[:, PART:]


def solution(mesh):
    return jax.shard_map(
        per_device,
        mesh=mesh,
        in_specs=(
            P("list", None, "tensor"),
            P("list"),
            P("list"),
            P(),
            P("list", "tensor"),
            P("list", "tensor"),
            P("tensor", "list"),
            P("tensor"),
            P("list", "tensor"),
        ),
        out_specs=(P("list", "tensor"), P("list", "tensor")),
        check_vma=False,
    )
```

```python
import functools

import jax
import jax.numpy as jnp
from jax import lax
from jax.experimental import pallas as pl
from jax.experimental.pallas import tpu as pltpu
from jax.sharding import PartitionSpec as P

MESH = pl.DeviceIdType.MESH
BF = jnp.bfloat16
F32 = jnp.float32

PASSES, SEQ, PART, WIDTH = 24, 16, 512, 4096
ROWS = PASSES * SEQ
HID = 896
TILES = HID // 128
PAD = 32
OWN_ROWS = 4096

R_Z = 0
R_Y = 4
R_H = 12
R_SC = 16
R_SY = 20
R_SH = 24
R_DN = 28
R_DS = 32
R_CR = 33
R_X = 35
R_G = 39
R_1 = 42
R_2 = 46
R_3 = 47
R_REQ = 48
R_RSP = 49
R_MEAN = 50
R_END = 51
S_W, S_Z, S_X, S_CR, S_DZ, S_DS, S_G, S_1, S_2, S_3, S_REQ, S_RSP, S_MEAN, S_END = range(14)


def kernel(
    lengths, assign, states, gain, gate, up, down, out_gain, centroids,
    out,
    wbuf, xbuf, acc, cbuf, dbuf, sbuf, g_in, u_in, gain_in, og_in,
    scale_s, mask_s, inv_s, hb, tf, tb, r1b, qs, rb, rb7, mine_m, other_m, sb, abuf, pick, cacc, resp, gotc, chosen_s, smean, out_s,
    ss, rs, ls,
):
    lst = lax.axis_index("list")
    ten = lax.axis_index("tensor")
    core = lax.rem(lst, 2)
    y = lax.rem(lst // 2, 4)
    zl = lst // 8
    x = ten // 2
    zh = lax.rem(ten, 2)
    me_g = lax.rem(lst, 8)

    def dev(list_=None, tensor=None):
        return {"list": lst if list_ is None else list_, "tensor": ten if tensor is None else tensor}

    def at_z(z):
        return dev(list_=z * 8 + me_g)

    def at_y(step):
        return dev(list_=zl * 8 + lax.rem(y + step + 4, 4) * 2 + core)

    def at_x(step):
        return dev(tensor=lax.rem(x + step + 4, 4) * 2 + zh)

    sibling = dev(list_=lst + 1 - 2 * core)
    partner = dev(tensor=x * 2 + 1 - zh)

    def remote(src, dst, kind, recv, device):
        return pltpu.make_async_remote_copy(
            src_ref=src, dst_ref=dst, send_sem=ss.at[kind], recv_sem=rs.at[recv],
            device_id=device, device_id_type=MESH,
        )

    def send(src, dst, kind, recv, device, cond=None):
        cp = remote(src, dst, kind, recv, device)
        if cond is None:
            cp.start()
        else:
            pl.when(cond)(cp.start)

    def arrived(dst, recv):
        remote(dst, dst, 0, recv, sibling).wait_recv()

    def sent(src, kind):
        remote(src, src, kind, 0, sibling).wait_send()

    locals_ = []

    def local(src, dst):
        cp = pltpu.make_async_copy(src, dst, ls.at[len(locals_)])
        locals_.append(cp)
        cp.start()
        return cp

    def dslot(z_, c_):
        return dbuf.at[:, pl.ds(pl.multiple_of(z_ * 256 + c_ * 128, 128), 128)]

    def xslot(z_hi, half, x_):
        return xbuf.at[z_hi * 2 + half, :, pl.ds(pl.multiple_of(x_ * 256, 256), 256)]

    def xslot(z_hi, half, x_):
        return xbuf.at[z_hi * 2 + half, :, pl.ds(pl.multiple_of(x_ * 256, 256), 256)]

    cps_w = [local(gate, g_in), local(up, u_in), local(gain, gain_in)]
    cps_x = [local(states.at[:, pl.ds(half * 256, 256)], xslot(zh, half, x)) for half in range(2)]
    cp_d = local(down, dslot(zl, core))
    cp_s = local(states, sbuf)
    cp_c = local(centroids, cbuf)
    cp_o = local(out_gain, og_in)
    barrier = pltpu.get_barrier_semaphore()

    def greet_list(i):
        pl.semaphore_signal(barrier, inc=1, device_id=dev(list_=lax.rem(lst + i, 32)), device_id_type=MESH)

    def greet_x(i):
        pl.semaphore_signal(barrier, inc=1, device_id=dev(tensor=lax.rem(ten + 2 * i, 8)), device_id_type=MESH)

    def greet_across(i):
        there = dev(list_=zl * 8 + lax.rem(y + i, 4) * 2 + core, tensor=x * 2 + 1 - zh)
        pl.semaphore_signal(barrier, inc=1, device_id=there, device_id_type=MESH)

    pl.loop(0, 4)(greet_across)
    pl.loop(1, 4)(greet_x)
    pl.loop(1, 32)(greet_list)
    for cp in cps_w:
        cp.wait()
    eye = lax.broadcasted_iota(jnp.int32, (128, 128), 0) == lax.broadcasted_iota(jnp.int32, (128, 128), 1)
    gcol = jnp.sum(jnp.where(eye, gain_in[pl.ds(lst, 1), :], 0.0), axis=1, keepdims=True)
    own_rows = pl.ds(pl.multiple_of(y * 1024 + zl * 256 + core * 128, 128), 128)
    for j in range(TILES):
        wbuf[own_rows, j * 256 : j * 256 + 128] = (g_in[:, j * 128 : j * 128 + 128].astype(F32) * gcol).astype(BF)
        wbuf[own_rows, j * 256 + 128 : j * 256 + 256] = (u_in[:, j * 128 : j * 128 + 128].astype(F32) * gcol).astype(BF)

    pl.semaphore_wait(barrier, 31 + 3 + 4)
    for step in (1, -1, 2):
        for half in range(2):
            send(states.at[:, pl.ds(half * 256, 256)], xslot(zh, half, x), S_X, R_X + half, at_x(step))

    def cross(n):
        half = lax.rem(y + n, 2)
        send(states.at[:, pl.ds(pl.multiple_of(half * 256, 256), 256)], xslot(zh, half, x), S_CR, R_CR + n, partner)

    def crossed(n):
        half = lax.rem(y + n, 2)
        block = xslot(1 - zh, half, x)
        arrived(block, R_CR + n)
        for step in (1, -1, 2):
            send(block, block, S_X, R_X + 2 + n, at_x(step))

    def x_arrived(n):
        arrived(xbuf.at[0, :, pl.ds(0, 768)], R_X + n)

    def wblock(y_, z_, c_, start=0, rows=128):
        return wbuf.at[pl.ds(pl.multiple_of(y_ * 1024 + z_ * 256 + c_ * 128 + start, 64), rows)]

    def place(k):
        inner = (zl == 1) | (zl == 2)
        o = jnp.where(inner, 1 - k, k) if k < 2 else k
        return jnp.where(zl < 2, o, 3 - o)

    inner_z = (zl == 1) | (zl == 2)

    def y_of(step):
        return lax.rem(y + step + 4, 4)

    def column(k):
        z_ = place(k)
        block = wblock(y, z_, core)
        if k == 0:
            send(block, block, S_Z, R_Z + z_, at_z(lax.rem(zl + 1, 4)), zl < 3)
            send(block, block, S_Z, R_Z + z_, at_z(lax.rem(zl + 3, 4)), zl > 0)
        else:
            arrived(block, R_Z + z_)
            onward = jnp.where(z_ < zl, zl + 1, zl - 1)
            send(block, block, S_Z, R_Z + z_, at_z(lax.rem(onward + 4, 4)), inner_z)
        send(block, block, S_W, R_Y + k, at_y(1))
        send(block, block, S_W, R_Y + 4 + k, at_y(-1))
        send(block, block, S_W, R_SC + k, sibling)

    def neighbour(k):
        z_ = place(k)
        for d, step in ((0, -1), (1, 1)):
            block = wblock(y_of(step), z_, core)
            arrived(block, R_Y + d * 4 + k)
            part = wblock(y_of(step), z_, core, d * 64, 64)
            send(part, part, S_W, R_H + k, at_y(-step))
            send(block, block, S_W, R_SY + k, sibling)

    def halves(k):
        block = wblock(y_of(2), place(k), core)
        arrived(block, R_H + k)
        send(block, block, S_W, R_SH + k, sibling)

    def down_column(k):
        z_ = place(k)
        block = dslot(z_, core)
        if k == 0:
            cp_d.wait()
            send(block, block, S_DZ, R_DN + z_, at_z(lax.rem(zl + 1, 4)), zl < 3)
            send(block, block, S_DZ, R_DN + z_, at_z(lax.rem(zl + 3, 4)), zl > 0)
        else:
            arrived(block, R_DN + z_)
            onward = jnp.where(z_ < zl, zl + 1, zl - 1)
            send(block, block, S_DZ, R_DN + z_, at_z(lax.rem(onward + 4, 4)), inner_z)
        send(block, block, S_DS, R_DS, sibling)

    def product(yy, k):
        ks = pl.ds(pl.multiple_of(place(k) * 256, 256), 256)
        rows = pl.ds(pl.multiple_of(yy * 1024 + place(k) * 256, 256), 256)
        for j in range(TILES):
            acc[j] += jnp.dot(xbuf[yy, :, ks], wbuf[rows, j * 256 : j * 256 + 256], preferred_element_type=F32)

    def squares_of(yy, init):
        @pl.loop(0, ROWS // 32)
        def _(r):
            rows = pl.ds(pl.multiple_of(r * 32, 32), 32)
            total = jnp.zeros((32, 128), F32) if init else scale_s[rows, :]
            for c in range(8):
                v = xbuf[yy, rows, c * 128 : c * 128 + 128].astype(F32)
                total = total + v * v
            scale_s[rows, :] = total

    def from_sibling_column(k):
        arrived(wblock(y, place(k), 1 - core), R_SC + k)

    def from_sibling_neighbours(k):
        arrived(wbuf.at[pl.ds(0, 256)], R_SY + k)

    def from_sibling_halves(k):
        arrived(wblock(y_of(2), place(k), 1 - core), R_SH + k)

    def packed(v):
        return jnp.concatenate([v[:, :128], v[:, 128:]], axis=0)

    column(0)

    lane = lax.broadcasted_iota(jnp.int32, (1, 128), 1)
    arow = jnp.full((1, 128), -1, jnp.int32)
    sub = lax.broadcasted_iota(jnp.int32, (PAD, 128), 0)
    acol = jnp.full((PAD, 128), -1, jnp.int32)
    lcol = jnp.ones((PAD, 128), jnp.int32)
    for p in range(PASSES):
        arow = jnp.where(lane == p, assign[p], arow)
        acol = jnp.where(sub == p, assign[p], acol)
        lcol = jnp.where(sub == p, lengths[p], lcol)
    abuf[lst] = arow

    @pl.loop(1, 32)
    def _(i):
        peer = lax.rem(lst + i, 32)
        send(abuf.at[lst], abuf.at[lst], S_REQ, R_REQ, dev(list_=peer))

    slot_row = lax.broadcasted_iota(jnp.int32, (PAD, ROWS), 0)
    slot_col = lax.broadcasted_iota(jnp.int32, (PAD, ROWS), 1)
    length = lcol[:, :1]
    in_pass = (slot_col >= slot_row * SEQ) & (slot_col < slot_row * SEQ + length) & (slot_row < PASSES)
    mask_s[...] = jnp.where(in_pass, 1.0, 0.0).astype(BF)
    inv_s[...] = 1.0 / lcol.astype(F32)
    cp_s.wait()
    smean[...] = jnp.dot(mask_s[...], sbuf[...], preferred_element_type=F32) * inv_s[:, :1]
    for i in range(2):
        mine_m[i] = packed(smean[:PASSES, i * 256 : i * 256 + 256]).astype(BF)
    send(mine_m, other_m, S_MEAN, R_MEAN, partner)

    column(1)
    pl.when(inner_z)(lambda: column(2))
    neighbour(0)

    arrived(abuf.at[pl.ds(0, 31)], R_REQ)
    cp_c.wait()
    wanted = jnp.broadcast_to(abuf[...], (32, 8, 128))
    lanes3 = lax.broadcasted_iota(jnp.int32, (32, 8, 128), 2)
    odd3 = lax.rem(lax.broadcasted_iota(jnp.int32, (32, 8, 128), 1), 2) == 1
    mine = (wanted >= lst * OWN_ROWS) & (wanted < lst * OWN_ROWS + OWN_ROWS)
    first = jnp.min(jnp.where(mine, lanes3, 128), axis=2, keepdims=True)
    last = jnp.max(jnp.where(mine, lanes3, -1), axis=2, keepdims=True)
    chosen_lane = jnp.where(odd3, last, first)
    hit = mine & (lanes3 == chosen_lane)
    ids = jnp.sum(jnp.where(hit, wanted - lst * OWN_ROWS, 0), axis=2, keepdims=True)
    pick[...] = jnp.broadcast_to(ids, (32, 8, 128)).reshape(256, 128)
    cacc[...] = jnp.zeros_like(cacc)

    @pl.loop(0, 8)
    def _(kc):
        base = lax.broadcasted_iota(jnp.int32, (256, 512), 1) + kc * 512
        one = jnp.where(base == pick[:, :1], 1.0, 0.0).astype(BF)
        cacc[...] += jnp.dot(one, cbuf[pl.ds(pl.multiple_of(kc * 512, 512), 512), :], preferred_element_type=F32)

    quarter = lax.rem(lax.broadcasted_iota(jnp.int32, (256, 128), 0), 8) // 2
    out_rows = jnp.zeros((256, 128), F32)
    for q in range(4):
        out_rows = jnp.where(quarter == q, cacc[:, q * 128 : q * 128 + 128], out_rows)
    resp[...] = out_rows.reshape(32, 8, 128)
    gotc[lst] = resp[lst]

    @pl.loop(1, 32)
    def _(i):
        peer = lax.rem(lst + i, 32)
        send(resp.at[peer], gotc.at[lst], S_RSP, R_RSP, dev(list_=peer))

    cross(0)
    outer_z = jnp.logical_not(inner_z)
    pl.when(inner_z)(lambda: column(3))
    neighbour(1)
    pl.when(outer_z)(lambda: column(2))
    for cp in cps_x:
        cp.wait()
    for half in range(2):
        x_arrived(half)
    acc[...] = jnp.zeros_like(acc)
    squares_of(zh * 2, True)
    squares_of(zh * 2 + 1, False)
    halves(0)
    crossed(0)
    y_a = jnp.where(y // 2 == zh, y + 1 - 2 * lax.rem(y, 2), lax.rem(y + 3 - 2 * lax.rem(y, 2), 4))
    y_b = lax.rem(y_a + 2, 4)
    for k in range(2):
        from_sibling_neighbours(k)
        product(y_a, k)
    pl.when(inner_z)(lambda: cross(1))
    neighbour(2)
    pl.when(outer_z)(lambda: column(3))
    pl.when(outer_z)(lambda: cross(1))
    crossed(1)
    down_column(0)
    halves(1)
    from_sibling_neighbours(2)
    product(y_a, 2)
    x_arrived(2)
    for k in range(4):
        from_sibling_column(k)
        product(y, k)
    squares_of((1 - zh) * 2 + lax.rem(y, 2), False)
    halves(2)
    for k in range(2):
        from_sibling_halves(k)
        product(y_of(2), k)
    down_column(1)
    pl.when(inner_z)(lambda: down_column(2))
    neighbour(3)
    from_sibling_halves(2)
    product(y_of(2), 2)
    from_sibling_neighbours(3)
    product(y_a, 3)
    pl.when(inner_z)(lambda: down_column(3))
    x_arrived(3)
    squares_of((1 - zh) * 2 + lax.rem(y + 1, 2), False)
    for k in range(4):
        product(y_b, k)
    scale_s[...] = jnp.broadcast_to(
        lax.rsqrt(jnp.sum(scale_s[...], axis=1, keepdims=True) / WIDTH + 1e-05), (ROWS, 128)
    )
    halves(3)
    from_sibling_halves(3)
    around = (2, 1, -1)

    def send_pooled(start, width):
        for n, step in enumerate(around):
            part = hb.at[y, :, pl.ds(start, width)]
            send(part, part, S_G, R_G + n, at_y(step))

    yy = y_of(2)
    ks = pl.ds(pl.multiple_of(place(3) * 256, 256), 256)
    wrows = pl.ds(pl.multiple_of(yy * 1024 + place(3) * 256, 256), 256)
    for j in range(TILES):
        r = acc[j] + jnp.dot(xbuf[yy, :, ks], wbuf[wrows, j * 256 : j * 256 + 256], preferred_element_type=F32)
        g = r[:, :128] * scale_s[...]
        u = r[:, 128:] * scale_s[...]
        h = (g * (0.5 + 0.5 * jnp.tanh(0.5 * g)) * u).astype(BF)
        pooled_h = jnp.dot(mask_s[...], h, preferred_element_type=F32) * inv_s[...]
        hb[y, :, j * 128 : j * 128 + 128] = pooled_h.astype(BF)
        if j == 3:
            send_pooled(0, 512)

    send_pooled(512, HID - 512)
    @pl.when(outer_z)
    def _():
        down_column(2)
        down_column(3)


    arrived(dbuf.at[:, pl.ds(0, 512)], R_DS)
    cp_o.wait()

    arrived(gotc.at[pl.ds(0, 31)], R_RSP)
    own_col = acol >> 12
    own_row = jnp.where(lane < PASSES, arow >> 12, -1)
    before = (own_col == own_row) & (lax.broadcasted_iota(jnp.int32, (PAD, 128), 1) < sub)
    slot = jnp.max(jnp.where(before, 1, 0), axis=1, keepdims=True)
    wide = lax.broadcasted_iota(jnp.int32, (PAD, 256), 1)
    table = gotc[...].reshape(256, 128).astype(BF)
    for q in range(4):
        one = jnp.where(wide == own_col[:, :1] * 8 + q * 2 + slot, 1.0, 0.0).astype(BF)
        chosen_s[:, q * 128 : q * 128 + 128] = jnp.dot(one, table, preferred_element_type=F32)


    passes_y = ((0, 0), (1, 2), (-1, 1), (2, 0))
    for n, (step, came) in enumerate(passes_y):
        y_ = y_of(step)
        if step != 0:
            arrived(hb.at[y_], R_G + came)
        term = jnp.dot(hb[y_], dbuf[...], preferred_element_type=F32)
        for z_ in range(4):
            v = packed(term[:PASSES, z_ * 256 : z_ * 256 + 256])
            tf[z_, y_] = v
            tb[z_, y_] = v.astype(BF)
        for x_step in (2, 1, -1):
            x_ = lax.rem(x + x_step + 4, 4)
            send(tb.at[x_, y_], r1b.at[x, y_], S_1, R_1 + n, at_x(x_step))
    for n, (step, _) in enumerate(passes_y):
        y_ = y_of(step)
        arrived(r1b.at[pl.ds(0, 3), 0], R_1 + n)
        v = tf[x, y_]
        for x_step in (1, -1, 2):
            v = v + r1b[lax.rem(x + x_step + 4, 4), y_].astype(F32)
        qs[y_] = v.astype(BF)
        for far in (1, 0):
            if step == 0 and far == 0:
                rb[zh, y] = qs[y]
            else:
                target = dev(list_=zl * 8 + y_ * 2 + core, tensor=x * 2 + lax.rem(zh + far, 2))
                send(qs.at[y_], rb.at[zh, y], S_2, R_2, target)
    arrived(other_m, R_MEAN)
    arrived(rb7.at[pl.ds(0, 7)], R_2)
    pooled = []
    squares = jnp.zeros((PASSES, 128), F32)
    for i in range(2):
        v = rb[0, zh * 2 + i].astype(F32) + rb[1, zh * 2 + i].astype(F32) + packed(smean[:PASSES, i * 256 : i * 256 + 256])
        w = rb[0, (1 - zh) * 2 + i].astype(F32) + rb[1, (1 - zh) * 2 + i].astype(F32) + other_m[i].astype(F32)
        both = v * v + w * w
        squares = squares + both[:PASSES] + both[PASSES:]
        pooled += [v[:PASSES], v[PASSES:]]
    turn = lax.broadcasted_iota(jnp.int32, (PASSES, 128), 0) == lax.broadcasted_iota(jnp.int32, (PASSES, 128), 1)
    sb[x] = jnp.sum(jnp.where(turn, jnp.sum(squares, axis=1, keepdims=True), 0.0), axis=0, keepdims=True)
    for step in (2, 1, -1):
        send(sb.at[x], sb.at[x], S_3, R_3, at_x(step))
    sent(wbuf.at[pl.ds(0, 28 * 128)], S_W)
    sent(xbuf.at[pl.ds(0, 3)], S_X)
    sent(xbuf.at[0, :, pl.ds(0, 512)], S_CR)
    sent(dbuf.at[:, pl.ds(0, 512)], S_DS)
    sent(hb.at[pl.ds(0, 3)], S_G)
    sent(tb.at[pl.ds(0, 3)], S_1)
    sent(abuf.at[pl.ds(0, 31)], S_REQ)
    sent(resp.at[pl.ds(0, 31)], S_RSP)

    @pl.when(inner_z)
    def _():
        sent(wbuf.at[pl.ds(0, 5 * 128)], S_Z)
        sent(dbuf.at[:, pl.ds(0, 5 * 128)], S_DZ)

    @pl.when(jnp.logical_not(inner_z))
    def _():
        sent(wbuf.at[pl.ds(0, 128)], S_Z)
        sent(dbuf.at[:, pl.ds(0, 128)], S_DZ)

    sent(rb7.at[pl.ds(0, 7)], S_2)
    sent(mine_m, S_MEAN)
    arrived(sb.at[pl.ds(0, 3)], R_3)
    total = sb[0]
    for x_ in range(1, 4):
        total = total + sb[x_]
    total = jnp.sum(jnp.where(turn, total, 0.0), axis=1, keepdims=True)
    norm = lax.rsqrt(total / WIDTH + 1e-05)
    for i in range(4):
        cols = slice(i * 128, i * 128 + 128)
        out_s[:, cols] = pooled[i] * norm * og_in[:, cols]
        out_s[:, i * 128 + PART : i * 128 + PART + 128] = chosen_s[:PASSES, cols]
    local(out_s, out).wait()
    sent(sb.at[pl.ds(0, 3)], S_3)


def per_device(
    states, lengths, assign, norm_gain, gate_weight, up_weight, down_weight, out_gain, centroids
):
    any_ = pl.BlockSpec(memory_space=pl.ANY)
    smem = pl.BlockSpec(memory_space=pltpu.SMEM)
    both = pl.pallas_call(
        kernel,
        out_shape=jax.ShapeDtypeStruct((PASSES, 2 * PART), F32),
        in_specs=[smem, smem] + [any_] * 7,
        out_specs=any_,
        scratch_shapes=[
            pltpu.VMEM((WIDTH, 2 * HID), BF),
            pltpu.VMEM((4, ROWS, 1024), BF),
            pltpu.VMEM((TILES, ROWS, 256), F32),
            pltpu.VMEM((OWN_ROWS, PART), BF),
            pltpu.VMEM((HID, 1024), BF),
            pltpu.VMEM((ROWS, PART), BF),
            pltpu.VMEM((128, HID), BF),
            pltpu.VMEM((128, HID), BF),
            pltpu.VMEM((32, 128), F32),
            pltpu.VMEM((1, PART), F32),
            pltpu.VMEM((ROWS, 128), F32),
            pltpu.VMEM((PAD, ROWS), BF),
            pltpu.VMEM((PAD, 128), F32),
            pltpu.VMEM((4, PAD, HID), BF),
            pltpu.VMEM((4, 4, 2 * PASSES, 128), F32),
            pltpu.VMEM((4, 4, 2 * PASSES, 128), BF),
            pltpu.VMEM((4, 4, 2 * PASSES, 128), BF),
            pltpu.VMEM((4, 2 * PASSES, 128), BF),
            pltpu.VMEM((2, 4, 2 * PASSES, 128), BF),
            pltpu.VMEM((8, 2 * PASSES, 128), BF),
            pltpu.VMEM((2, 2 * PASSES, 128), BF),
            pltpu.VMEM((2, 2 * PASSES, 128), BF),
            pltpu.VMEM((4, 1, 128), F32),
            pltpu.VMEM((32, 1, 128), jnp.int32),
            pltpu.VMEM((256, 128), jnp.int32),
            pltpu.VMEM((256, 512), F32),
            pltpu.VMEM((32, 8, 128), F32),
            pltpu.VMEM((32, 8, 128), F32),
            pltpu.VMEM((PAD, PART), F32),
            pltpu.VMEM((PAD, PART), F32),
            pltpu.VMEM((PASSES, 2 * PART), F32),
            pltpu.SemaphoreType.DMA((S_END,)),
            pltpu.SemaphoreType.DMA((R_END,)),
            pltpu.SemaphoreType.DMA((10,)),
        ],
        compiler_params=pltpu.CompilerParams(collective_id=0, has_side_effects=True, vmem_limit_bytes=56 << 20),
        name="passages",
    )(
        lengths,
        assign,
        states.reshape(ROWS, PART),
        norm_gain.reshape(32, 128),
        gate_weight,
        up_weight,
        down_weight,
        out_gain.reshape(1, PART),
        centroids,
    )
    embedding = both[:, :PART]
    return embedding, embedding - both[:, PART:]


def solution(mesh):
    return jax.shard_map(
        per_device,
        mesh=mesh,
        in_specs=(
            P("list", None, "tensor"),
            P("list"),
            P("list"),
            P(),
            P("list", "tensor"),
            P("list", "tensor"),
            P("tensor", "list"),
            P("tensor"),
            P("list", "tensor"),
        ),
        out_specs=(P("list", "tensor"), P("list", "tensor")),
        check_vma=False,
    )
```

```python
import functools

import jax
import jax.numpy as jnp
from jax import lax
from jax.experimental import pallas as pl
from jax.experimental.pallas import tpu as pltpu
from jax.sharding import PartitionSpec as P

MESH = pl.DeviceIdType.MESH
BF = jnp.bfloat16
F32 = jnp.float32

PASSES, SEQ, PART, WIDTH = 24, 16, 512, 4096
ROWS = PASSES * SEQ
HID = 896
TILES = HID // 128
PAD = 32
OWN_ROWS = 4096

R_Z = 0
R_Y = 4
R_H = 12
R_SC = 16
R_SY = 20
R_SH = 24
R_DN = 28
R_DS = 32
R_CR = 33
R_X = 35
R_G = 39
R_1 = 42
R_2 = 46
R_3 = 47
R_REQ = 48
R_RSP = 49
R_MEAN = 50
R_CB = 51
R_XB = 53
R_G2 = 55
R_END = 58
S_W, S_Z, S_X, S_CR, S_DZ, S_DS, S_G, S_1, S_2, S_3, S_REQ, S_RSP, S_MEAN, S_G2, S_END = range(15)


def kernel(
    lengths, assign, states, gain, gate, up, down, out_gain, centroids,
    out,
    wbuf, xbuf, acc, cbuf, dbuf, sbuf, g_in, u_in, gain_in, og_in,
    scale_s, mask_s, inv_s, hb, hb2, hid, tf, tb, r1b, qs, rb, rb7, mine_m, other_m, sb, abuf, pick, cacc, resp, gotc, chosen_s, smean, out_s,
    ss, rs, ls,
):
    lst = lax.axis_index("list")
    ten = lax.axis_index("tensor")
    core = lax.rem(lst, 2)
    y = lax.rem(lst // 2, 4)
    zl = lst // 8
    x = ten // 2
    zh = lax.rem(ten, 2)
    me_g = lax.rem(lst, 8)

    def dev(list_=None, tensor=None):
        return {"list": lst if list_ is None else list_, "tensor": ten if tensor is None else tensor}

    def at_z(z):
        return dev(list_=z * 8 + me_g)

    def at_y(step):
        return dev(list_=zl * 8 + lax.rem(y + step + 4, 4) * 2 + core)

    def at_x(step):
        return dev(tensor=lax.rem(x + step + 4, 4) * 2 + zh)

    sibling = dev(list_=lst + 1 - 2 * core)
    partner = dev(tensor=x * 2 + 1 - zh)

    def remote(src, dst, kind, recv, device):
        return pltpu.make_async_remote_copy(
            src_ref=src, dst_ref=dst, send_sem=ss.at[kind], recv_sem=rs.at[recv],
            device_id=device, device_id_type=MESH,
        )

    def send(src, dst, kind, recv, device, cond=None):
        cp = remote(src, dst, kind, recv, device)
        if cond is None:
            cp.start()
        else:
            pl.when(cond)(cp.start)

    def arrived(dst, recv):
        remote(dst, dst, 0, recv, sibling).wait_recv()

    def sent(src, kind):
        remote(src, src, kind, 0, sibling).wait_send()

    locals_ = []

    def local(src, dst):
        cp = pltpu.make_async_copy(src, dst, ls.at[len(locals_)])
        locals_.append(cp)
        cp.start()
        return cp

    def dslot(z_, c_):
        return dbuf.at[:, pl.ds(pl.multiple_of(z_ * 256 + c_ * 128, 128), 128)]

    def xslot(z_hi, half, x_):
        return xbuf.at[z_hi * 2 + half, :, pl.ds(pl.multiple_of(x_ * 256, 256), 256)]

    def xslot(z_hi, half, x_):
        return xbuf.at[z_hi * 2 + half, :, pl.ds(pl.multiple_of(x_ * 256, 256), 256)]

    cps_w = [local(gate, g_in), local(up, u_in), local(gain, gain_in)]
    cps_x = [local(states.at[:, pl.ds(half * 256, 256)], xslot(zh, half, x)) for half in range(2)]
    cp_d = local(down, dslot(zl, core))
    cp_s = local(states, sbuf)
    cp_c = local(centroids, cbuf)
    cp_o = local(out_gain, og_in)
    barrier = pltpu.get_barrier_semaphore()

    def greet_list(i):
        pl.semaphore_signal(barrier, inc=1, device_id=dev(list_=lax.rem(lst + i, 32)), device_id_type=MESH)

    def greet_x(i):
        pl.semaphore_signal(barrier, inc=1, device_id=dev(tensor=lax.rem(ten + 2 * i, 8)), device_id_type=MESH)

    def greet_across(i):
        there = dev(list_=zl * 8 + lax.rem(y + i, 4) * 2 + core, tensor=x * 2 + 1 - zh)
        pl.semaphore_signal(barrier, inc=1, device_id=there, device_id_type=MESH)

    pl.loop(0, 4)(greet_across)
    pl.loop(1, 4)(greet_x)
    pl.loop(1, 32)(greet_list)
    for cp in cps_w:
        cp.wait()
    eye = lax.broadcasted_iota(jnp.int32, (128, 128), 0) == lax.broadcasted_iota(jnp.int32, (128, 128), 1)
    gcol = jnp.sum(jnp.where(eye, gain_in[pl.ds(lst, 1), :], 0.0), axis=1, keepdims=True)
    own_rows = pl.ds(pl.multiple_of(y * 1024 + zl * 256 + core * 128, 128), 128)
    for j in range(TILES):
        wbuf[own_rows, j * 256 : j * 256 + 128] = (g_in[:, j * 128 : j * 128 + 128].astype(F32) * gcol).astype(BF)
        wbuf[own_rows, j * 256 + 128 : j * 256 + 256] = (u_in[:, j * 128 : j * 128 + 128].astype(F32) * gcol).astype(BF)

    pl.semaphore_wait(barrier, 31 + 3 + 4)
    for step in (1, -1, 2):
        for half in range(2):
            send(states.at[:, pl.ds(half * 256, 256)], xslot(zh, half, x), S_X, R_X + half, at_x(step))

    def piece(z_hi, n, p, x_):
        rows = pl.ds(0, ROWS) if n == 0 else pl.ds(p * (ROWS // 2), ROWS // 2)
        return xbuf.at[z_hi * 2 + lax.rem(y + n, 2), rows, pl.ds(pl.multiple_of(x_ * 256, 256), 256)]

    def cross(n, p=0):
        rows = pl.ds(0, ROWS) if n == 0 else pl.ds(p * (ROWS // 2), ROWS // 2)
        cols = pl.ds(pl.multiple_of(lax.rem(y + n, 2) * 256, 256), 256)
        send(states.at[rows, cols], piece(zh, n, p, x), S_CR, R_CR if n == 0 else R_CB + p, partner)

    def crossed(n, p=0):
        block = piece(1 - zh, n, p, x)
        arrived(block, R_CR if n == 0 else R_CB + p)
        for step in (1, -1, 2):
            send(block, block, S_X, R_X + 2 if n == 0 else R_XB + p, at_x(step))

    def x_arrived(n):
        arrived(xbuf.at[0, :, pl.ds(0, 768)], R_X + n)

    def wblock(y_, z_, c_, start=0, rows=128):
        return wbuf.at[pl.ds(pl.multiple_of(y_ * 1024 + z_ * 256 + c_ * 128 + start, 64), rows)]

    def place(k):
        inner = (zl == 1) | (zl == 2)
        o = jnp.where(inner, 1 - k, k) if k < 2 else k
        return jnp.where(zl < 2, o, 3 - o)

    inner_z = (zl == 1) | (zl == 2)

    def y_of(step):
        return lax.rem(y + step + 4, 4)

    def column(k):
        z_ = place(k)
        block = wblock(y, z_, core)
        if k == 0:
            send(block, block, S_Z, R_Z + z_, at_z(lax.rem(zl + 1, 4)), zl < 3)
            send(block, block, S_Z, R_Z + z_, at_z(lax.rem(zl + 3, 4)), zl > 0)
        else:
            arrived(block, R_Z + z_)
            onward = jnp.where(z_ < zl, zl + 1, zl - 1)
            send(block, block, S_Z, R_Z + z_, at_z(lax.rem(onward + 4, 4)), inner_z)
        send(block, block, S_W, R_Y + k, at_y(1))
        send(block, block, S_W, R_Y + 4 + k, at_y(-1))
        send(block, block, S_W, R_SC + k, sibling)

    def neighbour(k):
        z_ = place(k)
        for d, step in ((0, -1), (1, 1)):
            block = wblock(y_of(step), z_, core)
            arrived(block, R_Y + d * 4 + k)
            part = wblock(y_of(step), z_, core, d * 64, 64)
            send(part, part, S_W, R_H + k, at_y(-step))
            send(block, block, S_W, R_SY + k, sibling)

    def halves(k):
        block = wblock(y_of(2), place(k), core)
        arrived(block, R_H + k)
        send(block, block, S_W, R_SH + k, sibling)

    outer_z = jnp.logical_not(inner_z)
    near_end = jnp.where(zl < 2, 0, 3)
    near_mid = jnp.where(zl < 2, 1, 2)

    def down_to(z_, to):
        block = dslot(z_, core)
        send(block, block, S_DZ, R_DN + z_, at_z(to))

    def down_over(z_):
        block = dslot(z_, core)
        send(block, block, S_DS, R_DS, sibling)

    def down_from(z_):
        arrived(dslot(z_, core), R_DN + z_)
        down_over(z_)

    def product(yy, k):
        ks = pl.ds(pl.multiple_of(place(k) * 256, 256), 256)
        rows = pl.ds(pl.multiple_of(yy * 1024 + place(k) * 256, 256), 256)
        for j in range(TILES):
            acc[j] += jnp.dot(xbuf[yy, :, ks], wbuf[rows, j * 256 : j * 256 + 256], preferred_element_type=F32)

    def squares_of(yy, init):
        @pl.loop(0, ROWS // 32)
        def _(r):
            rows = pl.ds(pl.multiple_of(r * 32, 32), 32)
            total = jnp.zeros((32, 128), F32) if init else scale_s[rows, :]
            for c in range(8):
                v = xbuf[yy, rows, c * 128 : c * 128 + 128].astype(F32)
                total = total + v * v
            scale_s[rows, :] = total

    def from_sibling_column(k):
        arrived(wblock(y, place(k), 1 - core), R_SC + k)

    def from_sibling_neighbours(k):
        arrived(wbuf.at[pl.ds(0, 256)], R_SY + k)

    def from_sibling_halves(k):
        arrived(wblock(y_of(2), place(k), 1 - core), R_SH + k)

    def packed(v):
        return jnp.concatenate([v[:, :128], v[:, 128:]], axis=0)

    column(0)

    lane = lax.broadcasted_iota(jnp.int32, (1, 128), 1)
    arow = jnp.full((1, 128), -1, jnp.int32)
    sub = lax.broadcasted_iota(jnp.int32, (PAD, 128), 0)
    acol = jnp.full((PAD, 128), -1, jnp.int32)
    lcol = jnp.ones((PAD, 128), jnp.int32)
    for p in range(PASSES):
        arow = jnp.where(lane == p, assign[p], arow)
        acol = jnp.where(sub == p, assign[p], acol)
        lcol = jnp.where(sub == p, lengths[p], lcol)
    abuf[lst] = arow

    @pl.loop(1, 32)
    def _(i):
        peer = lax.rem(lst + i, 32)
        send(abuf.at[lst], abuf.at[lst], S_REQ, R_REQ, dev(list_=peer))

    slot_row = lax.broadcasted_iota(jnp.int32, (PAD, ROWS), 0)
    slot_col = lax.broadcasted_iota(jnp.int32, (PAD, ROWS), 1)
    length = lcol[:, :1]
    in_pass = (slot_col >= slot_row * SEQ) & (slot_col < slot_row * SEQ + length) & (slot_row < PASSES)
    mask_s[...] = jnp.where(in_pass, 1.0, 0.0).astype(BF)
    inv_s[...] = 1.0 / lcol.astype(F32)
    cp_s.wait()
    smean[...] = jnp.dot(mask_s[...], sbuf[...], preferred_element_type=F32) * inv_s[:, :1]
    for i in range(2):
        mine_m[i] = packed(smean[:PASSES, i * 256 : i * 256 + 256]).astype(BF)
    send(mine_m, other_m, S_MEAN, R_MEAN, partner)

    column(1)
    pl.when(inner_z)(lambda: column(2))
    neighbour(0)

    arrived(abuf.at[pl.ds(0, 31)], R_REQ)
    cp_c.wait()
    wanted = jnp.broadcast_to(abuf[...], (32, 8, 128))
    lanes3 = lax.broadcasted_iota(jnp.int32, (32, 8, 128), 2)
    odd3 = lax.rem(lax.broadcasted_iota(jnp.int32, (32, 8, 128), 1), 2) == 1
    mine = (wanted >= lst * OWN_ROWS) & (wanted < lst * OWN_ROWS + OWN_ROWS)
    first = jnp.min(jnp.where(mine, lanes3, 128), axis=2, keepdims=True)
    last = jnp.max(jnp.where(mine, lanes3, -1), axis=2, keepdims=True)
    chosen_lane = jnp.where(odd3, last, first)
    hit = mine & (lanes3 == chosen_lane)
    ids = jnp.sum(jnp.where(hit, wanted - lst * OWN_ROWS, 0), axis=2, keepdims=True)
    pick[...] = jnp.broadcast_to(ids, (32, 8, 128)).reshape(256, 128)
    cacc[...] = jnp.zeros_like(cacc)

    @pl.loop(0, 8)
    def _(kc):
        base = lax.broadcasted_iota(jnp.int32, (256, 512), 1) + kc * 512
        one = jnp.where(base == pick[:, :1], 1.0, 0.0).astype(BF)
        cacc[...] += jnp.dot(one, cbuf[pl.ds(pl.multiple_of(kc * 512, 512), 512), :], preferred_element_type=F32)

    quarter = lax.rem(lax.broadcasted_iota(jnp.int32, (256, 128), 0), 8) // 2
    out_rows = jnp.zeros((256, 128), F32)
    for q in range(4):
        out_rows = jnp.where(quarter == q, cacc[:, q * 128 : q * 128 + 128], out_rows)
    resp[...] = out_rows.reshape(32, 8, 128)
    gotc[lst] = resp[lst]

    @pl.loop(1, 32)
    def _(i):
        peer = lax.rem(lst + i, 32)
        send(resp.at[peer], gotc.at[lst], S_RSP, R_RSP, dev(list_=peer))

    cross(0)
    pl.when(inner_z)(lambda: column(3))
    neighbour(1)
    pl.when(outer_z)(lambda: column(2))
    for cp in cps_x:
        cp.wait()
    for half in range(2):
        x_arrived(half)
    acc[...] = jnp.zeros_like(acc)
    squares_of(zh * 2, True)
    squares_of(zh * 2 + 1, False)
    halves(0)
    crossed(0)
    y_a = jnp.where(y // 2 == zh, y + 1 - 2 * lax.rem(y, 2), lax.rem(y + 3 - 2 * lax.rem(y, 2), 4))
    y_b = lax.rem(y_a + 2, 4)
    for k in range(2):
        from_sibling_neighbours(k)
        product(y_a, k)
    cp_d.wait()
    down_to(zl, jnp.where(inner_z, 3 - zl, near_mid))
    down_over(zl)
    cross(1, 0)
    neighbour(2)
    pl.when(outer_z)(lambda: column(3))
    cross(1, 1)
    @pl.when(inner_z)
    def _():
        down_from(near_end)
        down_to(near_end, 3 - zl)
        down_to(zl, near_end)

    crossed(1, 0)
    halves(1)
    from_sibling_neighbours(2)
    product(y_a, 2)
    x_arrived(2)
    for k in range(4):
        from_sibling_column(k)
        product(y, k)
    crossed(1, 1)
    @pl.when(inner_z)
    def _():
        down_from(3 - zl)
        down_to(3 - zl, near_end)

    squares_of((1 - zh) * 2 + lax.rem(y, 2), False)
    halves(2)
    for k in range(2):
        from_sibling_halves(k)
        product(y_of(2), k)
    neighbour(3)
    @pl.when(inner_z)
    def _():
        down_from(3 - near_end)
        down_to(3 - near_end, near_end)

    from_sibling_halves(2)
    product(y_of(2), 2)
    from_sibling_neighbours(3)
    product(y_a, 3)
    for p in range(2):
        arrived(xbuf.at[0, pl.ds(0, ROWS // 2), pl.ds(0, 768)], R_XB + p)
    squares_of((1 - zh) * 2 + lax.rem(y + 1, 2), False)
    product(y_b, 0)
    product(y_b, 1)
    halves(3)
    product(y_b, 2)
    product(y_b, 3)
    scale_s[...] = jnp.broadcast_to(
        lax.rsqrt(jnp.sum(scale_s[...], axis=1, keepdims=True) / WIDTH + 1e-05), (ROWS, 128)
    )
    from_sibling_halves(3)
    around = (2, 1, -1)

    yy = y_of(2)
    ks = pl.ds(pl.multiple_of(place(3) * 256, 256), 256)
    wrows = pl.ds(pl.multiple_of(yy * 1024 + place(3) * 256, 256), 256)
    for first, last_, buf, kind, recv in ((0, 4, hb, S_G, R_G), (4, TILES, hb2, S_G2, R_G2)):
        for j in range(first, last_):
            r = acc[j] + jnp.dot(xbuf[yy, :, ks], wbuf[wrows, j * 256 : j * 256 + 256], preferred_element_type=F32)
            g = r[:, :128] * scale_s[...]
            u = r[:, 128:] * scale_s[...]
            hid[:, j * 128 : j * 128 + 128] = (g * (0.5 + 0.5 * jnp.tanh(0.5 * g)) * u).astype(BF)
        p = jnp.dot(mask_s[...], hid[:, first * 128 : last_ * 128], preferred_element_type=F32)
        rows_p = [p[:PASSES, i * 128 : i * 128 + 128] * inv_s[:PASSES] for i in range(last_ - first)]
        if first:
            rows_p.append(jnp.zeros((8, 128), F32))
        buf[y] = jnp.concatenate(rows_p, axis=0).astype(BF)
        for n, step in enumerate(around):
            send(buf.at[y], buf.at[y], kind, recv + n, at_y(step))
    @pl.when(outer_z)
    def _():
        down_from(near_mid)
        down_from(3 - near_mid)
        down_from(3 - zl)

    arrived(dbuf.at[:, pl.ds(0, 512)], R_DS)
    cp_o.wait()

    arrived(gotc.at[pl.ds(0, 31)], R_RSP)
    own_col = acol >> 12
    own_row = jnp.where(lane < PASSES, arow >> 12, -1)
    before = (own_col == own_row) & (lax.broadcasted_iota(jnp.int32, (PAD, 128), 1) < sub)
    slot = jnp.max(jnp.where(before, 1, 0), axis=1, keepdims=True)
    wide = lax.broadcasted_iota(jnp.int32, (PAD, 256), 1)
    table = gotc[...].reshape(256, 128).astype(BF)
    for q in range(4):
        one = jnp.where(wide == own_col[:, :1] * 8 + q * 2 + slot, 1.0, 0.0).astype(BF)
        chosen_s[:, q * 128 : q * 128 + 128] = jnp.dot(one, table, preferred_element_type=F32)


    passes_y = ((0, 0), (1, 2), (-1, 1), (2, 0))
    for n, (step, came) in enumerate(passes_y):
        y_ = y_of(step)
        if step != 0:
            arrived(hb.at[y_], R_G + came)
            arrived(hb2.at[y_], R_G2 + came)
        a, b = hb[y_].astype(F32), hb2[y_].astype(F32)
        parts = [a[i * PASSES : i * PASSES + PASSES] for i in range(4)] + [b[i * PASSES : i * PASSES + PASSES] for i in range(3)]
        rows_in = jnp.concatenate(parts, axis=1).astype(BF)
        term = jnp.dot(rows_in, dbuf[...], preferred_element_type=F32)
        for z_ in range(4):
            v = packed(term[:, z_ * 256 : z_ * 256 + 256])
            tf[z_, y_] = v
            tb[z_, y_] = v.astype(BF)
        for x_step in (2, 1, -1):
            x_ = lax.rem(x + x_step + 4, 4)
            send(tb.at[x_, y_], r1b.at[x, y_], S_1, R_1 + n, at_x(x_step))
    for n, (step, _) in enumerate(passes_y):
        y_ = y_of(step)
        arrived(r1b.at[pl.ds(0, 3), 0], R_1 + n)
        v = tf[x, y_]
        for x_step in (1, -1, 2):
            v = v + r1b[lax.rem(x + x_step + 4, 4), y_].astype(F32)
        qs[y_] = v.astype(BF)
        for far in (1, 0):
            if step == 0 and far == 0:
                rb[zh, y] = qs[y]
            else:
                target = dev(list_=zl * 8 + y_ * 2 + core, tensor=x * 2 + lax.rem(zh + far, 2))
                send(qs.at[y_], rb.at[zh, y], S_2, R_2, target)
    arrived(other_m, R_MEAN)
    arrived(rb7.at[pl.ds(0, 7)], R_2)
    pooled = []
    squares = jnp.zeros((PASSES, 128), F32)
    for i in range(2):
        v = rb[0, zh * 2 + i].astype(F32) + rb[1, zh * 2 + i].astype(F32) + packed(smean[:PASSES, i * 256 : i * 256 + 256])
        w = rb[0, (1 - zh) * 2 + i].astype(F32) + rb[1, (1 - zh) * 2 + i].astype(F32) + other_m[i].astype(F32)
        both = v * v + w * w
        squares = squares + both[:PASSES] + both[PASSES:]
        pooled += [v[:PASSES], v[PASSES:]]
    turn = lax.broadcasted_iota(jnp.int32, (PASSES, 128), 0) == lax.broadcasted_iota(jnp.int32, (PASSES, 128), 1)
    sb[x] = jnp.sum(jnp.where(turn, jnp.sum(squares, axis=1, keepdims=True), 0.0), axis=0, keepdims=True)
    for step in (2, 1, -1):
        send(sb.at[x], sb.at[x], S_3, R_3, at_x(step))
    sent(wbuf.at[pl.ds(0, 28 * 128)], S_W)
    sent(xbuf.at[pl.ds(0, 3)], S_X)
    sent(xbuf.at[0, :, pl.ds(0, 512)], S_CR)
    sent(dbuf.at[:, pl.ds(0, 512)], S_DS)
    sent(hb.at[pl.ds(0, 3)], S_G)
    sent(hb2.at[pl.ds(0, 3)], S_G2)
    sent(tb.at[pl.ds(0, 3)], S_1)
    sent(abuf.at[pl.ds(0, 31)], S_REQ)
    sent(resp.at[pl.ds(0, 31)], S_RSP)

    @pl.when(inner_z)
    def _():
        sent(wbuf.at[pl.ds(0, 5 * 128)], S_Z)
        sent(dbuf.at[:, pl.ds(0, 5 * 128)], S_DZ)

    @pl.when(jnp.logical_not(inner_z))
    def _():
        sent(wbuf.at[pl.ds(0, 128)], S_Z)
        sent(dbuf.at[:, pl.ds(0, 128)], S_DZ)

    sent(rb7.at[pl.ds(0, 7)], S_2)
    sent(mine_m, S_MEAN)
    arrived(sb.at[pl.ds(0, 3)], R_3)
    total = sb[0]
    for x_ in range(1, 4):
        total = total + sb[x_]
    total = jnp.sum(jnp.where(turn, total, 0.0), axis=1, keepdims=True)
    norm = lax.rsqrt(total / WIDTH + 1e-05)
    for i in range(4):
        cols = slice(i * 128, i * 128 + 128)
        out[:, cols] = pooled[i] * norm * og_in[:, cols]
        out[:, i * 128 + PART : i * 128 + PART + 128] = chosen_s[:PASSES, cols]
    sent(sb.at[pl.ds(0, 3)], S_3)


def per_device(
    states, lengths, assign, norm_gain, gate_weight, up_weight, down_weight, out_gain, centroids
):
    any_ = pl.BlockSpec(memory_space=pl.ANY)
    smem = pl.BlockSpec(memory_space=pltpu.SMEM)
    both = pl.pallas_call(
        kernel,
        out_shape=pltpu.VMEM((PASSES, 2 * PART), F32),
        in_specs=[smem, smem] + [any_] * 7,
        out_specs=pl.BlockSpec(memory_space=pltpu.VMEM),
        scratch_shapes=[
            pltpu.VMEM((WIDTH, 2 * HID), BF),
            pltpu.VMEM((4, ROWS, 1024), BF),
            pltpu.VMEM((TILES, ROWS, 256), F32),
            pltpu.VMEM((OWN_ROWS, PART), BF),
            pltpu.VMEM((HID, 1024), BF),
            pltpu.VMEM((ROWS, PART), BF),
            pltpu.VMEM((128, HID), BF),
            pltpu.VMEM((128, HID), BF),
            pltpu.VMEM((32, 128), F32),
            pltpu.VMEM((1, PART), F32),
            pltpu.VMEM((ROWS, 128), F32),
            pltpu.VMEM((PAD, ROWS), BF),
            pltpu.VMEM((PAD, 128), F32),
            pltpu.VMEM((4, 4 * PASSES, 128), BF),
            pltpu.VMEM((4, 3 * PASSES + 8, 128), BF),
            pltpu.VMEM((ROWS, HID), BF),
            pltpu.VMEM((4, 4, 2 * PASSES, 128), F32),
            pltpu.VMEM((4, 4, 2 * PASSES, 128), BF),
            pltpu.VMEM((4, 4, 2 * PASSES, 128), BF),
            pltpu.VMEM((4, 2 * PASSES, 128), BF),
            pltpu.VMEM((2, 4, 2 * PASSES, 128), BF),
            pltpu.VMEM((8, 2 * PASSES, 128), BF),
            pltpu.VMEM((2, 2 * PASSES, 128), BF),
            pltpu.VMEM((2, 2 * PASSES, 128), BF),
            pltpu.VMEM((4, 1, 128), F32),
            pltpu.VMEM((32, 1, 128), jnp.int32),
            pltpu.VMEM((256, 128), jnp.int32),
            pltpu.VMEM((256, 512), F32),
            pltpu.VMEM((32, 8, 128), F32),
            pltpu.VMEM((32, 8, 128), F32),
            pltpu.VMEM((PAD, PART), F32),
            pltpu.VMEM((PAD, PART), F32),
            pltpu.VMEM((PASSES, 2 * PART), F32),
            pltpu.SemaphoreType.DMA((S_END,)),
            pltpu.SemaphoreType.DMA((R_END,)),
            pltpu.SemaphoreType.DMA((10,)),
        ],
        compiler_params=pltpu.CompilerParams(collective_id=0, has_side_effects=True, vmem_limit_bytes=56 << 20),
        name="passages",
    )(
        lengths,
        assign,
        states.reshape(ROWS, PART),
        norm_gain.reshape(32, 128),
        gate_weight,
        up_weight,
        down_weight,
        out_gain.reshape(1, PART),
        centroids,
    )
    embedding = both[:, :PART]
    return embedding, embedding - both[:, PART:]


def solution(mesh):
    return jax.shard_map(
        per_device,
        mesh=mesh,
        in_specs=(
            P("list", None, "tensor"),
            P("list"),
            P("list"),
            P(),
            P("list", "tensor"),
            P("list", "tensor"),
            P("tensor", "list"),
            P("tensor"),
            P("list", "tensor"),
        ),
        out_specs=(P("list", "tensor"), P("list", "tensor")),
        check_vma=False,
    )
```

```python
import functools

import jax
import jax.numpy as jnp
from jax import lax
from jax.experimental import pallas as pl
from jax.experimental.pallas import tpu as pltpu
from jax.sharding import PartitionSpec as P

MESH = pl.DeviceIdType.MESH
BF = jnp.bfloat16
F32 = jnp.float32

PASSES, SEQ, PART, WIDTH = 24, 16, 512, 4096
ROWS = PASSES * SEQ
HID = 896
TILES = HID // 128
PAD = 32
OWN_ROWS = 4096

R_Z = 0
R_Y = 4
R_H = 12
R_SC = 16
R_SY = 20
R_SH = 24
R_DN = 28
R_DS = 32
R_CR = 33
R_X = 35
R_G = 39
R_1 = 42
R_2 = 46
R_3 = 47
R_REQ = 48
R_RSP = 49
R_MEAN = 50
R_CB = 51
R_XB = 53
R_G2 = 55
R_END = 58
S_W, S_Z, S_X, S_CR, S_DZ, S_DS, S_G, S_1, S_2, S_3, S_REQ, S_RSP, S_MEAN, S_G2, S_END = range(15)


def kernel(
    lengths, assign, states, gain, gate, up, down, out_gain, centroids,
    out,
    wbuf, xbuf, acc, cbuf, dbuf, sbuf, g_in, u_in, gain_in, og_in,
    scale_s, mask_s, inv_s, hb, hb2, hid, tf, tb, r1b, qs, rb, rb7, mine_m, other_m, sb, abuf, pick, cacc, resp, gotc, chosen_s, smean, out_s,
    ss, rs, ls,
):
    lst = lax.axis_index("list")
    ten = lax.axis_index("tensor")
    core = lax.rem(lst, 2)
    y = lax.rem(lst // 2, 4)
    zl = lst // 8
    x = ten // 2
    zh = lax.rem(ten, 2)
    me_g = lax.rem(lst, 8)

    def dev(list_=None, tensor=None):
        return {"list": lst if list_ is None else list_, "tensor": ten if tensor is None else tensor}

    def at_z(z):
        return dev(list_=z * 8 + me_g)

    def at_y(step):
        return dev(list_=zl * 8 + lax.rem(y + step + 4, 4) * 2 + core)

    def at_x(step):
        return dev(tensor=lax.rem(x + step + 4, 4) * 2 + zh)

    sibling = dev(list_=lst + 1 - 2 * core)
    partner = dev(tensor=x * 2 + 1 - zh)

    def remote(src, dst, kind, recv, device):
        return pltpu.make_async_remote_copy(
            src_ref=src, dst_ref=dst, send_sem=ss.at[kind], recv_sem=rs.at[recv],
            device_id=device, device_id_type=MESH,
        )

    def send(src, dst, kind, recv, device, cond=None):
        cp = remote(src, dst, kind, recv, device)
        if cond is None:
            cp.start()
        else:
            pl.when(cond)(cp.start)

    def arrived(dst, recv):
        remote(dst, dst, 0, recv, sibling).wait_recv()

    def sent(src, kind):
        remote(src, src, kind, 0, sibling).wait_send()

    locals_ = []

    def local(src, dst):
        cp = pltpu.make_async_copy(src, dst, ls.at[len(locals_)])
        locals_.append(cp)
        cp.start()
        return cp

    def dslot(z_, c_):
        return dbuf.at[:, pl.ds(pl.multiple_of(z_ * 256 + c_ * 128, 128), 128)]

    def xslot(z_hi, half, x_):
        return xbuf.at[z_hi * 2 + half, :, pl.ds(pl.multiple_of(x_ * 256, 256), 256)]

    def xslot(z_hi, half, x_):
        return xbuf.at[z_hi * 2 + half, :, pl.ds(pl.multiple_of(x_ * 256, 256), 256)]

    cps_w = [local(gate, g_in), local(up, u_in), local(gain, gain_in)]
    cps_x = [local(states.at[:, pl.ds(half * 256, 256)], xslot(zh, half, x)) for half in range(2)]
    cp_d = local(down, dslot(zl, core))
    cp_s = local(states, sbuf)
    cp_c = local(centroids, cbuf)
    cp_o = local(out_gain, og_in)
    barrier = pltpu.get_barrier_semaphore()

    def greet_list(i):
        pl.semaphore_signal(barrier, inc=1, device_id=dev(list_=lax.rem(lst + i, 32)), device_id_type=MESH)

    def greet_x(i):
        pl.semaphore_signal(barrier, inc=1, device_id=dev(tensor=lax.rem(ten + 2 * i, 8)), device_id_type=MESH)

    def greet_across(i):
        there = dev(list_=zl * 8 + lax.rem(y + i, 4) * 2 + core, tensor=x * 2 + 1 - zh)
        pl.semaphore_signal(barrier, inc=1, device_id=there, device_id_type=MESH)

    greet_across(0)
    pl.loop(1, 4)(greet_x)
    pl.loop(1, 32)(greet_list)
    for cp in cps_w:
        cp.wait()
    eye = lax.broadcasted_iota(jnp.int32, (128, 128), 0) == lax.broadcasted_iota(jnp.int32, (128, 128), 1)
    gcol = jnp.sum(jnp.where(eye, gain_in[pl.ds(lst, 1), :], 0.0), axis=1, keepdims=True)
    own_rows = pl.ds(pl.multiple_of(y * 1024 + zl * 256 + core * 128, 128), 128)
    for j in range(TILES):
        wbuf[own_rows, j * 256 : j * 256 + 128] = (g_in[:, j * 128 : j * 128 + 128].astype(F32) * gcol).astype(BF)
        wbuf[own_rows, j * 256 + 128 : j * 256 + 256] = (u_in[:, j * 128 : j * 128 + 128].astype(F32) * gcol).astype(BF)

    pl.semaphore_wait(barrier, 31 + 3 + 1)
    for step in (1, -1, 2):
        for half in range(2):
            send(states.at[:, pl.ds(half * 256, 256)], xslot(zh, half, x), S_X, R_X + half, at_x(step))

    def piece(z_hi, n, p, x_):
        rows = pl.ds(0, ROWS) if n == 0 else pl.ds(p * (ROWS // 2), ROWS // 2)
        return xbuf.at[z_hi * 2 + lax.rem(y + n, 2), rows, pl.ds(pl.multiple_of(x_ * 256, 256), 256)]

    def cross(n, p=0):
        rows = pl.ds(0, ROWS) if n == 0 else pl.ds(p * (ROWS // 2), ROWS // 2)
        cols = pl.ds(pl.multiple_of(lax.rem(y + n, 2) * 256, 256), 256)
        send(states.at[rows, cols], piece(zh, n, p, x), S_CR, R_CR if n == 0 else R_CB + p, partner)

    def crossed(n, p=0):
        block = piece(1 - zh, n, p, x)
        arrived(block, R_CR if n == 0 else R_CB + p)
        for step in (1, -1, 2):
            send(block, block, S_X, R_X + 2 if n == 0 else R_XB + p, at_x(step))

    def x_arrived(n):
        arrived(xbuf.at[0, :, pl.ds(0, 768)], R_X + n)

    def wblock(y_, z_, c_, start=0, rows=128):
        return wbuf.at[pl.ds(pl.multiple_of(y_ * 1024 + z_ * 256 + c_ * 128 + start, 64), rows)]

    def place(k):
        inner = (zl == 1) | (zl == 2)
        o = jnp.where(inner, 1 - k, k) if k < 2 else k
        return jnp.where(zl < 2, o, 3 - o)

    inner_z = (zl == 1) | (zl == 2)

    def y_of(step):
        return lax.rem(y + step + 4, 4)

    def column(k):
        z_ = place(k)
        block = wblock(y, z_, core)
        if k == 0:
            send(block, block, S_Z, R_Z + z_, at_z(lax.rem(zl + 1, 4)), zl < 3)
            send(block, block, S_Z, R_Z + z_, at_z(lax.rem(zl + 3, 4)), zl > 0)
        else:
            arrived(block, R_Z + z_)
            onward = jnp.where(z_ < zl, zl + 1, zl - 1)
            send(block, block, S_Z, R_Z + z_, at_z(lax.rem(onward + 4, 4)), inner_z)
        send(block, block, S_W, R_Y + k, at_y(1))
        send(block, block, S_W, R_Y + 4 + k, at_y(-1))
        send(block, block, S_W, R_SC + k, sibling)

    def neighbour(k):
        z_ = place(k)
        for d, step in ((0, -1), (1, 1)):
            block = wblock(y_of(step), z_, core)
            arrived(block, R_Y + d * 4 + k)
            part = wblock(y_of(step), z_, core, d * 64, 64)
            send(part, part, S_W, R_H + k, at_y(-step))
            send(block, block, S_W, R_SY + k, sibling)

    def halves(k):
        block = wblock(y_of(2), place(k), core)
        arrived(block, R_H + k)
        send(block, block, S_W, R_SH + k, sibling)

    outer_z = jnp.logical_not(inner_z)
    near_end = jnp.where(zl < 2, 0, 3)
    near_mid = jnp.where(zl < 2, 1, 2)

    def down_to(z_, to):
        block = dslot(z_, core)
        send(block, block, S_DZ, R_DN + z_, at_z(to))

    def down_over(z_):
        block = dslot(z_, core)
        send(block, block, S_DS, R_DS, sibling)

    def down_from(z_):
        arrived(dslot(z_, core), R_DN + z_)
        down_over(z_)

    def product(yy, k):
        ks = pl.ds(pl.multiple_of(place(k) * 256, 256), 256)
        rows = pl.ds(pl.multiple_of(yy * 1024 + place(k) * 256, 256), 256)
        for j in range(TILES):
            acc[j] += jnp.dot(xbuf[yy, :, ks], wbuf[rows, j * 256 : j * 256 + 256], preferred_element_type=F32)

    def squares_of(yy, init):
        @pl.loop(0, ROWS // 32)
        def _(r):
            rows = pl.ds(pl.multiple_of(r * 32, 32), 32)
            total = jnp.zeros((32, 128), F32) if init else scale_s[rows, :]
            for c in range(8):
                v = xbuf[yy, rows, c * 128 : c * 128 + 128].astype(F32)
                total = total + v * v
            scale_s[rows, :] = total

    def from_sibling_column(k):
        arrived(wblock(y, place(k), 1 - core), R_SC + k)

    def from_sibling_neighbours(k):
        arrived(wbuf.at[pl.ds(0, 256)], R_SY + k)

    def from_sibling_halves(k):
        arrived(wblock(y_of(2), place(k), 1 - core), R_SH + k)

    def packed(v):
        return jnp.concatenate([v[:, :128], v[:, 128:]], axis=0)

    column(0)

    lane = lax.broadcasted_iota(jnp.int32, (1, 128), 1)
    arow = jnp.full((1, 128), -1, jnp.int32)
    sub = lax.broadcasted_iota(jnp.int32, (PAD, 128), 0)
    acol = jnp.full((PAD, 128), -1, jnp.int32)
    lcol = jnp.ones((PAD, 128), jnp.int32)
    for p in range(PASSES):
        arow = jnp.where(lane == p, assign[p], arow)
        acol = jnp.where(sub == p, assign[p], acol)
        lcol = jnp.where(sub == p, lengths[p], lcol)
    abuf[lst] = arow

    @pl.loop(1, 32)
    def _(i):
        peer = lax.rem(lst + i, 32)
        send(abuf.at[lst], abuf.at[lst], S_REQ, R_REQ, dev(list_=peer))

    slot_row = lax.broadcasted_iota(jnp.int32, (PAD, ROWS), 0)
    slot_col = lax.broadcasted_iota(jnp.int32, (PAD, ROWS), 1)
    length = lcol[:, :1]
    in_pass = (slot_col >= slot_row * SEQ) & (slot_col < slot_row * SEQ + length) & (slot_row < PASSES)
    mask_s[...] = jnp.where(in_pass, 1.0, 0.0).astype(BF)
    inv_s[...] = 1.0 / lcol.astype(F32)
    cp_s.wait()
    smean[...] = jnp.dot(mask_s[...], sbuf[...], preferred_element_type=F32) * inv_s[:, :1]
    for i in range(2):
        mine_m[i] = packed(smean[:PASSES, i * 256 : i * 256 + 256]).astype(BF)
    send(mine_m, other_m, S_MEAN, R_MEAN, partner)

    column(1)
    pl.when(inner_z)(lambda: column(2))
    neighbour(0)

    pl.when(jnp.logical_not(inner_z))(lambda: cross(0))
    arrived(abuf.at[pl.ds(0, 31)], R_REQ)
    cp_c.wait()
    wanted = jnp.broadcast_to(abuf[...], (32, 8, 128))
    lanes3 = lax.broadcasted_iota(jnp.int32, (32, 8, 128), 2)
    odd3 = lax.rem(lax.broadcasted_iota(jnp.int32, (32, 8, 128), 1), 2) == 1
    mine = (wanted >= lst * OWN_ROWS) & (wanted < lst * OWN_ROWS + OWN_ROWS)
    first = jnp.min(jnp.where(mine, lanes3, 128), axis=2, keepdims=True)
    last = jnp.max(jnp.where(mine, lanes3, -1), axis=2, keepdims=True)
    chosen_lane = jnp.where(odd3, last, first)
    hit = mine & (lanes3 == chosen_lane)
    ids = jnp.sum(jnp.where(hit, wanted - lst * OWN_ROWS, 0), axis=2, keepdims=True)
    pick[...] = jnp.broadcast_to(ids, (32, 8, 128)).reshape(256, 128)
    cacc[...] = jnp.zeros_like(cacc)

    @pl.loop(0, 8)
    def _(kc):
        base = lax.broadcasted_iota(jnp.int32, (256, 512), 1) + kc * 512
        one = jnp.where(base == pick[:, :1], 1.0, 0.0).astype(BF)
        cacc[...] += jnp.dot(one, cbuf[pl.ds(pl.multiple_of(kc * 512, 512), 512), :], preferred_element_type=F32)

    quarter = lax.rem(lax.broadcasted_iota(jnp.int32, (256, 128), 0), 8) // 2
    out_rows = jnp.zeros((256, 128), F32)
    for q in range(4):
        out_rows = jnp.where(quarter == q, cacc[:, q * 128 : q * 128 + 128], out_rows)
    resp[...] = out_rows.reshape(32, 8, 128)
    gotc[lst] = resp[lst]

    @pl.loop(1, 32)
    def _(i):
        peer = lax.rem(lst + i, 32)
        send(resp.at[peer], gotc.at[lst], S_RSP, R_RSP, dev(list_=peer))

    pl.when(inner_z)(lambda: cross(0))
    pl.when(inner_z)(lambda: column(3))
    neighbour(1)
    pl.when(outer_z)(lambda: column(2))
    for cp in cps_x:
        cp.wait()
    for half in range(2):
        x_arrived(half)
    acc[...] = jnp.zeros_like(acc)
    squares_of(zh * 2, True)
    squares_of(zh * 2 + 1, False)
    halves(0)
    crossed(0)
    y_a = jnp.where(y // 2 == zh, y + 1 - 2 * lax.rem(y, 2), lax.rem(y + 3 - 2 * lax.rem(y, 2), 4))
    y_b = lax.rem(y_a + 2, 4)
    for k in range(2):
        from_sibling_neighbours(k)
        product(y_a, k)
    cp_d.wait()
    down_to(zl, jnp.where(inner_z, 3 - zl, near_mid))
    down_over(zl)
    cross(1, 0)
    neighbour(2)
    pl.when(outer_z)(lambda: column(3))
    cross(1, 1)
    @pl.when(inner_z)
    def _():
        down_from(near_end)
        down_to(near_end, 3 - zl)
        down_to(zl, near_end)

    crossed(1, 0)
    halves(1)
    from_sibling_neighbours(2)
    product(y_a, 2)
    x_arrived(2)
    for k in range(4):
        from_sibling_column(k)
        product(y, k)
    crossed(1, 1)
    @pl.when(inner_z)
    def _():
        down_from(3 - zl)
        down_to(3 - zl, near_end)

    squares_of((1 - zh) * 2 + lax.rem(y, 2), False)
    halves(2)
    for k in range(2):
        from_sibling_halves(k)
        product(y_of(2), k)
    neighbour(3)
    @pl.when(inner_z)
    def _():
        down_from(3 - near_end)
        down_to(3 - near_end, near_end)

    from_sibling_halves(2)
    product(y_of(2), 2)
    from_sibling_neighbours(3)
    product(y_a, 3)
    for p in range(2):
        arrived(xbuf.at[0, pl.ds(0, ROWS // 2), pl.ds(0, 768)], R_XB + p)
    squares_of((1 - zh) * 2 + lax.rem(y + 1, 2), False)
    product(y_b, 0)
    product(y_b, 1)
    product(y_b, 2)
    product(y_b, 3)
    halves(3)
    scale_s[...] = jnp.broadcast_to(
        lax.rsqrt(jnp.sum(scale_s[...], axis=1, keepdims=True) / WIDTH + 1e-05), (ROWS, 128)
    )
    from_sibling_halves(3)
    around = (2, 1, -1)

    yy = y_of(2)
    ks = pl.ds(pl.multiple_of(place(3) * 256, 256), 256)
    wrows = pl.ds(pl.multiple_of(yy * 1024 + place(3) * 256, 256), 256)
    for first, last_, buf, kind, recv in ((0, 4, hb, S_G, R_G), (4, TILES, hb2, S_G2, R_G2)):
        for j in range(first, last_):
            r = acc[j] + jnp.dot(xbuf[yy, :, ks], wbuf[wrows, j * 256 : j * 256 + 256], preferred_element_type=F32)
            g = r[:, :128] * scale_s[...]
            u = r[:, 128:] * scale_s[...]
            hid[:, j * 128 : j * 128 + 128] = (g * (0.5 + 0.5 * jnp.tanh(0.5 * g)) * u).astype(BF)
        p = jnp.dot(mask_s[...], hid[:, first * 128 : last_ * 128], preferred_element_type=F32)
        rows_p = [p[:PASSES, i * 128 : i * 128 + 128] * inv_s[:PASSES] for i in range(last_ - first)]
        if first:
            rows_p.append(jnp.zeros((8, 128), F32))
        buf[y] = jnp.concatenate(rows_p, axis=0).astype(BF)
        for n, step in enumerate(around):
            send(buf.at[y], buf.at[y], kind, recv + n, at_y(step))
    @pl.when(outer_z)
    def _():
        down_from(near_mid)
        down_from(3 - near_mid)
        down_from(3 - zl)

    arrived(dbuf.at[:, pl.ds(0, 512)], R_DS)
    cp_o.wait()

    arrived(gotc.at[pl.ds(0, 31)], R_RSP)
    own_col = acol >> 12
    own_row = jnp.where(lane < PASSES, arow >> 12, -1)
    before = (own_col == own_row) & (lax.broadcasted_iota(jnp.int32, (PAD, 128), 1) < sub)
    slot = jnp.max(jnp.where(before, 1, 0), axis=1, keepdims=True)
    wide = lax.broadcasted_iota(jnp.int32, (PAD, 256), 1)
    table = gotc[...].reshape(256, 128).astype(BF)
    for q in range(4):
        one = jnp.where(wide == own_col[:, :1] * 8 + q * 2 + slot, 1.0, 0.0).astype(BF)
        chosen_s[:, q * 128 : q * 128 + 128] = jnp.dot(one, table, preferred_element_type=F32)


    steps = (0, 1, -1, 2)
    came = {1: 2, -1: 1, 2: 0}
    groups = ((0, 1), (1, 3), (3, 4))
    for n, (lo, hi) in enumerate(groups):
        rows_in = []
        for step in steps[lo:hi]:
            y_ = y_of(step)
            if step != 0:
                arrived(hb.at[y_], R_G + came[step])
                arrived(hb2.at[y_], R_G2 + came[step])
            a, b = hb[y_].astype(F32), hb2[y_].astype(F32)
            parts = [a[i * PASSES : i * PASSES + PASSES] for i in range(4)] + [b[i * PASSES : i * PASSES + PASSES] for i in range(3)]
            rows_in.append(jnp.concatenate(parts, axis=1))
        rows_in = (rows_in[0] if len(rows_in) == 1 else jnp.concatenate(rows_in, axis=0)).astype(BF)
        term = jnp.dot(rows_in, dbuf[...], preferred_element_type=F32)
        for m in range(lo, hi):
            for z_ in range(4):
                v = packed(term[(m - lo) * PASSES : (m - lo + 1) * PASSES, z_ * 256 : z_ * 256 + 256])
                tf[z_, m] = v
                tb[z_, m] = v.astype(BF)
        for x_step in (2, 1, -1):
            x_ = lax.rem(x + x_step + 4, 4)
            here = pl.ds(lo, hi - lo)
            send(tb.at[x_, here], r1b.at[x, here], S_1, R_1 + n, at_x(x_step))
    for n, (lo, hi) in enumerate(groups):
        arrived(r1b.at[pl.ds(0, 3), pl.ds(0, hi - lo)], R_1 + n)
        for m in range(lo, hi):
            y_ = y_of(steps[m])
            v = tf[x, m]
            for x_step in (1, -1, 2):
                v = v + r1b[lax.rem(x + x_step + 4, 4), m].astype(F32)
            qs[y_] = v.astype(BF)
            for far in (1, 0):
                if m == 0 and far == 0:
                    rb[zh, y] = qs[y]
                else:
                    target = dev(list_=zl * 8 + y_ * 2 + core, tensor=x * 2 + lax.rem(zh + far, 2))
                    send(qs.at[y_], rb.at[zh, y], S_2, R_2, target)
    arrived(other_m, R_MEAN)
    arrived(rb7.at[pl.ds(0, 7)], R_2)
    pooled = []
    squares = jnp.zeros((PASSES, 128), F32)
    for i in range(2):
        v = rb[0, zh * 2 + i].astype(F32) + rb[1, zh * 2 + i].astype(F32) + packed(smean[:PASSES, i * 256 : i * 256 + 256])
        w = rb[0, (1 - zh) * 2 + i].astype(F32) + rb[1, (1 - zh) * 2 + i].astype(F32) + other_m[i].astype(F32)
        both = v * v + w * w
        squares = squares + both[:PASSES] + both[PASSES:]
        pooled += [v[:PASSES], v[PASSES:]]
    turn = lax.broadcasted_iota(jnp.int32, (PASSES, 128), 0) == lax.broadcasted_iota(jnp.int32, (PASSES, 128), 1)
    sb[x] = jnp.sum(jnp.where(turn, jnp.sum(squares, axis=1, keepdims=True), 0.0), axis=0, keepdims=True)
    for step in (2, 1, -1):
        send(sb.at[x], sb.at[x], S_3, R_3, at_x(step))
    sent(wbuf.at[pl.ds(0, 28 * 128)], S_W)
    sent(xbuf.at[pl.ds(0, 3)], S_X)
    sent(xbuf.at[0, :, pl.ds(0, 512)], S_CR)
    sent(dbuf.at[:, pl.ds(0, 512)], S_DS)
    sent(hb.at[pl.ds(0, 3)], S_G)
    sent(hb2.at[pl.ds(0, 3)], S_G2)
    sent(tb.at[pl.ds(0, 3)], S_1)
    sent(abuf.at[pl.ds(0, 31)], S_REQ)
    sent(resp.at[pl.ds(0, 31)], S_RSP)

    @pl.when(inner_z)
    def _():
        sent(wbuf.at[pl.ds(0, 5 * 128)], S_Z)
        sent(dbuf.at[:, pl.ds(0, 5 * 128)], S_DZ)

    @pl.when(jnp.logical_not(inner_z))
    def _():
        sent(wbuf.at[pl.ds(0, 128)], S_Z)
        sent(dbuf.at[:, pl.ds(0, 128)], S_DZ)

    sent(rb7.at[pl.ds(0, 7)], S_2)
    sent(mine_m, S_MEAN)
    arrived(sb.at[pl.ds(0, 3)], R_3)
    total = sb[0]
    for x_ in range(1, 4):
        total = total + sb[x_]
    total = jnp.sum(jnp.where(turn, total, 0.0), axis=1, keepdims=True)
    norm = lax.rsqrt(total / WIDTH + 1e-05)
    for i in range(4):
        cols = slice(i * 128, i * 128 + 128)
        out[:, cols] = pooled[i] * norm * og_in[:, cols]
        out[:, i * 128 + PART : i * 128 + PART + 128] = chosen_s[:PASSES, cols]
    sent(sb.at[pl.ds(0, 3)], S_3)


def per_device(
    states, lengths, assign, norm_gain, gate_weight, up_weight, down_weight, out_gain, centroids
):
    any_ = pl.BlockSpec(memory_space=pl.ANY)
    smem = pl.BlockSpec(memory_space=pltpu.SMEM)
    both = pl.pallas_call(
        kernel,
        out_shape=pltpu.VMEM((PASSES, 2 * PART), F32),
        in_specs=[smem, smem] + [any_] * 7,
        out_specs=pl.BlockSpec(memory_space=pltpu.VMEM),
        scratch_shapes=[
            pltpu.VMEM((WIDTH, 2 * HID), BF),
            pltpu.VMEM((4, ROWS, 1024), BF),
            pltpu.VMEM((TILES, ROWS, 256), F32),
            pltpu.VMEM((OWN_ROWS, PART), BF),
            pltpu.VMEM((HID, 1024), BF),
            pltpu.VMEM((ROWS, PART), BF),
            pltpu.VMEM((128, HID), BF),
            pltpu.VMEM((128, HID), BF),
            pltpu.VMEM((32, 128), F32),
            pltpu.VMEM((1, PART), F32),
            pltpu.VMEM((ROWS, 128), F32),
            pltpu.VMEM((PAD, ROWS), BF),
            pltpu.VMEM((PAD, 128), F32),
            pltpu.VMEM((4, 4 * PASSES, 128), BF),
            pltpu.VMEM((4, 3 * PASSES + 8, 128), BF),
            pltpu.VMEM((ROWS, HID), BF),
            pltpu.VMEM((4, 4, 2 * PASSES, 128), F32),
            pltpu.VMEM((4, 4, 2 * PASSES, 128), BF),
            pltpu.VMEM((4, 4, 2 * PASSES, 128), BF),
            pltpu.VMEM((4, 2 * PASSES, 128), BF),
            pltpu.VMEM((2, 4, 2 * PASSES, 128), BF),
            pltpu.VMEM((8, 2 * PASSES, 128), BF),
            pltpu.VMEM((2, 2 * PASSES, 128), BF),
            pltpu.VMEM((2, 2 * PASSES, 128), BF),
            pltpu.VMEM((4, 1, 128), F32),
            pltpu.VMEM((32, 1, 128), jnp.int32),
            pltpu.VMEM((256, 128), jnp.int32),
            pltpu.VMEM((256, 512), F32),
            pltpu.VMEM((32, 8, 128), F32),
            pltpu.VMEM((32, 8, 128), F32),
            pltpu.VMEM((PAD, PART), F32),
            pltpu.VMEM((PAD, PART), F32),
            pltpu.VMEM((PASSES, 2 * PART), F32),
            pltpu.SemaphoreType.DMA((S_END,)),
            pltpu.SemaphoreType.DMA((R_END,)),
            pltpu.SemaphoreType.DMA((10,)),
        ],
        compiler_params=pltpu.CompilerParams(collective_id=0, has_side_effects=True, vmem_limit_bytes=56 << 20),
        name="passages",
    )(
        lengths,
        assign,
        states.reshape(ROWS, PART),
        norm_gain.reshape(32, 128),
        gate_weight,
        up_weight,
        down_weight,
        out_gain.reshape(1, PART),
        centroids,
    )
    embedding = both[:, :PART]
    return embedding, embedding - both[:, PART:]


def solution(mesh):
    return jax.shard_map(
        per_device,
        mesh=mesh,
        in_specs=(
            P("list", None, "tensor"),
            P("list"),
            P("list"),
            P(),
            P("list", "tensor"),
            P("list", "tensor"),
            P("tensor", "list"),
            P("tensor"),
            P("list", "tensor"),
        ),
        out_specs=(P("list", "tensor"), P("list", "tensor")),
        check_vma=False,
    )
```

```python
import functools

import jax
import jax.numpy as jnp
from jax import lax
from jax.experimental import pallas as pl
from jax.experimental.pallas import tpu as pltpu
from jax.sharding import PartitionSpec as P

MESH = pl.DeviceIdType.MESH
BF = jnp.bfloat16
F32 = jnp.float32

PASSES, SEQ, PART, WIDTH = 24, 16, 512, 4096
ROWS = PASSES * SEQ
HID = 896
TILES = HID // 128
PAD = 32
OWN_ROWS = 4096

R_Z = 0
R_Y = 4
R_H = 12
R_SC = 16
R_SY = 20
R_SH = 24
R_DN = 28
R_DS = 32
R_CR = 33
R_X = 35
R_G = 39
R_1 = 42
R_2 = 46
R_3 = 47
R_REQ = 48
R_RSP = 49
R_MEAN = 50
R_CB = 51
R_XB = 53
R_G2 = 55
R_END = 58
S_W, S_Z, S_X, S_CR, S_DZ, S_DS, S_G, S_1, S_2, S_3, S_REQ, S_RSP, S_MEAN, S_G2, S_END = range(15)


def kernel(
    lengths, assign, states, gain, gate, up, down, out_gain, centroids,
    out,
    wbuf, xbuf, acc, cbuf, dbuf, sbuf, g_in, u_in, gain_in, og_in,
    scale_s, mask_s, inv_s, hb, hb2, hid, tf, tb, r1b, qs, rb, rb7, mine_m, other_m, sb, abuf, pick, cacc, resp, gotc, chosen_s, smean, out_s,
    ss, rs, ls, word,
):
    lst = lax.axis_index("list")
    ten = lax.axis_index("tensor")
    core = lax.rem(lst, 2)
    y = lax.rem(lst // 2, 4)
    zl = lst // 8
    x = ten // 2
    zh = lax.rem(ten, 2)
    me_g = lax.rem(lst, 8)

    def dev(list_=None, tensor=None):
        return {"list": lst if list_ is None else list_, "tensor": ten if tensor is None else tensor}

    def at_z(z):
        return dev(list_=z * 8 + me_g)

    def at_y(step):
        return dev(list_=zl * 8 + lax.rem(y + step + 4, 4) * 2 + core)

    def at_x(step):
        return dev(tensor=lax.rem(x + step + 4, 4) * 2 + zh)

    sibling = dev(list_=lst + 1 - 2 * core)
    partner = dev(tensor=x * 2 + 1 - zh)

    def remote(src, dst, kind, recv, device):
        return pltpu.make_async_remote_copy(
            src_ref=src, dst_ref=dst, send_sem=ss.at[kind], recv_sem=rs.at[recv],
            device_id=device, device_id_type=MESH,
        )

    def send(src, dst, kind, recv, device, cond=None):
        cp = remote(src, dst, kind, recv, device)
        if cond is None:
            cp.start()
        else:
            pl.when(cond)(cp.start)

    def arrived(dst, recv):
        remote(dst, dst, 0, recv, sibling).wait_recv()

    def sent(src, kind):
        remote(src, src, kind, 0, sibling).wait_send()

    locals_ = []

    def local(src, dst):
        cp = pltpu.make_async_copy(src, dst, ls.at[len(locals_)])
        locals_.append(cp)
        cp.start()
        return cp

    def dslot(z_, c_):
        return dbuf.at[:, pl.ds(pl.multiple_of(z_ * 256 + c_ * 128, 128), 128)]

    def xslot(z_hi, half, x_):
        return xbuf.at[z_hi * 2 + half, :, pl.ds(pl.multiple_of(x_ * 256, 256), 256)]

    def xslot(z_hi, half, x_):
        return xbuf.at[z_hi * 2 + half, :, pl.ds(pl.multiple_of(x_ * 256, 256), 256)]

    cps_w = [local(gate, g_in), local(up, u_in), local(gain, gain_in)]
    cps_x = [local(states.at[:, pl.ds(half * 256, 256)], xslot(zh, half, x)) for half in range(2)]
    cp_d = local(down, dslot(zl, core))
    cp_s = local(states, sbuf)
    cp_c = local(centroids, cbuf)
    cp_o = local(out_gain, og_in)
    barrier = pltpu.get_barrier_semaphore()

    def ring_z(step):
        z_ = lax.rem(zh * 4 + zl + step + 8, 8)
        return dev(list_=lax.rem(z_, 4) * 8 + me_g, tensor=x * 2 + z_ // 4)

    def greet(semaphore, devices):
        for there in devices:
            pl.semaphore_signal(semaphore, inc=1, device_id=there, device_id_type=MESH)

    near = [at_x(2), at_y(2), ring_z(1), ring_z(-1), at_y(1), at_y(-1), at_x(1), at_x(-1), sibling]
    greet(barrier, near)
    for cp in cps_w:
        cp.wait()
    eye = lax.broadcasted_iota(jnp.int32, (128, 128), 0) == lax.broadcasted_iota(jnp.int32, (128, 128), 1)
    gcol = jnp.sum(jnp.where(eye, gain_in[pl.ds(lst, 1), :], 0.0), axis=1, keepdims=True)
    own_rows = pl.ds(pl.multiple_of(y * 1024 + zl * 256 + core * 128, 128), 128)
    for j in range(TILES):
        wbuf[own_rows, j * 256 : j * 256 + 128] = (g_in[:, j * 128 : j * 128 + 128].astype(F32) * gcol).astype(BF)
        wbuf[own_rows, j * 256 + 128 : j * 256 + 256] = (u_in[:, j * 128 : j * 128 + 128].astype(F32) * gcol).astype(BF)

    pl.semaphore_wait(barrier, len(near))
    for step in (1, -1, 2):
        for half in range(2):
            send(states.at[:, pl.ds(half * 256, 256)], xslot(zh, half, x), S_X, R_X + half, at_x(step))

    def piece(z_hi, n, p, x_):
        rows = pl.ds(0, ROWS) if n == 0 else pl.ds(p * (ROWS // 2), ROWS // 2)
        return xbuf.at[z_hi * 2 + lax.rem(y + n, 2), rows, pl.ds(pl.multiple_of(x_ * 256, 256), 256)]

    def cross(n, p=0):
        rows = pl.ds(0, ROWS) if n == 0 else pl.ds(p * (ROWS // 2), ROWS // 2)
        cols = pl.ds(pl.multiple_of(lax.rem(y + n, 2) * 256, 256), 256)
        send(states.at[rows, cols], piece(zh, n, p, x), S_CR, R_CR if n == 0 else R_CB + p, partner)

    def crossed(n, p=0):
        block = piece(1 - zh, n, p, x)
        arrived(block, R_CR if n == 0 else R_CB + p)
        for step in (1, -1, 2):
            send(block, block, S_X, R_X + 2 if n == 0 else R_XB + p, at_x(step))

    def x_arrived(n):
        arrived(xbuf.at[0, :, pl.ds(0, 768)], R_X + n)

    def wblock(y_, z_, c_, start=0, rows=128):
        return wbuf.at[pl.ds(pl.multiple_of(y_ * 1024 + z_ * 256 + c_ * 128 + start, 64), rows)]

    def place(k):
        inner = (zl == 1) | (zl == 2)
        o = jnp.where(inner, 1 - k, k) if k < 2 else k
        return jnp.where(zl < 2, o, 3 - o)

    inner_z = (zl == 1) | (zl == 2)

    def y_of(step):
        return lax.rem(y + step + 4, 4)

    def column(k):
        z_ = place(k)
        block = wblock(y, z_, core)
        if k == 0:
            send(block, block, S_Z, R_Z + z_, at_z(lax.rem(zl + 1, 4)), zl < 3)
            send(block, block, S_Z, R_Z + z_, at_z(lax.rem(zl + 3, 4)), zl > 0)
        else:
            arrived(block, R_Z + z_)
            onward = jnp.where(z_ < zl, zl + 1, zl - 1)
            send(block, block, S_Z, R_Z + z_, at_z(lax.rem(onward + 4, 4)), inner_z)
        send(block, block, S_W, R_Y + k, at_y(1))
        send(block, block, S_W, R_Y + 4 + k, at_y(-1))
        send(block, block, S_W, R_SC + k, sibling)

    def neighbour(k):
        z_ = place(k)
        for d, step in ((0, -1), (1, 1)):
            block = wblock(y_of(step), z_, core)
            arrived(block, R_Y + d * 4 + k)
            part = wblock(y_of(step), z_, core, d * 64, 64)
            send(part, part, S_W, R_H + k, at_y(-step))
            send(block, block, S_W, R_SY + k, sibling)

    def halves(k):
        block = wblock(y_of(2), place(k), core)
        arrived(block, R_H + k)
        send(block, block, S_W, R_SH + k, sibling)

    outer_z = jnp.logical_not(inner_z)
    near_end = jnp.where(zl < 2, 0, 3)
    near_mid = jnp.where(zl < 2, 1, 2)

    def down_to(z_, to):
        block = dslot(z_, core)
        send(block, block, S_DZ, R_DN + z_, at_z(to))

    def down_over(z_):
        block = dslot(z_, core)
        send(block, block, S_DS, R_DS, sibling)

    def down_from(z_):
        arrived(dslot(z_, core), R_DN + z_)
        down_over(z_)

    def product(yy, k):
        ks = pl.ds(pl.multiple_of(place(k) * 256, 256), 256)
        rows = pl.ds(pl.multiple_of(yy * 1024 + place(k) * 256, 256), 256)
        for j in range(TILES):
            acc[j] += jnp.dot(xbuf[yy, :, ks], wbuf[rows, j * 256 : j * 256 + 256], preferred_element_type=F32)

    def squares_of(yy, init):
        @pl.loop(0, ROWS // 32)
        def _(r):
            rows = pl.ds(pl.multiple_of(r * 32, 32), 32)
            total = jnp.zeros((32, 128), F32) if init else scale_s[rows, :]
            for c in range(8):
                v = xbuf[yy, rows, c * 128 : c * 128 + 128].astype(F32)
                total = total + v * v
            scale_s[rows, :] = total

    def from_sibling_column(k):
        arrived(wblock(y, place(k), 1 - core), R_SC + k)

    def from_sibling_neighbours(k):
        arrived(wbuf.at[pl.ds(0, 256)], R_SY + k)

    def from_sibling_halves(k):
        arrived(wblock(y_of(2), place(k), 1 - core), R_SH + k)

    def packed(v):
        return jnp.concatenate([v[:, :128], v[:, 128:]], axis=0)

    column(0)

    lane = lax.broadcasted_iota(jnp.int32, (1, 128), 1)
    arow = jnp.full((1, 128), -1, jnp.int32)
    sub = lax.broadcasted_iota(jnp.int32, (PAD, 128), 0)
    acol = jnp.full((PAD, 128), -1, jnp.int32)
    lcol = jnp.ones((PAD, 128), jnp.int32)
    for p in range(PASSES):
        arow = jnp.where(lane == p, assign[p], arow)
        acol = jnp.where(sub == p, assign[p], acol)
        lcol = jnp.where(sub == p, lengths[p], lcol)
    abuf[lst] = arow

    greet(word.at[0], [sibling])
    pl.semaphore_wait(word.at[0], 1)
    for r in range(1, 5):
        greet(word.at[r], [ring_z(1), ring_z(-1)])
        pl.semaphore_wait(word.at[r], 2)

    @pl.loop(1, 32)
    def _(i):
        peer = lax.rem(lst + i, 32)
        send(abuf.at[lst], abuf.at[lst], S_REQ, R_REQ, dev(list_=peer))

    slot_row = lax.broadcasted_iota(jnp.int32, (PAD, ROWS), 0)
    slot_col = lax.broadcasted_iota(jnp.int32, (PAD, ROWS), 1)
    length = lcol[:, :1]
    in_pass = (slot_col >= slot_row * SEQ) & (slot_col < slot_row * SEQ + length) & (slot_row < PASSES)
    mask_s[...] = jnp.where(in_pass, 1.0, 0.0).astype(BF)
    inv_s[...] = 1.0 / lcol.astype(F32)
    cp_s.wait()
    smean[...] = jnp.dot(mask_s[...], sbuf[...], preferred_element_type=F32) * inv_s[:, :1]
    for i in range(2):
        mine_m[i] = packed(smean[:PASSES, i * 256 : i * 256 + 256]).astype(BF)
    send(mine_m, other_m, S_MEAN, R_MEAN, partner)

    column(1)
    pl.when(inner_z)(lambda: column(2))
    neighbour(0)

    pl.when(jnp.logical_not(inner_z))(lambda: cross(0))
    arrived(abuf.at[pl.ds(0, 31)], R_REQ)
    cp_c.wait()
    wanted = jnp.broadcast_to(abuf[...], (32, 8, 128))
    lanes3 = lax.broadcasted_iota(jnp.int32, (32, 8, 128), 2)
    odd3 = lax.rem(lax.broadcasted_iota(jnp.int32, (32, 8, 128), 1), 2) == 1
    mine = (wanted >= lst * OWN_ROWS) & (wanted < lst * OWN_ROWS + OWN_ROWS)
    first = jnp.min(jnp.where(mine, lanes3, 128), axis=2, keepdims=True)
    last = jnp.max(jnp.where(mine, lanes3, -1), axis=2, keepdims=True)
    chosen_lane = jnp.where(odd3, last, first)
    hit = mine & (lanes3 == chosen_lane)
    ids = jnp.sum(jnp.where(hit, wanted - lst * OWN_ROWS, 0), axis=2, keepdims=True)
    pick[...] = jnp.broadcast_to(ids, (32, 8, 128)).reshape(256, 128)
    cacc[...] = jnp.zeros_like(cacc)

    @pl.loop(0, 8)
    def _(kc):
        base = lax.broadcasted_iota(jnp.int32, (256, 512), 1) + kc * 512
        one = jnp.where(base == pick[:, :1], 1.0, 0.0).astype(BF)
        cacc[...] += jnp.dot(one, cbuf[pl.ds(pl.multiple_of(kc * 512, 512), 512), :], preferred_element_type=F32)

    quarter = lax.rem(lax.broadcasted_iota(jnp.int32, (256, 128), 0), 8) // 2
    out_rows = jnp.zeros((256, 128), F32)
    for q in range(4):
        out_rows = jnp.where(quarter == q, cacc[:, q * 128 : q * 128 + 128], out_rows)
    resp[...] = out_rows.reshape(32, 8, 128)
    gotc[lst] = resp[lst]

    @pl.loop(1, 32)
    def _(i):
        peer = lax.rem(lst + i, 32)
        send(resp.at[peer], gotc.at[lst], S_RSP, R_RSP, dev(list_=peer))

    pl.when(inner_z)(lambda: cross(0))
    pl.when(inner_z)(lambda: column(3))
    neighbour(1)
    pl.when(outer_z)(lambda: column(2))
    for cp in cps_x:
        cp.wait()
    for half in range(2):
        x_arrived(half)
    acc[...] = jnp.zeros_like(acc)
    squares_of(zh * 2, True)
    squares_of(zh * 2 + 1, False)
    halves(0)
    crossed(0)
    y_a = jnp.where(y // 2 == zh, y + 1 - 2 * lax.rem(y, 2), lax.rem(y + 3 - 2 * lax.rem(y, 2), 4))
    y_b = lax.rem(y_a + 2, 4)
    for k in range(2):
        from_sibling_neighbours(k)
        product(y_a, k)
    cp_d.wait()
    down_to(zl, jnp.where(inner_z, 3 - zl, near_mid))
    down_over(zl)
    cross(1, 0)
    neighbour(2)
    pl.when(outer_z)(lambda: column(3))
    cross(1, 1)
    @pl.when(inner_z)
    def _():
        down_from(near_end)
        down_to(near_end, 3 - zl)
        down_to(zl, near_end)

    crossed(1, 0)
    halves(1)
    from_sibling_neighbours(2)
    product(y_a, 2)
    x_arrived(2)
    for k in range(4):
        from_sibling_column(k)
        product(y, k)
    crossed(1, 1)
    @pl.when(inner_z)
    def _():
        down_from(3 - zl)
        down_to(3 - zl, near_end)

    squares_of((1 - zh) * 2 + lax.rem(y, 2), False)
    halves(2)
    for k in range(2):
        from_sibling_halves(k)
        product(y_of(2), k)
    neighbour(3)
    @pl.when(inner_z)
    def _():
        down_from(3 - near_end)
        down_to(3 - near_end, near_end)

    from_sibling_halves(2)
    product(y_of(2), 2)
    from_sibling_neighbours(3)
    product(y_a, 3)
    for p in range(2):
        arrived(xbuf.at[0, pl.ds(0, ROWS // 2), pl.ds(0, 768)], R_XB + p)
    squares_of((1 - zh) * 2 + lax.rem(y + 1, 2), False)
    product(y_b, 0)
    product(y_b, 1)
    product(y_b, 2)
    product(y_b, 3)
    halves(3)
    scale_s[...] = jnp.broadcast_to(
        lax.rsqrt(jnp.sum(scale_s[...], axis=1, keepdims=True) / WIDTH + 1e-05), (ROWS, 128)
    )
    from_sibling_halves(3)
    around = (2, 1, -1)

    yy = y_of(2)
    ks = pl.ds(pl.multiple_of(place(3) * 256, 256), 256)
    wrows = pl.ds(pl.multiple_of(yy * 1024 + place(3) * 256, 256), 256)
    for first, last_, buf, kind, recv in ((0, 4, hb, S_G, R_G), (4, TILES, hb2, S_G2, R_G2)):
        for j in range(first, last_):
            r = acc[j] + jnp.dot(xbuf[yy, :, ks], wbuf[wrows, j * 256 : j * 256 + 256], preferred_element_type=F32)
            g = r[:, :128] * scale_s[...]
            u = r[:, 128:] * scale_s[...]
            hid[:, j * 128 : j * 128 + 128] = (g * (0.5 + 0.5 * jnp.tanh(0.5 * g)) * u).astype(BF)
        p = jnp.dot(mask_s[...], hid[:, first * 128 : last_ * 128], preferred_element_type=F32)
        rows_p = [p[:PASSES, i * 128 : i * 128 + 128] * inv_s[:PASSES] for i in range(last_ - first)]
        if first:
            rows_p.append(jnp.zeros((8, 128), F32))
        buf[y] = jnp.concatenate(rows_p, axis=0).astype(BF)
        for n, step in enumerate(around):
            send(buf.at[y], buf.at[y], kind, recv + n, at_y(step))
    @pl.when(outer_z)
    def _():
        down_from(near_mid)
        down_from(3 - near_mid)
        down_from(3 - zl)

    arrived(dbuf.at[:, pl.ds(0, 512)], R_DS)
    cp_o.wait()

    arrived(gotc.at[pl.ds(0, 31)], R_RSP)
    own_col = acol >> 12
    own_row = jnp.where(lane < PASSES, arow >> 12, -1)
    before = (own_col == own_row) & (lax.broadcasted_iota(jnp.int32, (PAD, 128), 1) < sub)
    slot = jnp.max(jnp.where(before, 1, 0), axis=1, keepdims=True)
    wide = lax.broadcasted_iota(jnp.int32, (PAD, 256), 1)
    table = gotc[...].reshape(256, 128).astype(BF)
    for q in range(4):
        one = jnp.where(wide == own_col[:, :1] * 8 + q * 2 + slot, 1.0, 0.0).astype(BF)
        chosen_s[:, q * 128 : q * 128 + 128] = jnp.dot(one, table, preferred_element_type=F32)


    steps = (0, 1, -1, 2)
    came = {1: 2, -1: 1, 2: 0}
    groups = ((0, 1), (1, 3), (3, 4))
    for n, (lo, hi) in enumerate(groups):
        rows_in = []
        for step in steps[lo:hi]:
            y_ = y_of(step)
            if step != 0:
                arrived(hb.at[y_], R_G + came[step])
                arrived(hb2.at[y_], R_G2 + came[step])
            a, b = hb[y_].astype(F32), hb2[y_].astype(F32)
            parts = [a[i * PASSES : i * PASSES + PASSES] for i in range(4)] + [b[i * PASSES : i * PASSES + PASSES] for i in range(3)]
            rows_in.append(jnp.concatenate(parts, axis=1))
        rows_in = (rows_in[0] if len(rows_in) == 1 else jnp.concatenate(rows_in, axis=0)).astype(BF)
        term = jnp.dot(rows_in, dbuf[...], preferred_element_type=F32)
        for m in range(lo, hi):
            for z_ in range(4):
                v = packed(term[(m - lo) * PASSES : (m - lo + 1) * PASSES, z_ * 256 : z_ * 256 + 256])
                tf[z_, m] = v
                tb[z_, m] = v.astype(BF)
        for x_step in (2, 1, -1):
            x_ = lax.rem(x + x_step + 4, 4)
            here = pl.ds(lo, hi - lo)
            send(tb.at[x_, here], r1b.at[x, here], S_1, R_1 + n, at_x(x_step))
    for n, (lo, hi) in enumerate(groups):
        arrived(r1b.at[pl.ds(0, 3), pl.ds(0, hi - lo)], R_1 + n)
        for m in range(lo, hi):
            y_ = y_of(steps[m])
            v = tf[x, m]
            for x_step in (1, -1, 2):
                v = v + r1b[lax.rem(x + x_step + 4, 4), m].astype(F32)
            qs[y_] = v.astype(BF)
            for far in (1, 0):
                if m == 0 and far == 0:
                    rb[zh, y] = qs[y]
                else:
                    target = dev(list_=zl * 8 + y_ * 2 + core, tensor=x * 2 + lax.rem(zh + far, 2))
                    send(qs.at[y_], rb.at[zh, y], S_2, R_2, target)
    arrived(other_m, R_MEAN)
    arrived(rb7.at[pl.ds(0, 7)], R_2)
    pooled = []
    squares = jnp.zeros((PASSES, 128), F32)
    for i in range(2):
        v = rb[0, zh * 2 + i].astype(F32) + rb[1, zh * 2 + i].astype(F32) + packed(smean[:PASSES, i * 256 : i * 256 + 256])
        w = rb[0, (1 - zh) * 2 + i].astype(F32) + rb[1, (1 - zh) * 2 + i].astype(F32) + other_m[i].astype(F32)
        both = v * v + w * w
        squares = squares + both[:PASSES] + both[PASSES:]
        pooled += [v[:PASSES], v[PASSES:]]
    turn = lax.broadcasted_iota(jnp.int32, (PASSES, 128), 0) == lax.broadcasted_iota(jnp.int32, (PASSES, 128), 1)
    sb[x] = jnp.sum(jnp.where(turn, jnp.sum(squares, axis=1, keepdims=True), 0.0), axis=0, keepdims=True)
    for step in (2, 1, -1):
        send(sb.at[x], sb.at[x], S_3, R_3, at_x(step))
    sent(wbuf.at[pl.ds(0, 28 * 128)], S_W)
    sent(xbuf.at[pl.ds(0, 3)], S_X)
    sent(xbuf.at[0, :, pl.ds(0, 512)], S_CR)
    sent(dbuf.at[:, pl.ds(0, 512)], S_DS)
    sent(hb.at[pl.ds(0, 3)], S_G)
    sent(hb2.at[pl.ds(0, 3)], S_G2)
    sent(tb.at[pl.ds(0, 3)], S_1)
    sent(abuf.at[pl.ds(0, 31)], S_REQ)
    sent(resp.at[pl.ds(0, 31)], S_RSP)

    @pl.when(inner_z)
    def _():
        sent(wbuf.at[pl.ds(0, 5 * 128)], S_Z)
        sent(dbuf.at[:, pl.ds(0, 5 * 128)], S_DZ)

    @pl.when(jnp.logical_not(inner_z))
    def _():
        sent(wbuf.at[pl.ds(0, 128)], S_Z)
        sent(dbuf.at[:, pl.ds(0, 128)], S_DZ)

    sent(rb7.at[pl.ds(0, 7)], S_2)
    sent(mine_m, S_MEAN)
    arrived(sb.at[pl.ds(0, 3)], R_3)
    total = sb[0]
    for x_ in range(1, 4):
        total = total + sb[x_]
    total = jnp.sum(jnp.where(turn, total, 0.0), axis=1, keepdims=True)
    norm = lax.rsqrt(total / WIDTH + 1e-05)
    for i in range(4):
        cols = slice(i * 128, i * 128 + 128)
        out[:, cols] = pooled[i] * norm * og_in[:, cols]
        out[:, i * 128 + PART : i * 128 + PART + 128] = chosen_s[:PASSES, cols]
    sent(sb.at[pl.ds(0, 3)], S_3)


def per_device(
    states, lengths, assign, norm_gain, gate_weight, up_weight, down_weight, out_gain, centroids
):
    any_ = pl.BlockSpec(memory_space=pl.ANY)
    smem = pl.BlockSpec(memory_space=pltpu.SMEM)
    both = pl.pallas_call(
        kernel,
        out_shape=pltpu.VMEM((PASSES, 2 * PART), F32),
        in_specs=[smem, smem] + [any_] * 7,
        out_specs=pl.BlockSpec(memory_space=pltpu.VMEM),
        scratch_shapes=[
            pltpu.VMEM((WIDTH, 2 * HID), BF),
            pltpu.VMEM((4, ROWS, 1024), BF),
            pltpu.VMEM((TILES, ROWS, 256), F32),
            pltpu.VMEM((OWN_ROWS, PART), BF),
            pltpu.VMEM((HID, 1024), BF),
            pltpu.VMEM((ROWS, PART), BF),
            pltpu.VMEM((128, HID), BF),
            pltpu.VMEM((128, HID), BF),
            pltpu.VMEM((32, 128), F32),
            pltpu.VMEM((1, PART), F32),
            pltpu.VMEM((ROWS, 128), F32),
            pltpu.VMEM((PAD, ROWS), BF),
            pltpu.VMEM((PAD, 128), F32),
            pltpu.VMEM((4, 4 * PASSES, 128), BF),
            pltpu.VMEM((4, 3 * PASSES + 8, 128), BF),
            pltpu.VMEM((ROWS, HID), BF),
            pltpu.VMEM((4, 4, 2 * PASSES, 128), F32),
            pltpu.VMEM((4, 4, 2 * PASSES, 128), BF),
            pltpu.VMEM((4, 4, 2 * PASSES, 128), BF),
            pltpu.VMEM((4, 2 * PASSES, 128), BF),
            pltpu.VMEM((2, 4, 2 * PASSES, 128), BF),
            pltpu.VMEM((8, 2 * PASSES, 128), BF),
            pltpu.VMEM((2, 2 * PASSES, 128), BF),
            pltpu.VMEM((2, 2 * PASSES, 128), BF),
            pltpu.VMEM((4, 1, 128), F32),
            pltpu.VMEM((32, 1, 128), jnp.int32),
            pltpu.VMEM((256, 128), jnp.int32),
            pltpu.VMEM((256, 512), F32),
            pltpu.VMEM((32, 8, 128), F32),
            pltpu.VMEM((32, 8, 128), F32),
            pltpu.VMEM((PAD, PART), F32),
            pltpu.VMEM((PAD, PART), F32),
            pltpu.VMEM((PASSES, 2 * PART), F32),
            pltpu.SemaphoreType.DMA((S_END,)),
            pltpu.SemaphoreType.DMA((R_END,)),
            pltpu.SemaphoreType.DMA((10,)),
            pltpu.SemaphoreType.REGULAR((5,)),
        ],
        compiler_params=pltpu.CompilerParams(collective_id=0, has_side_effects=True, vmem_limit_bytes=56 << 20),
        name="passages",
    )(
        lengths,
        assign,
        states.reshape(ROWS, PART),
        norm_gain.reshape(32, 128),
        gate_weight,
        up_weight,
        down_weight,
        out_gain.reshape(1, PART),
        centroids,
    )
    embedding = both[:, :PART]
    return embedding, embedding - both[:, PART:]


def solution(mesh):
    return jax.shard_map(
        per_device,
        mesh=mesh,
        in_specs=(
            P("list", None, "tensor"),
            P("list"),
            P("list"),
            P(),
            P("list", "tensor"),
            P("list", "tensor"),
            P("tensor", "list"),
            P("tensor"),
            P("list", "tensor"),
        ),
        out_specs=(P("list", "tensor"), P("list", "tensor")),
        check_vma=False,
    )
```

```python
import functools

import jax
import jax.numpy as jnp
from jax import lax
from jax.experimental import pallas as pl
from jax.experimental.pallas import tpu as pltpu
from jax.sharding import PartitionSpec as P

MESH = pl.DeviceIdType.MESH
BF = jnp.bfloat16
F32 = jnp.float32

PASSES, SEQ, PART, WIDTH = 24, 16, 512, 4096
ROWS = PASSES * SEQ
HID = 896
TILES = HID // 128
PAD = 32
OWN_ROWS = 4096

R_Z = 0
R_Y = 4
R_H = 12
R_SC = 16
R_SY = 20
R_SH = 24
R_DN = 28
R_DS = 32
R_CR = 33
R_X = 35
R_G = 39
R_1 = 42
R_2 = 46
R_3 = 47
R_REQ = 48
R_RSP = 49
R_MEAN = 50
R_CB = 51
R_XB = 53
R_G2 = 55
R_END = 58
S_W, S_Z, S_X, S_CR, S_DZ, S_DS, S_G, S_1, S_2, S_3, S_REQ, S_RSP, S_MEAN, S_G2, S_END = range(15)


def kernel(
    lengths, assign, states, gain, gate, up, down, out_gain, centroids,
    out,
    wbuf, xbuf, acc, cbuf, dbuf, sbuf, g_in, u_in, gain_in, og_in,
    scale_s, mask_s, inv_s, hb, hb2, hid, tf, tb, r1b, qs, rb, rb7, mine_m, other_m, sb, abuf, pick, cacc, resp, gotc, chosen_s, smean, out_s,
    ss, rs, ls, word,
):
    lst = lax.axis_index("list")
    ten = lax.axis_index("tensor")
    core = lax.rem(lst, 2)
    y = lax.rem(lst // 2, 4)
    zl = lst // 8
    x = ten // 2
    zh = lax.rem(ten, 2)
    me_g = lax.rem(lst, 8)

    def dev(list_=None, tensor=None):
        return {"list": lst if list_ is None else list_, "tensor": ten if tensor is None else tensor}

    def at_z(z):
        return dev(list_=z * 8 + me_g)

    def at_y(step):
        return dev(list_=zl * 8 + lax.rem(y + step + 4, 4) * 2 + core)

    def at_x(step):
        return dev(tensor=lax.rem(x + step + 4, 4) * 2 + zh)

    sibling = dev(list_=lst + 1 - 2 * core)
    partner = dev(tensor=x * 2 + 1 - zh)

    def remote(src, dst, kind, recv, device):
        return pltpu.make_async_remote_copy(
            src_ref=src, dst_ref=dst, send_sem=ss.at[kind], recv_sem=rs.at[recv],
            device_id=device, device_id_type=MESH,
        )

    def send(src, dst, kind, recv, device, cond=None):
        cp = remote(src, dst, kind, recv, device)
        if cond is None:
            cp.start()
        else:
            pl.when(cond)(cp.start)

    def arrived(dst, recv):
        remote(dst, dst, 0, recv, sibling).wait_recv()

    def sent(src, kind):
        remote(src, src, kind, 0, sibling).wait_send()

    locals_ = []

    def local(src, dst):
        cp = pltpu.make_async_copy(src, dst, ls.at[len(locals_)])
        locals_.append(cp)
        cp.start()
        return cp

    def dslot(z_, c_):
        return dbuf.at[:, pl.ds(pl.multiple_of(z_ * 256 + c_ * 128, 128), 128)]

    def xslot(z_hi, half, x_):
        return xbuf.at[z_hi * 2 + half, :, pl.ds(pl.multiple_of(x_ * 256, 256), 256)]

    def xslot(z_hi, half, x_):
        return xbuf.at[z_hi * 2 + half, :, pl.ds(pl.multiple_of(x_ * 256, 256), 256)]

    cps_w = [local(gate, g_in), local(up, u_in), local(gain, gain_in)]
    cps_x = [local(states.at[:, pl.ds(half * 256, 256)], xslot(zh, half, x)) for half in range(2)]
    cp_d = local(down, dslot(zl, core))
    cp_s = local(states, sbuf)
    cp_c = local(centroids, cbuf)
    cp_o = local(out_gain, og_in)
    barrier = pltpu.get_barrier_semaphore()

    def ring_z(step):
        z_ = lax.rem(zh * 4 + zl + step + 8, 8)
        return dev(list_=lax.rem(z_, 4) * 8 + me_g, tensor=x * 2 + z_ // 4)

    def greet(semaphore, devices):
        for there in devices:
            pl.semaphore_signal(semaphore, inc=1, device_id=there, device_id_type=MESH)

    near = [ring_z(1), ring_z(-1), at_y(1), at_y(-1), at_x(1), at_x(-1), sibling]
    greet(barrier, near)
    for cp in cps_w:
        cp.wait()
    eye = lax.broadcasted_iota(jnp.int32, (128, 128), 0) == lax.broadcasted_iota(jnp.int32, (128, 128), 1)
    gcol = jnp.sum(jnp.where(eye, gain_in[pl.ds(lst, 1), :], 0.0), axis=1, keepdims=True)
    own_rows = pl.ds(pl.multiple_of(y * 1024 + zl * 256 + core * 128, 128), 128)
    for j in range(TILES):
        wbuf[own_rows, j * 256 : j * 256 + 128] = (g_in[:, j * 128 : j * 128 + 128].astype(F32) * gcol).astype(BF)
        wbuf[own_rows, j * 256 + 128 : j * 256 + 256] = (u_in[:, j * 128 : j * 128 + 128].astype(F32) * gcol).astype(BF)

    pl.semaphore_wait(barrier, len(near))
    def x_send(step):
        for half in range(2):
            send(states.at[:, pl.ds(half * 256, 256)], xslot(zh, half, x), S_X, R_X + half, at_x(step))

    x_send(1)
    x_send(-1)

    def piece(z_hi, n, p, x_):
        rows = pl.ds(0, ROWS) if n == 0 else pl.ds(p * (ROWS // 2), ROWS // 2)
        return xbuf.at[z_hi * 2 + lax.rem(y + n, 2), rows, pl.ds(pl.multiple_of(x_ * 256, 256), 256)]

    def cross(n, p=0):
        rows = pl.ds(0, ROWS) if n == 0 else pl.ds(p * (ROWS // 2), ROWS // 2)
        cols = pl.ds(pl.multiple_of(lax.rem(y + n, 2) * 256, 256), 256)
        send(states.at[rows, cols], piece(zh, n, p, x), S_CR, R_CR if n == 0 else R_CB + p, partner)

    def crossed(n, p=0):
        block = piece(1 - zh, n, p, x)
        arrived(block, R_CR if n == 0 else R_CB + p)
        for step in (1, -1, 2):
            send(block, block, S_X, R_X + 2 if n == 0 else R_XB + p, at_x(step))

    def x_arrived(n):
        arrived(xbuf.at[0, :, pl.ds(0, 768)], R_X + n)

    def wblock(y_, z_, c_, start=0, rows=128):
        return wbuf.at[pl.ds(pl.multiple_of(y_ * 1024 + z_ * 256 + c_ * 128 + start, 64), rows)]

    def place(k):
        inner = (zl == 1) | (zl == 2)
        o = jnp.where(inner, 1 - k, k) if k < 2 else k
        return jnp.where(zl < 2, o, 3 - o)

    inner_z = (zl == 1) | (zl == 2)

    def y_of(step):
        return lax.rem(y + step + 4, 4)

    def column(k):
        z_ = place(k)
        block = wblock(y, z_, core)
        if k == 0:
            send(block, block, S_Z, R_Z + z_, at_z(lax.rem(zl + 1, 4)), zl < 3)
            send(block, block, S_Z, R_Z + z_, at_z(lax.rem(zl + 3, 4)), zl > 0)
        else:
            arrived(block, R_Z + z_)
            onward = jnp.where(z_ < zl, zl + 1, zl - 1)
            send(block, block, S_Z, R_Z + z_, at_z(lax.rem(onward + 4, 4)), inner_z)
        send(block, block, S_W, R_Y + k, at_y(1))
        send(block, block, S_W, R_Y + 4 + k, at_y(-1))
        send(block, block, S_W, R_SC + k, sibling)

    def neighbour(k):
        z_ = place(k)
        for d, step in ((0, -1), (1, 1)):
            block = wblock(y_of(step), z_, core)
            arrived(block, R_Y + d * 4 + k)
            part = wblock(y_of(step), z_, core, d * 64, 64)
            send(part, part, S_W, R_H + k, at_y(-step))
            send(block, block, S_W, R_SY + k, sibling)

    def halves(k):
        block = wblock(y_of(2), place(k), core)
        arrived(block, R_H + k)
        send(block, block, S_W, R_SH + k, sibling)

    outer_z = jnp.logical_not(inner_z)
    near_end = jnp.where(zl < 2, 0, 3)
    near_mid = jnp.where(zl < 2, 1, 2)

    def down_to(z_, to):
        block = dslot(z_, core)
        send(block, block, S_DZ, R_DN + z_, at_z(to))

    def down_over(z_):
        block = dslot(z_, core)
        send(block, block, S_DS, R_DS, sibling)

    def down_from(z_):
        arrived(dslot(z_, core), R_DN + z_)
        down_over(z_)

    def product(yy, k):
        ks = pl.ds(pl.multiple_of(place(k) * 256, 256), 256)
        rows = pl.ds(pl.multiple_of(yy * 1024 + place(k) * 256, 256), 256)
        for j in range(TILES):
            acc[j] += jnp.dot(xbuf[yy, :, ks], wbuf[rows, j * 256 : j * 256 + 256], preferred_element_type=F32)

    def squares_of(yy, init):
        @pl.loop(0, ROWS // 32)
        def _(r):
            rows = pl.ds(pl.multiple_of(r * 32, 32), 32)
            total = jnp.zeros((32, 128), F32) if init else scale_s[rows, :]
            for c in range(8):
                v = xbuf[yy, rows, c * 128 : c * 128 + 128].astype(F32)
                total = total + v * v
            scale_s[rows, :] = total

    def from_sibling_column(k):
        arrived(wblock(y, place(k), 1 - core), R_SC + k)

    def from_sibling_neighbours(k):
        arrived(wbuf.at[pl.ds(0, 256)], R_SY + k)

    def from_sibling_halves(k):
        arrived(wblock(y_of(2), place(k), 1 - core), R_SH + k)

    def packed(v):
        return jnp.concatenate([v[:, :128], v[:, 128:]], axis=0)

    column(0)

    lane = lax.broadcasted_iota(jnp.int32, (1, 128), 1)
    arow = jnp.full((1, 128), -1, jnp.int32)
    sub = lax.broadcasted_iota(jnp.int32, (PAD, 128), 0)
    acol = jnp.full((PAD, 128), -1, jnp.int32)
    lcol = jnp.ones((PAD, 128), jnp.int32)
    for p in range(PASSES):
        arow = jnp.where(lane == p, assign[p], arow)
        acol = jnp.where(sub == p, assign[p], acol)
        lcol = jnp.where(sub == p, lengths[p], lcol)
    abuf[lst] = arow

    for r in range(5):
        greet(word.at[r], near)
        pl.semaphore_wait(word.at[r], len(near))
        if r == 0:
            x_send(2)

    @pl.loop(1, 32)
    def _(i):
        peer = lax.rem(lst + i, 32)
        send(abuf.at[lst], abuf.at[lst], S_REQ, R_REQ, dev(list_=peer))

    slot_row = lax.broadcasted_iota(jnp.int32, (PAD, ROWS), 0)
    slot_col = lax.broadcasted_iota(jnp.int32, (PAD, ROWS), 1)
    length = lcol[:, :1]
    in_pass = (slot_col >= slot_row * SEQ) & (slot_col < slot_row * SEQ + length) & (slot_row < PASSES)
    mask_s[...] = jnp.where(in_pass, 1.0, 0.0).astype(BF)
    inv_s[...] = 1.0 / lcol.astype(F32)
    cp_s.wait()
    smean[...] = jnp.dot(mask_s[...], sbuf[...], preferred_element_type=F32) * inv_s[:, :1]
    for i in range(2):
        mine_m[i] = packed(smean[:PASSES, i * 256 : i * 256 + 256]).astype(BF)
    send(mine_m, other_m, S_MEAN, R_MEAN, partner)

    column(1)
    pl.when(inner_z)(lambda: column(2))
    neighbour(0)

    pl.when(jnp.logical_not(inner_z))(lambda: cross(0))
    arrived(abuf.at[pl.ds(0, 31)], R_REQ)
    cp_c.wait()
    wanted = jnp.broadcast_to(abuf[...], (32, 8, 128))
    lanes3 = lax.broadcasted_iota(jnp.int32, (32, 8, 128), 2)
    odd3 = lax.rem(lax.broadcasted_iota(jnp.int32, (32, 8, 128), 1), 2) == 1
    mine = (wanted >= lst * OWN_ROWS) & (wanted < lst * OWN_ROWS + OWN_ROWS)
    first = jnp.min(jnp.where(mine, lanes3, 128), axis=2, keepdims=True)
    last = jnp.max(jnp.where(mine, lanes3, -1), axis=2, keepdims=True)
    chosen_lane = jnp.where(odd3, last, first)
    hit = mine & (lanes3 == chosen_lane)
    ids = jnp.sum(jnp.where(hit, wanted - lst * OWN_ROWS, 0), axis=2, keepdims=True)
    pick[...] = jnp.broadcast_to(ids, (32, 8, 128)).reshape(256, 128)
    cacc[...] = jnp.zeros_like(cacc)

    @pl.loop(0, 8)
    def _(kc):
        base = lax.broadcasted_iota(jnp.int32, (256, 512), 1) + kc * 512
        one = jnp.where(base == pick[:, :1], 1.0, 0.0).astype(BF)
        cacc[...] += jnp.dot(one, cbuf[pl.ds(pl.multiple_of(kc * 512, 512), 512), :], preferred_element_type=F32)

    quarter = lax.rem(lax.broadcasted_iota(jnp.int32, (256, 128), 0), 8) // 2
    out_rows = jnp.zeros((256, 128), F32)
    for q in range(4):
        out_rows = jnp.where(quarter == q, cacc[:, q * 128 : q * 128 + 128], out_rows)
    resp[...] = out_rows.reshape(32, 8, 128)
    gotc[lst] = resp[lst]

    @pl.loop(1, 32)
    def _(i):
        peer = lax.rem(lst + i, 32)
        send(resp.at[peer], gotc.at[lst], S_RSP, R_RSP, dev(list_=peer))

    pl.when(inner_z)(lambda: cross(0))
    pl.when(inner_z)(lambda: column(3))
    neighbour(1)
    pl.when(outer_z)(lambda: column(2))
    for cp in cps_x:
        cp.wait()
    for half in range(2):
        x_arrived(half)
    acc[...] = jnp.zeros_like(acc)
    squares_of(zh * 2, True)
    squares_of(zh * 2 + 1, False)
    halves(0)
    crossed(0)
    y_a = jnp.where(y // 2 == zh, y + 1 - 2 * lax.rem(y, 2), lax.rem(y + 3 - 2 * lax.rem(y, 2), 4))
    y_b = lax.rem(y_a + 2, 4)
    for k in range(2):
        from_sibling_neighbours(k)
        product(y_a, k)
    cp_d.wait()
    down_to(zl, jnp.where(inner_z, 3 - zl, near_mid))
    down_over(zl)
    cross(1, 0)
    neighbour(2)
    pl.when(outer_z)(lambda: column(3))
    cross(1, 1)
    @pl.when(inner_z)
    def _():
        down_from(near_end)
        down_to(near_end, 3 - zl)
        down_to(zl, near_end)

    crossed(1, 0)
    x_arrived(2)
    for k in range(4):
        from_sibling_column(k)
        product(y, k)
    crossed(1, 1)
    @pl.when(inner_z)
    def _():
        down_from(3 - zl)
        down_to(3 - zl, near_end)

    halves(1)
    from_sibling_neighbours(2)
    product(y_a, 2)
    squares_of((1 - zh) * 2 + lax.rem(y, 2), False)
    halves(2)
    for k in range(2):
        from_sibling_halves(k)
        product(y_of(2), k)
    neighbour(3)
    @pl.when(inner_z)
    def _():
        down_from(3 - near_end)
        down_to(3 - near_end, near_end)

    from_sibling_halves(2)
    product(y_of(2), 2)
    from_sibling_neighbours(3)
    product(y_a, 3)
    for p in range(2):
        arrived(xbuf.at[0, pl.ds(0, ROWS // 2), pl.ds(0, 768)], R_XB + p)
    squares_of((1 - zh) * 2 + lax.rem(y + 1, 2), False)
    product(y_b, 0)
    product(y_b, 1)
    product(y_b, 2)
    product(y_b, 3)
    halves(3)
    scale_s[...] = jnp.broadcast_to(
        lax.rsqrt(jnp.sum(scale_s[...], axis=1, keepdims=True) / WIDTH + 1e-05), (ROWS, 128)
    )
    from_sibling_halves(3)
    around = (2, 1, -1)

    yy = y_of(2)
    ks = pl.ds(pl.multiple_of(place(3) * 256, 256), 256)
    wrows = pl.ds(pl.multiple_of(yy * 1024 + place(3) * 256, 256), 256)
    for first, last_, buf, kind, recv in ((0, 4, hb, S_G, R_G), (4, TILES, hb2, S_G2, R_G2)):
        for j in range(first, last_):
            r = acc[j] + jnp.dot(xbuf[yy, :, ks], wbuf[wrows, j * 256 : j * 256 + 256], preferred_element_type=F32)
            g = r[:, :128] * scale_s[...]
            u = r[:, 128:] * scale_s[...]
            hid[:, j * 128 : j * 128 + 128] = (g * (0.5 + 0.5 * jnp.tanh(0.5 * g)) * u).astype(BF)
        p = jnp.dot(mask_s[...], hid[:, first * 128 : last_ * 128], preferred_element_type=F32)
        rows_p = [p[:PASSES, i * 128 : i * 128 + 128] * inv_s[:PASSES] for i in range(last_ - first)]
        if first:
            rows_p.append(jnp.zeros((8, 128), F32))
        buf[y] = jnp.concatenate(rows_p, axis=0).astype(BF)
        for n, step in enumerate(around):
            send(buf.at[y], buf.at[y], kind, recv + n, at_y(step))
    @pl.when(outer_z)
    def _():
        down_from(near_mid)
        down_from(3 - near_mid)
        down_from(3 - zl)

    arrived(dbuf.at[:, pl.ds(0, 512)], R_DS)
    cp_o.wait()

    arrived(gotc.at[pl.ds(0, 31)], R_RSP)
    own_col = acol >> 12
    own_row = jnp.where(lane < PASSES, arow >> 12, -1)
    before = (own_col == own_row) & (lax.broadcasted_iota(jnp.int32, (PAD, 128), 1) < sub)
    slot = jnp.max(jnp.where(before, 1, 0), axis=1, keepdims=True)
    wide = lax.broadcasted_iota(jnp.int32, (PAD, 256), 1)
    table = gotc[...].reshape(256, 128).astype(BF)
    for q in range(4):
        one = jnp.where(wide == own_col[:, :1] * 8 + q * 2 + slot, 1.0, 0.0).astype(BF)
        chosen_s[:, q * 128 : q * 128 + 128] = jnp.dot(one, table, preferred_element_type=F32)


    steps = (0, 1, -1, 2)
    came = {1: 2, -1: 1, 2: 0}
    groups = ((0, 1), (1, 3), (3, 4))
    for n, (lo, hi) in enumerate(groups):
        rows_in = []
        for step in steps[lo:hi]:
            y_ = y_of(step)
            if step != 0:
                arrived(hb.at[y_], R_G + came[step])
                arrived(hb2.at[y_], R_G2 + came[step])
            a, b = hb[y_].astype(F32), hb2[y_].astype(F32)
            parts = [a[i * PASSES : i * PASSES + PASSES] for i in range(4)] + [b[i * PASSES : i * PASSES + PASSES] for i in range(3)]
            rows_in.append(jnp.concatenate(parts, axis=1))
        rows_in = (rows_in[0] if len(rows_in) == 1 else jnp.concatenate(rows_in, axis=0)).astype(BF)
        term = jnp.dot(rows_in, dbuf[...], preferred_element_type=F32)
        for m in range(lo, hi):
            for z_ in range(4):
                v = packed(term[(m - lo) * PASSES : (m - lo + 1) * PASSES, z_ * 256 : z_ * 256 + 256])
                tf[z_, m] = v
                tb[z_, m] = v.astype(BF)
        for x_step in (2, 1, -1):
            x_ = lax.rem(x + x_step + 4, 4)
            here = pl.ds(lo, hi - lo)
            send(tb.at[x_, here], r1b.at[x, here], S_1, R_1 + n, at_x(x_step))
    for n, (lo, hi) in enumerate(groups):
        arrived(r1b.at[pl.ds(0, 3), pl.ds(0, hi - lo)], R_1 + n)
        for m in range(lo, hi):
            y_ = y_of(steps[m])
            v = tf[x, m]
            for x_step in (1, -1, 2):
                v = v + r1b[lax.rem(x + x_step + 4, 4), m].astype(F32)
            qs[y_] = v.astype(BF)
            for far in (1, 0):
                if m == 0 and far == 0:
                    rb[zh, y] = qs[y]
                else:
                    target = dev(list_=zl * 8 + y_ * 2 + core, tensor=x * 2 + lax.rem(zh + far, 2))
                    send(qs.at[y_], rb.at[zh, y], S_2, R_2, target)
    arrived(other_m, R_MEAN)
    arrived(rb7.at[pl.ds(0, 7)], R_2)
    pooled = []
    squares = jnp.zeros((PASSES, 128), F32)
    for i in range(2):
        v = rb[0, zh * 2 + i].astype(F32) + rb[1, zh * 2 + i].astype(F32) + packed(smean[:PASSES, i * 256 : i * 256 + 256])
        w = rb[0, (1 - zh) * 2 + i].astype(F32) + rb[1, (1 - zh) * 2 + i].astype(F32) + other_m[i].astype(F32)
        both = v * v + w * w
        squares = squares + both[:PASSES] + both[PASSES:]
        pooled += [v[:PASSES], v[PASSES:]]
    turn = lax.broadcasted_iota(jnp.int32, (PASSES, 128), 0) == lax.broadcasted_iota(jnp.int32, (PASSES, 128), 1)
    sb[x] = jnp.sum(jnp.where(turn, jnp.sum(squares, axis=1, keepdims=True), 0.0), axis=0, keepdims=True)
    for step in (2, 1, -1):
        send(sb.at[x], sb.at[x], S_3, R_3, at_x(step))
    sent(wbuf.at[pl.ds(0, 28 * 128)], S_W)
    sent(xbuf.at[pl.ds(0, 3)], S_X)
    sent(xbuf.at[0, :, pl.ds(0, 512)], S_CR)
    sent(dbuf.at[:, pl.ds(0, 512)], S_DS)
    sent(hb.at[pl.ds(0, 3)], S_G)
    sent(hb2.at[pl.ds(0, 3)], S_G2)
    sent(tb.at[pl.ds(0, 3)], S_1)
    sent(abuf.at[pl.ds(0, 31)], S_REQ)
    sent(resp.at[pl.ds(0, 31)], S_RSP)

    @pl.when(inner_z)
    def _():
        sent(wbuf.at[pl.ds(0, 5 * 128)], S_Z)
        sent(dbuf.at[:, pl.ds(0, 5 * 128)], S_DZ)

    @pl.when(jnp.logical_not(inner_z))
    def _():
        sent(wbuf.at[pl.ds(0, 128)], S_Z)
        sent(dbuf.at[:, pl.ds(0, 128)], S_DZ)

    sent(rb7.at[pl.ds(0, 7)], S_2)
    sent(mine_m, S_MEAN)
    arrived(sb.at[pl.ds(0, 3)], R_3)
    total = sb[0]
    for x_ in range(1, 4):
        total = total + sb[x_]
    total = jnp.sum(jnp.where(turn, total, 0.0), axis=1, keepdims=True)
    norm = lax.rsqrt(total / WIDTH + 1e-05)
    for i in range(4):
        cols = slice(i * 128, i * 128 + 128)
        out[:, cols] = pooled[i] * norm * og_in[:, cols]
        out[:, i * 128 + PART : i * 128 + PART + 128] = chosen_s[:PASSES, cols]
    sent(sb.at[pl.ds(0, 3)], S_3)


def per_device(
    states, lengths, assign, norm_gain, gate_weight, up_weight, down_weight, out_gain, centroids
):
    any_ = pl.BlockSpec(memory_space=pl.ANY)
    smem = pl.BlockSpec(memory_space=pltpu.SMEM)
    both = pl.pallas_call(
        kernel,
        out_shape=pltpu.VMEM((PASSES, 2 * PART), F32),
        in_specs=[smem, smem] + [any_] * 7,
        out_specs=pl.BlockSpec(memory_space=pltpu.VMEM),
        scratch_shapes=[
            pltpu.VMEM((WIDTH, 2 * HID), BF),
            pltpu.VMEM((4, ROWS, 1024), BF),
            pltpu.VMEM((TILES, ROWS, 256), F32),
            pltpu.VMEM((OWN_ROWS, PART), BF),
            pltpu.VMEM((HID, 1024), BF),
            pltpu.VMEM((ROWS, PART), BF),
            pltpu.VMEM((128, HID), BF),
            pltpu.VMEM((128, HID), BF),
            pltpu.VMEM((32, 128), F32),
            pltpu.VMEM((1, PART), F32),
            pltpu.VMEM((ROWS, 128), F32),
            pltpu.VMEM((PAD, ROWS), BF),
            pltpu.VMEM((PAD, 128), F32),
            pltpu.VMEM((4, 4 * PASSES, 128), BF),
            pltpu.VMEM((4, 3 * PASSES + 8, 128), BF),
            pltpu.VMEM((ROWS, HID), BF),
            pltpu.VMEM((4, 4, 2 * PASSES, 128), F32),
            pltpu.VMEM((4, 4, 2 * PASSES, 128), BF),
            pltpu.VMEM((4, 4, 2 * PASSES, 128), BF),
            pltpu.VMEM((4, 2 * PASSES, 128), BF),
            pltpu.VMEM((2, 4, 2 * PASSES, 128), BF),
            pltpu.VMEM((8, 2 * PASSES, 128), BF),
            pltpu.VMEM((2, 2 * PASSES, 128), BF),
            pltpu.VMEM((2, 2 * PASSES, 128), BF),
            pltpu.VMEM((4, 1, 128), F32),
            pltpu.VMEM((32, 1, 128), jnp.int32),
            pltpu.VMEM((256, 128), jnp.int32),
            pltpu.VMEM((256, 512), F32),
            pltpu.VMEM((32, 8, 128), F32),
            pltpu.VMEM((32, 8, 128), F32),
            pltpu.VMEM((PAD, PART), F32),
            pltpu.VMEM((PAD, PART), F32),
            pltpu.VMEM((PASSES, 2 * PART), F32),
            pltpu.SemaphoreType.DMA((S_END,)),
            pltpu.SemaphoreType.DMA((R_END,)),
            pltpu.SemaphoreType.DMA((10,)),
            pltpu.SemaphoreType.REGULAR((5,)),
        ],
        compiler_params=pltpu.CompilerParams(collective_id=0, has_side_effects=True, vmem_limit_bytes=56 << 20),
        name="passages",
    )(
        lengths,
        assign,
        states.reshape(ROWS, PART),
        norm_gain.reshape(32, 128),
        gate_weight,
        up_weight,
        down_weight,
        out_gain.reshape(1, PART),
        centroids,
    )
    embedding = both[:, :PART]
    return embedding, embedding - both[:, PART:]


def solution(mesh):
    return jax.shard_map(
        per_device,
        mesh=mesh,
        in_specs=(
            P("list", None, "tensor"),
            P("list"),
            P("list"),
            P(),
            P("list", "tensor"),
            P("list", "tensor"),
            P("tensor", "list"),
            P("tensor"),
            P("list", "tensor"),
        ),
        out_specs=(P("list", "tensor"), P("list", "tensor")),
        check_vma=False,
    )
```

```python
import functools

import jax
import jax.numpy as jnp
from jax import lax
from jax.experimental import pallas as pl
from jax.experimental.pallas import tpu as pltpu
from jax.sharding import PartitionSpec as P

MESH = pl.DeviceIdType.MESH
BF = jnp.bfloat16
F32 = jnp.float32

PASSES, SEQ, PART, WIDTH = 24, 16, 512, 4096
ROWS = PASSES * SEQ
HID = 896
TILES = HID // 128
PAD = 32
OWN_ROWS = 4096

R_Z = 0
R_Y = 4
R_H = 12
R_SC = 16
R_SY = 20
R_SH = 24
R_DN = 28
R_DS = 32
R_CR = 33
R_X = 35
R_G = 39
R_1 = 42
R_2 = 46
R_3 = 47
R_REQ = 48
R_RSP = 49
R_MEAN = 50
R_CB = 51
R_XB = 53
R_G2 = 55
R_END = 58
S_W, S_Z, S_X, S_CR, S_DZ, S_DS, S_G, S_1, S_2, S_3, S_REQ, S_RSP, S_MEAN, S_G2, S_END = range(15)


def kernel(
    lengths, assign, states, gain, gate, up, down, out_gain, centroids,
    out,
    wbuf, xbuf, acc, cbuf, dbuf, sbuf, g_in, u_in, gain_in, og_in,
    scale_s, mask_s, inv_s, hb, hb2, hid, tf, tb, r1b, qs, rb, rb7, mine_m, other_m, sb, abuf, pick, cacc, resp, gotc, chosen_s, smean, out_s,
    ss, rs, ls, word,
):
    lst = lax.axis_index("list")
    ten = lax.axis_index("tensor")
    core = lax.rem(lst, 2)
    y = lax.rem(lst // 2, 4)
    zl = lst // 8
    x = ten // 2
    zh = lax.rem(ten, 2)
    me_g = lax.rem(lst, 8)

    def dev(list_=None, tensor=None):
        return {"list": lst if list_ is None else list_, "tensor": ten if tensor is None else tensor}

    def at_z(z):
        return dev(list_=z * 8 + me_g)

    def at_y(step):
        return dev(list_=zl * 8 + lax.rem(y + step + 4, 4) * 2 + core)

    def at_x(step):
        return dev(tensor=lax.rem(x + step + 4, 4) * 2 + zh)

    sibling = dev(list_=lst + 1 - 2 * core)
    partner = dev(tensor=x * 2 + 1 - zh)

    def remote(src, dst, kind, recv, device):
        return pltpu.make_async_remote_copy(
            src_ref=src, dst_ref=dst, send_sem=ss.at[kind], recv_sem=rs.at[recv],
            device_id=device, device_id_type=MESH,
        )

    def send(src, dst, kind, recv, device, cond=None):
        cp = remote(src, dst, kind, recv, device)
        if cond is None:
            cp.start()
        else:
            pl.when(cond)(cp.start)

    def arrived(dst, recv):
        remote(dst, dst, 0, recv, sibling).wait_recv()

    def sent(src, kind):
        remote(src, src, kind, 0, sibling).wait_send()

    locals_ = []

    def local(src, dst):
        cp = pltpu.make_async_copy(src, dst, ls.at[len(locals_)])
        locals_.append(cp)
        cp.start()
        return cp

    def dslot(z_, c_):
        return dbuf.at[:, pl.ds(pl.multiple_of(z_ * 256 + c_ * 128, 128), 128)]

    def xslot(z_hi, half, x_):
        return xbuf.at[z_hi * 2 + half, :, pl.ds(pl.multiple_of(x_ * 256, 256), 256)]

    def xslot(z_hi, half, x_):
        return xbuf.at[z_hi * 2 + half, :, pl.ds(pl.multiple_of(x_ * 256, 256), 256)]

    barrier = pltpu.get_barrier_semaphore()

    def ring_z(step):
        z_ = lax.rem(zh * 4 + zl + step + 8, 8)
        return dev(list_=lax.rem(z_, 4) * 8 + me_g, tensor=x * 2 + z_ // 4)

    def greet(semaphore, devices):
        for there in devices:
            pl.semaphore_signal(semaphore, inc=1, device_id=there, device_id_type=MESH)

    near = [ring_z(1), ring_z(-1), at_y(1), at_y(-1), at_x(1), at_x(-1), sibling]
    greet(barrier, near)
    cps_w = [local(gate, g_in), local(up, u_in), local(gain, gain_in)]
    cps_x = [local(states.at[:, pl.ds(half * 256, 256)], xslot(zh, half, x)) for half in range(2)]
    cp_d = local(down, dslot(zl, core))
    cp_s = local(states, sbuf)
    cp_c = local(centroids, cbuf)
    cp_o = local(out_gain, og_in)
    for cp in cps_w:
        cp.wait()
    eye = lax.broadcasted_iota(jnp.int32, (128, 128), 0) == lax.broadcasted_iota(jnp.int32, (128, 128), 1)
    gcol = jnp.sum(jnp.where(eye, gain_in[pl.ds(lst, 1), :], 0.0), axis=1, keepdims=True)
    own_rows = pl.ds(pl.multiple_of(y * 1024 + zl * 256 + core * 128, 128), 128)
    for j in range(TILES):
        wbuf[own_rows, j * 256 : j * 256 + 128] = (g_in[:, j * 128 : j * 128 + 128].astype(F32) * gcol).astype(BF)
        wbuf[own_rows, j * 256 + 128 : j * 256 + 256] = (u_in[:, j * 128 : j * 128 + 128].astype(F32) * gcol).astype(BF)

    pl.semaphore_wait(barrier, len(near))
    def x_send(step):
        for half in range(2):
            send(states.at[:, pl.ds(half * 256, 256)], xslot(zh, half, x), S_X, R_X + half, at_x(step))

    x_send(1)
    x_send(-1)

    def piece(z_hi, n, p, x_):
        rows = pl.ds(0, ROWS) if n == 0 else pl.ds(p * (ROWS // 2), ROWS // 2)
        return xbuf.at[z_hi * 2 + lax.rem(y + n, 2), rows, pl.ds(pl.multiple_of(x_ * 256, 256), 256)]

    def cross(n, p=0):
        rows = pl.ds(0, ROWS) if n == 0 else pl.ds(p * (ROWS // 2), ROWS // 2)
        cols = pl.ds(pl.multiple_of(lax.rem(y + n, 2) * 256, 256), 256)
        send(states.at[rows, cols], piece(zh, n, p, x), S_CR, R_CR if n == 0 else R_CB + p, partner)

    def crossed(n, p=0):
        block = piece(1 - zh, n, p, x)
        arrived(block, R_CR if n == 0 else R_CB + p)
        for step in (1, -1, 2):
            send(block, block, S_X, R_X + 2 if n == 0 else R_XB + p, at_x(step))

    def x_arrived(n):
        arrived(xbuf.at[0, :, pl.ds(0, 768)], R_X + n)

    def wblock(y_, z_, c_, start=0, rows=128):
        return wbuf.at[pl.ds(pl.multiple_of(y_ * 1024 + z_ * 256 + c_ * 128 + start, 64), rows)]

    def place(k):
        inner = (zl == 1) | (zl == 2)
        o = jnp.where(inner, 1 - k, k) if k < 2 else k
        return jnp.where(zl < 2, o, 3 - o)

    inner_z = (zl == 1) | (zl == 2)

    def y_of(step):
        return lax.rem(y + step + 4, 4)

    def column(k):
        z_ = place(k)
        block = wblock(y, z_, core)
        if k == 0:
            send(block, block, S_Z, R_Z + z_, at_z(lax.rem(zl + 1, 4)), zl < 3)
            send(block, block, S_Z, R_Z + z_, at_z(lax.rem(zl + 3, 4)), zl > 0)
        else:
            arrived(block, R_Z + z_)
            onward = jnp.where(z_ < zl, zl + 1, zl - 1)
            send(block, block, S_Z, R_Z + z_, at_z(lax.rem(onward + 4, 4)), inner_z)
        send(block, block, S_W, R_Y + k, at_y(1))
        send(block, block, S_W, R_Y + 4 + k, at_y(-1))
        send(block, block, S_W, R_SC + k, sibling)

    def neighbour(k):
        z_ = place(k)
        for d, step in ((0, -1), (1, 1)):
            block = wblock(y_of(step), z_, core)
            arrived(block, R_Y + d * 4 + k)
            part = wblock(y_of(step), z_, core, d * 64, 64)
            send(part, part, S_W, R_H + k, at_y(-step))
            send(block, block, S_W, R_SY + k, sibling)

    def halves(k):
        block = wblock(y_of(2), place(k), core)
        arrived(block, R_H + k)
        send(block, block, S_W, R_SH + k, sibling)

    outer_z = jnp.logical_not(inner_z)
    near_end = jnp.where(zl < 2, 0, 3)
    near_mid = jnp.where(zl < 2, 1, 2)

    def down_to(z_, to):
        block = dslot(z_, core)
        send(block, block, S_DZ, R_DN + z_, at_z(to))

    def down_over(z_):
        block = dslot(z_, core)
        send(block, block, S_DS, R_DS, sibling)

    def down_from(z_):
        arrived(dslot(z_, core), R_DN + z_)
        down_over(z_)

    def product(yy, k):
        ks = pl.ds(pl.multiple_of(place(k) * 256, 256), 256)
        rows = pl.ds(pl.multiple_of(yy * 1024 + place(k) * 256, 256), 256)
        for j in range(TILES):
            acc[j] += jnp.dot(xbuf[yy, :, ks], wbuf[rows, j * 256 : j * 256 + 256], preferred_element_type=F32)

    def squares_of(yy, init):
        @pl.loop(0, ROWS // 32)
        def _(r):
            rows = pl.ds(pl.multiple_of(r * 32, 32), 32)
            total = jnp.zeros((32, 128), F32) if init else scale_s[rows, :]
            for c in range(8):
                v = xbuf[yy, rows, c * 128 : c * 128 + 128].astype(F32)
                total = total + v * v
            scale_s[rows, :] = total

    def from_sibling_column(k):
        arrived(wblock(y, place(k), 1 - core), R_SC + k)

    def from_sibling_neighbours(k):
        arrived(wbuf.at[pl.ds(0, 256)], R_SY + k)

    def from_sibling_halves(k):
        arrived(wblock(y_of(2), place(k), 1 - core), R_SH + k)

    def packed(v):
        return jnp.concatenate([v[:, :128], v[:, 128:]], axis=0)

    column(0)

    lane = lax.broadcasted_iota(jnp.int32, (1, 128), 1)
    arow = jnp.full((1, 128), -1, jnp.int32)
    sub = lax.broadcasted_iota(jnp.int32, (PAD, 128), 0)
    acol = jnp.full((PAD, 128), -1, jnp.int32)
    lcol = jnp.ones((PAD, 128), jnp.int32)
    for p in range(PASSES):
        arow = jnp.where(lane == p, assign[p], arow)
        acol = jnp.where(sub == p, assign[p], acol)
        lcol = jnp.where(sub == p, lengths[p], lcol)
    abuf[lst] = arow

    for r in range(5):
        greet(word.at[r], near)
        pl.semaphore_wait(word.at[r], len(near))
        if r == 0:
            x_send(2)

    @pl.loop(1, 32)
    def _(i):
        peer = lax.rem(lst + i, 32)
        send(abuf.at[lst], abuf.at[lst], S_REQ, R_REQ, dev(list_=peer))

    slot_row = lax.broadcasted_iota(jnp.int32, (PAD, ROWS), 0)
    slot_col = lax.broadcasted_iota(jnp.int32, (PAD, ROWS), 1)
    length = lcol[:, :1]
    in_pass = (slot_col >= slot_row * SEQ) & (slot_col < slot_row * SEQ + length) & (slot_row < PASSES)
    mask_s[...] = jnp.where(in_pass, 1.0, 0.0).astype(BF)
    inv_s[...] = 1.0 / lcol.astype(F32)
    cp_s.wait()
    smean[...] = jnp.dot(mask_s[...], sbuf[...], preferred_element_type=F32) * inv_s[:, :1]
    for i in range(2):
        mine_m[i] = packed(smean[:PASSES, i * 256 : i * 256 + 256]).astype(BF)
    send(mine_m, other_m, S_MEAN, R_MEAN, partner)

    column(1)
    pl.when(inner_z)(lambda: column(2))
    neighbour(0)

    pl.when(jnp.logical_not(inner_z))(lambda: cross(0))
    arrived(abuf.at[pl.ds(0, 31)], R_REQ)
    cp_c.wait()
    wanted = jnp.broadcast_to(abuf[...], (32, 8, 128))
    lanes3 = lax.broadcasted_iota(jnp.int32, (32, 8, 128), 2)
    odd3 = lax.rem(lax.broadcasted_iota(jnp.int32, (32, 8, 128), 1), 2) == 1
    mine = (wanted >= lst * OWN_ROWS) & (wanted < lst * OWN_ROWS + OWN_ROWS)
    first = jnp.min(jnp.where(mine, lanes3, 128), axis=2, keepdims=True)
    last = jnp.max(jnp.where(mine, lanes3, -1), axis=2, keepdims=True)
    chosen_lane = jnp.where(odd3, last, first)
    hit = mine & (lanes3 == chosen_lane)
    ids = jnp.sum(jnp.where(hit, wanted - lst * OWN_ROWS, 0), axis=2, keepdims=True)
    pick[...] = jnp.broadcast_to(ids, (32, 8, 128)).reshape(256, 128)
    cacc[...] = jnp.zeros_like(cacc)

    @pl.loop(0, 8)
    def _(kc):
        base = lax.broadcasted_iota(jnp.int32, (256, 512), 1) + kc * 512
        one = jnp.where(base == pick[:, :1], 1.0, 0.0).astype(BF)
        cacc[...] += jnp.dot(one, cbuf[pl.ds(pl.multiple_of(kc * 512, 512), 512), :], preferred_element_type=F32)

    quarter = lax.rem(lax.broadcasted_iota(jnp.int32, (256, 128), 0), 8) // 2
    out_rows = jnp.zeros((256, 128), F32)
    for q in range(4):
        out_rows = jnp.where(quarter == q, cacc[:, q * 128 : q * 128 + 128], out_rows)
    resp[...] = out_rows.reshape(32, 8, 128)
    gotc[lst] = resp[lst]

    @pl.loop(1, 32)
    def _(i):
        peer = lax.rem(lst + i, 32)
        send(resp.at[peer], gotc.at[lst], S_RSP, R_RSP, dev(list_=peer))

    pl.when(inner_z)(lambda: cross(0))
    pl.when(inner_z)(lambda: column(3))
    neighbour(1)
    pl.when(outer_z)(lambda: column(2))
    for cp in cps_x:
        cp.wait()
    for half in range(2):
        x_arrived(half)
    acc[...] = jnp.zeros_like(acc)
    squares_of(zh * 2, True)
    squares_of(zh * 2 + 1, False)
    halves(0)
    crossed(0)
    y_a = jnp.where(y // 2 == zh, y + 1 - 2 * lax.rem(y, 2), lax.rem(y + 3 - 2 * lax.rem(y, 2), 4))
    y_b = lax.rem(y_a + 2, 4)
    for k in range(2):
        from_sibling_neighbours(k)
        product(y_a, k)
    cp_d.wait()
    down_to(zl, jnp.where(inner_z, 3 - zl, near_mid))
    down_over(zl)
    neighbour(2)
    cross(1, 0)
    pl.when(outer_z)(lambda: column(3))
    cross(1, 1)
    @pl.when(inner_z)
    def _():
        down_from(near_end)
        down_to(near_end, 3 - zl)
        down_to(zl, near_end)

    crossed(1, 0)
    x_arrived(2)
    for k in range(4):
        from_sibling_column(k)
        product(y, k)
    crossed(1, 1)
    @pl.when(inner_z)
    def _():
        down_from(3 - zl)
        down_to(3 - zl, near_end)

    halves(1)
    from_sibling_neighbours(2)
    product(y_a, 2)
    squares_of((1 - zh) * 2 + lax.rem(y, 2), False)
    halves(2)
    for k in range(2):
        from_sibling_halves(k)
        product(y_of(2), k)
    neighbour(3)
    @pl.when(inner_z)
    def _():
        down_from(3 - near_end)
        down_to(3 - near_end, near_end)

    from_sibling_halves(2)
    product(y_of(2), 2)
    from_sibling_neighbours(3)
    product(y_a, 3)
    for p in range(2):
        arrived(xbuf.at[0, pl.ds(0, ROWS // 2), pl.ds(0, 768)], R_XB + p)
    squares_of((1 - zh) * 2 + lax.rem(y + 1, 2), False)
    product(y_b, 0)
    product(y_b, 1)
    product(y_b, 2)
    product(y_b, 3)
    halves(3)
    scale_s[...] = jnp.broadcast_to(
        lax.rsqrt(jnp.sum(scale_s[...], axis=1, keepdims=True) / WIDTH + 1e-05), (ROWS, 128)
    )
    from_sibling_halves(3)
    around = (2, 1, -1)

    yy = y_of(2)
    ks = pl.ds(pl.multiple_of(place(3) * 256, 256), 256)
    wrows = pl.ds(pl.multiple_of(yy * 1024 + place(3) * 256, 256), 256)
    for first, last_, buf, kind, recv in ((0, 4, hb, S_G, R_G), (4, TILES, hb2, S_G2, R_G2)):
        for j in range(first, last_):
            r = acc[j] + jnp.dot(xbuf[yy, :, ks], wbuf[wrows, j * 256 : j * 256 + 256], preferred_element_type=F32)
            g = r[:, :128] * scale_s[...]
            u = r[:, 128:] * scale_s[...]
            hid[:, j * 128 : j * 128 + 128] = (g * (0.5 + 0.5 * jnp.tanh(0.5 * g)) * u).astype(BF)
        p = jnp.dot(mask_s[...], hid[:, first * 128 : last_ * 128], preferred_element_type=F32)
        rows_p = [p[:PASSES, i * 128 : i * 128 + 128] * inv_s[:PASSES] for i in range(last_ - first)]
        if first:
            rows_p.append(jnp.zeros((8, 128), F32))
        buf[y] = jnp.concatenate(rows_p, axis=0).astype(BF)
        for n, step in enumerate(around):
            send(buf.at[y], buf.at[y], kind, recv + n, at_y(step))
    @pl.when(outer_z)
    def _():
        down_from(near_mid)
        down_from(3 - near_mid)
        down_from(3 - zl)

    arrived(dbuf.at[:, pl.ds(0, 512)], R_DS)
    cp_o.wait()

    arrived(gotc.at[pl.ds(0, 31)], R_RSP)
    own_col = acol >> 12
    own_row = jnp.where(lane < PASSES, arow >> 12, -1)
    before = (own_col == own_row) & (lax.broadcasted_iota(jnp.int32, (PAD, 128), 1) < sub)
    slot = jnp.max(jnp.where(before, 1, 0), axis=1, keepdims=True)
    wide = lax.broadcasted_iota(jnp.int32, (PAD, 256), 1)
    table = gotc[...].reshape(256, 128).astype(BF)
    for q in range(4):
        one = jnp.where(wide == own_col[:, :1] * 8 + q * 2 + slot, 1.0, 0.0).astype(BF)
        chosen_s[:, q * 128 : q * 128 + 128] = jnp.dot(one, table, preferred_element_type=F32)


    steps = (0, 1, -1, 2)
    came = {1: 2, -1: 1, 2: 0}
    groups = ((0, 1), (1, 3), (3, 4))
    for n, (lo, hi) in enumerate(groups):
        rows_in = []
        for step in steps[lo:hi]:
            y_ = y_of(step)
            if step != 0:
                arrived(hb.at[y_], R_G + came[step])
                arrived(hb2.at[y_], R_G2 + came[step])
            a, b = hb[y_].astype(F32), hb2[y_].astype(F32)
            parts = [a[i * PASSES : i * PASSES + PASSES] for i in range(4)] + [b[i * PASSES : i * PASSES + PASSES] for i in range(3)]
            rows_in.append(jnp.concatenate(parts, axis=1))
        rows_in = (rows_in[0] if len(rows_in) == 1 else jnp.concatenate(rows_in, axis=0)).astype(BF)
        term = jnp.dot(rows_in, dbuf[...], preferred_element_type=F32)
        for m in range(lo, hi):
            for z_ in range(4):
                v = packed(term[(m - lo) * PASSES : (m - lo + 1) * PASSES, z_ * 256 : z_ * 256 + 256])
                tf[z_, m] = v
                tb[z_, m] = v.astype(BF)
        for x_step in (2, 1, -1):
            x_ = lax.rem(x + x_step + 4, 4)
            here = pl.ds(lo, hi - lo)
            send(tb.at[x_, here], r1b.at[x, here], S_1, R_1 + n, at_x(x_step))
    for n, (lo, hi) in enumerate(groups):
        arrived(r1b.at[pl.ds(0, 3), pl.ds(0, hi - lo)], R_1 + n)
        for m in range(lo, hi):
            y_ = y_of(steps[m])
            v = tf[x, m]
            for x_step in (1, -1, 2):
                v = v + r1b[lax.rem(x + x_step + 4, 4), m].astype(F32)
            qs[y_] = v.astype(BF)
            for far in (1, 0):
                if m == 0 and far == 0:
                    rb[zh, y] = qs[y]
                else:
                    target = dev(list_=zl * 8 + y_ * 2 + core, tensor=x * 2 + lax.rem(zh + far, 2))
                    send(qs.at[y_], rb.at[zh, y], S_2, R_2, target)
    arrived(other_m, R_MEAN)
    arrived(rb7.at[pl.ds(0, 7)], R_2)
    pooled = []
    squares = jnp.zeros((PASSES, 128), F32)
    for i in range(2):
        v = rb[0, zh * 2 + i].astype(F32) + rb[1, zh * 2 + i].astype(F32) + packed(smean[:PASSES, i * 256 : i * 256 + 256])
        w = rb[0, (1 - zh) * 2 + i].astype(F32) + rb[1, (1 - zh) * 2 + i].astype(F32) + other_m[i].astype(F32)
        both = v * v + w * w
        squares = squares + both[:PASSES] + both[PASSES:]
        pooled += [v[:PASSES], v[PASSES:]]
    turn = lax.broadcasted_iota(jnp.int32, (PASSES, 128), 0) == lax.broadcasted_iota(jnp.int32, (PASSES, 128), 1)
    sb[x] = jnp.sum(jnp.where(turn, jnp.sum(squares, axis=1, keepdims=True), 0.0), axis=0, keepdims=True)
    for step in (2, 1, -1):
        send(sb.at[x], sb.at[x], S_3, R_3, at_x(step))
    sent(wbuf.at[pl.ds(0, 28 * 128)], S_W)
    sent(xbuf.at[pl.ds(0, 3)], S_X)
    sent(xbuf.at[0, :, pl.ds(0, 512)], S_CR)
    sent(dbuf.at[:, pl.ds(0, 512)], S_DS)
    sent(hb.at[pl.ds(0, 3)], S_G)
    sent(hb2.at[pl.ds(0, 3)], S_G2)
    sent(tb.at[pl.ds(0, 3)], S_1)
    sent(abuf.at[pl.ds(0, 31)], S_REQ)
    sent(resp.at[pl.ds(0, 31)], S_RSP)

    @pl.when(inner_z)
    def _():
        sent(wbuf.at[pl.ds(0, 5 * 128)], S_Z)
        sent(dbuf.at[:, pl.ds(0, 5 * 128)], S_DZ)

    @pl.when(jnp.logical_not(inner_z))
    def _():
        sent(wbuf.at[pl.ds(0, 128)], S_Z)
        sent(dbuf.at[:, pl.ds(0, 128)], S_DZ)

    sent(rb7.at[pl.ds(0, 7)], S_2)
    sent(mine_m, S_MEAN)
    arrived(sb.at[pl.ds(0, 3)], R_3)
    total = sb[0]
    for x_ in range(1, 4):
        total = total + sb[x_]
    total = jnp.sum(jnp.where(turn, total, 0.0), axis=1, keepdims=True)
    norm = lax.rsqrt(total / WIDTH + 1e-05)
    for i in range(4):
        cols = slice(i * 128, i * 128 + 128)
        out[:, cols] = pooled[i] * norm * og_in[:, cols]
        out[:, i * 128 + PART : i * 128 + PART + 128] = chosen_s[:PASSES, cols]
    sent(sb.at[pl.ds(0, 3)], S_3)


def per_device(
    states, lengths, assign, norm_gain, gate_weight, up_weight, down_weight, out_gain, centroids
):
    any_ = pl.BlockSpec(memory_space=pl.ANY)
    smem = pl.BlockSpec(memory_space=pltpu.SMEM)
    both = pl.pallas_call(
        kernel,
        out_shape=pltpu.VMEM((PASSES, 2 * PART), F32),
        in_specs=[smem, smem] + [any_] * 7,
        out_specs=pl.BlockSpec(memory_space=pltpu.VMEM),
        scratch_shapes=[
            pltpu.VMEM((WIDTH, 2 * HID), BF),
            pltpu.VMEM((4, ROWS, 1024), BF),
            pltpu.VMEM((TILES, ROWS, 256), F32),
            pltpu.VMEM((OWN_ROWS, PART), BF),
            pltpu.VMEM((HID, 1024), BF),
            pltpu.VMEM((ROWS, PART), BF),
            pltpu.VMEM((128, HID), BF),
            pltpu.VMEM((128, HID), BF),
            pltpu.VMEM((32, 128), F32),
            pltpu.VMEM((1, PART), F32),
            pltpu.VMEM((ROWS, 128), F32),
            pltpu.VMEM((PAD, ROWS), BF),
            pltpu.VMEM((PAD, 128), F32),
            pltpu.VMEM((4, 4 * PASSES, 128), BF),
            pltpu.VMEM((4, 3 * PASSES + 8, 128), BF),
            pltpu.VMEM((ROWS, HID), BF),
            pltpu.VMEM((4, 4, 2 * PASSES, 128), F32),
            pltpu.VMEM((4, 4, 2 * PASSES, 128), BF),
            pltpu.VMEM((4, 4, 2 * PASSES, 128), BF),
            pltpu.VMEM((4, 2 * PASSES, 128), BF),
            pltpu.VMEM((2, 4, 2 * PASSES, 128), BF),
            pltpu.VMEM((8, 2 * PASSES, 128), BF),
            pltpu.VMEM((2, 2 * PASSES, 128), BF),
            pltpu.VMEM((2, 2 * PASSES, 128), BF),
            pltpu.VMEM((4, 1, 128), F32),
            pltpu.VMEM((32, 1, 128), jnp.int32),
            pltpu.VMEM((256, 128), jnp.int32),
            pltpu.VMEM((256, 512), F32),
            pltpu.VMEM((32, 8, 128), F32),
            pltpu.VMEM((32, 8, 128), F32),
            pltpu.VMEM((PAD, PART), F32),
            pltpu.VMEM((PAD, PART), F32),
            pltpu.VMEM((PASSES, 2 * PART), F32),
            pltpu.SemaphoreType.DMA((S_END,)),
            pltpu.SemaphoreType.DMA((R_END,)),
            pltpu.SemaphoreType.DMA((10,)),
            pltpu.SemaphoreType.REGULAR((5,)),
        ],
        compiler_params=pltpu.CompilerParams(collective_id=0, has_side_effects=True, vmem_limit_bytes=56 << 20),
        name="passages",
    )(
        lengths,
        assign,
        states.reshape(ROWS, PART),
        norm_gain.reshape(32, 128),
        gate_weight,
        up_weight,
        down_weight,
        out_gain.reshape(1, PART),
        centroids,
    )
    embedding = both[:, :PART]
    return embedding, embedding - both[:, PART:]


def solution(mesh):
    return jax.shard_map(
        per_device,
        mesh=mesh,
        in_specs=(
            P("list", None, "tensor"),
            P("list"),
            P("list"),
            P(),
            P("list", "tensor"),
            P("list", "tensor"),
            P("tensor", "list"),
            P("tensor"),
            P("list", "tensor"),
        ),
        out_specs=(P("list", "tensor"), P("list", "tensor")),
        check_vma=False,
    )
```
